32 devices in a mesh: groups: 2 (over y), space: 16 (over z, x, core).
Axes of the slice: x: 2, y: 2, z: 4, core: 2. Of those that a mesh axis runs over, the one named last changes fastest.
Arguments:
- latent: float32 [131072], P(('groups', 'space')), parts along dimension 0, may hold values from -6 to 6
- responses: int32 [131072], P(('groups', 'space')), parts along dimension 0, may hold values from 0 to 1
- probes: float32 [32, 131072], P(None, ('groups', 'space')), parts along dimension 1
- prior_diag: float32 [131072], P(('groups', 'space')), parts along dimension 0, may hold values from 0.5 to 8
- factor: bfloat16 [1024, 4, 128, 128], P(('groups', 'space')), parts along dimension 0, may hold values from -0.25 to 0.25
- cond_ids: int32 [1024, 3], P(('groups', 'space')), parts along dimension 0, may hold values from 0 to 510, as said below
- inducing_map: bfloat16 [131072, 256], P(('groups', 'space')), parts along dimension 0, may hold values from -0.375 to 0.375
- inner_inverse: float32 [512, 256], P('groups'), parts along dimension 0
Outputs:
- solution: float32 [33, 131072], P(None, ('groups', 'space')), parts along dimension 1
- residual: float32 [33, 131072], P(None, ('groups', 'space')), parts along dimension 1
- next_direction: float32 [33, 131072], P(None, ('groups', 'space')), parts along dimension 1
The draws below stay inside these ranges and needn't reach their ends.
There are 2 independent parts, one for each index of `groups`. The reference program is written for one: setup_inputs(seed, part) draws one part's arguments, and reference() takes and returns one part's arrays. A program takes and returns all parts, laid end to end along the dimension named above; each array names one. Nothing has to cross between parts.
Inputs may be any that keep to these rules, and one draw needn't show every extreme that they name: `cond_ids`: each id of block b lies from max(b - 64, 0) to max(b - 1, 0); the first block of every device names, as its third id, the block 64 before it where that exists.
All inputs are finite; a program needn't handle non-finite values.
Results may differ from the reference program's by a relative error of at most 0.006.
Values may be sent and summed in bfloat16 or wider, within the bound.
No kernel may reach another device: no remote copies, remote signals or barrier semaphores. Data moves between devices by JAX's collectives and lax.ppermute only.
A program may use at most 64 MiB of HBM per device.

```python
import math
import jax
import jax.numpy as jnp
from jax import lax

BS = 128
NB_DEV = 32
PROBES = 32
INDUCING = 256
NBLK = 512
POINTS = 65536


def draw_probes(key, part):
    key = jax.random.fold_in(key, 5)
    position = jnp.arange(POINTS, dtype=jnp.float32) / POINTS
    scaling = 1.0 + position
    random_part = jax.random.normal(key, (PROBES, POINTS), jnp.float32)
    return jnp.clip(random_part, -4.0, 4.0) * scaling


def draw_cond_ids(key, part):
    key = jax.random.fold_in(key, 11)
    reach = 2 * NB_DEV
    offsets = jax.random.randint(key, (NBLK, 3), 1, reach + 1)
    block_index = jnp.arange(NBLK, dtype=jnp.int32)[:, None]
    slot_index = jnp.arange(3, dtype=jnp.int32)[None, :]
    forced = jnp.logical_and(block_index % NB_DEV == 0, slot_index == 2)
    offsets = jnp.where(forced, reach, offsets)
    last_one = jnp.logical_and(block_index == NBLK - 1, slot_index == 0)
    offsets = jnp.where(last_one, 1, offsets)
    return jnp.maximum(block_index - offsets, 0).astype(jnp.int32)


def draw_inner_inverse(key, part):
    key = jax.random.fold_in(key, 7)
    random_part = jax.random.normal(key, (INDUCING, INDUCING), jnp.float32)
    symmetric = (random_part + random_part.T) * (0.3 / math.sqrt(2.0 * INDUCING))
    identity_mat = jnp.eye(INDUCING, dtype=jnp.float32)
    return (identity_mat + symmetric) * (8.0 / math.sqrt(POINTS))


def set_ends(drawn, stream_key, smallest, high):
    index_at = [jax.random.randint(jax.random.fold_in(stream_key, axis), (), 0, length) for axis, length in enumerate(drawn.shape)]
    main_axis = drawn.shape.index(max(drawn.shape))
    beside = index_at[:main_axis] + [(index_at[main_axis] + 1) % drawn.shape[main_axis]] + index_at[main_axis + 1:]
    return drawn.at[tuple(index_at)].set(smallest).at[tuple(beside)].set(high)


def block_levels(stream_key, dims, shards, smallest, largest):
    def one(dim, blocks):
        steps = jax.random.uniform(jax.random.fold_in(jax.random.fold_in(stream_key, 6), dim), (blocks,), jnp.float32, smallest / len(shards), largest / len(shards))
        return jnp.repeat(jnp.exp(steps), dims[dim] // blocks).reshape((-1,) + (1,) * (len(dims) - dim - 1))

    factor_of = one(*shards[0])
    for cut in shards[1:]:
        factor_of = factor_of * one(*cut)
    return factor_of


def scatter_about(key, extent, scale, bound, cuts=(), held_as=jnp.bfloat16):
    values = jax.random.normal(key, extent, jnp.float32) * scale
    if len(cuts) > 0:
        values = block_levels(key, extent, cuts, -0.22, 0.18) * values
    return jnp.clip(values, min=-bound, max=bound).astype(held_as)


def setup_inputs(seed: int = 0, part: int = 0) -> dict:
    key_of = jax.random.split(jax.random.key(seed), 9)
    part_splits = jax.random.split(jax.random.fold_in(key_of[8], part), 9)
    return {
        "latent": scatter_about(part_splits[0], (POINTS,), 1.5, 6.0, ((0, 16),), jnp.float32),
        "responses": set_ends(jax.random.randint(part_splits[1], (POINTS,), 0, 2), jax.random.fold_in(part_splits[1], 1), 0, 1).astype(jnp.int32),
        "probes": draw_probes(jax.random.fold_in(jax.random.fold_in(key_of[8], part), 71), part),
        "prior_diag": jnp.clip(jnp.exp(math.log(8.0) - 2.7725887 * jax.random.uniform(part_splits[3], (POINTS,), jnp.float32) ** block_levels(part_splits[3], (POINTS,), ((0, 16),), -0.2, 0.2)), 0.5, 8.0),
        "factor": scatter_about(part_splits[4], (NBLK, 4, BS, BS), (4 * BS) ** -0.5, 0.25, ((0, 16),)),
        "cond_ids": draw_cond_ids(jax.random.fold_in(jax.random.fold_in(key_of[8], part), 71), part),
        "inducing_map": scatter_about(part_splits[6], (POINTS, INDUCING), INDUCING ** -0.5, 0.375, ((0, 16),)),
        "inner_inverse": draw_inner_inverse(jax.random.fold_in(jax.random.fold_in(key_of[8], part), 71), part),
    }


def precondition(field, inv_diag, inducing_map, inner_inverse):
    scaled_f = field * inv_diag
    scaled = scaled_f.astype(jnp.bfloat16)
    inducing_sum = jnp.dot(scaled, inducing_map, preferred_element_type=jnp.float32)
    coeffs = jnp.dot(inducing_sum, inner_inverse, precision=lax.Precision.HIGHEST).astype(jnp.bfloat16)
    correction = jnp.dot(coeffs, inducing_map.T, preferred_element_type=jnp.float32)
    return scaled_f + correction * inv_diag


def apply_hessian(direction, weights, factor, cond_ids):
    columns = direction.shape[0]
    rounded = direction.astype(jnp.bfloat16)
    blocks = rounded.reshape(columns, NBLK, BS)
    chosen = jnp.concatenate([blocks[:, :, None, :], blocks[:, cond_ids]], axis=2)
    widened = factor.astype(jnp.float32)
    image = jnp.einsum('bkij,cbkj->cbi', widened, chosen.astype(jnp.float32), precision=lax.Precision.HIGHEST)
    imaged = image.astype(jnp.bfloat16).astype(jnp.float32)
    returned = jnp.einsum('bkij,cbi->cbkj', widened, imaged, precision=lax.Precision.HIGHEST)
    summed = returned[:, :, 0].at[:, cond_ids].add(returned[:, :, 1:])
    return summed.reshape(columns, POINTS) + weights * direction


def reference(latent, responses, probes, prior_diag, factor, cond_ids, inducing_map, inner_inverse):
    probability = jax.nn.sigmoid(latent)
    weights = probability * (1.0 - probability)
    first_column = responses.astype(jnp.float32) - probability
    right_side = jnp.concatenate([first_column[None, :], probes], axis=0)
    inv_diag = 1.0 / (weights + prior_diag)
    direction = precondition(right_side, inv_diag, inducing_map, inner_inverse)
    energy = jnp.sum(right_side * direction, axis=1)
    hess_dir = apply_hessian(direction, weights, factor, cond_ids)
    curve_sum = jnp.sum(direction * hess_dir, axis=1)
    step_length = (energy / curve_sum)[:, None]
    solution = step_length * direction
    residual = right_side - step_length * hess_dir
    smoothed = precondition(residual, inv_diag, inducing_map, inner_inverse)
    energy_next = jnp.sum(residual * smoothed, axis=1)
    next_direction = smoothed + (energy_next / energy)[:, None] * direction
    return solution, residual, next_direction
```

```python
import functools

import jax
import jax.numpy as jnp
from jax import lax
from jax.experimental import pallas as pl
from jax.experimental.pallas import tpu as pltpu
from jax.sharding import PartitionSpec as P

F32, BF16 = jnp.float32, jnp.bfloat16
PAIR = 2


def shifted(block, axis, distance):
    devices = range(lax.axis_size(axis))
    route = [(i - distance, i) for i in devices if i - distance in devices]
    return lax.ppermute(block, axis, route)


def total(x, axis):
    n = lax.axis_size(axis)
    if n & (n - 1):
        return lax.psum(x, axis)
    step = 1
    while step < n:
        partners = [m * step for m in range(1, 4) if m * step < n]
        got = [lax.ppermute(x, axis, [(i, i ^ d) for i in range(n)]) for d in partners]
        for y in got:
            x = x + y
        step *= 4
    return x


def eye(rows, lanes):
    return lax.broadcasted_iota(jnp.int32, (rows, lanes), 0) == lax.broadcasted_iota(jnp.int32, (rows, lanes), 1)


def as_row(column, lanes):
    return jnp.sum(jnp.where(eye(column.shape[0], lanes), column, 0.0), axis=0, keepdims=True)


def as_column(row, rows):
    return jnp.sum(jnp.where(eye(rows, row.shape[1]), row, 0.0), axis=1, keepdims=True)


def point_terms(latent, prior):
    probability = 1.0 / (1.0 + jnp.exp(-latent))
    weights = probability * (1.0 - probability)
    return probability, weights, 1.0 / (weights + prior)


def right_side_of(probes_ref, gradient, b, bs, rows):
    count = probes_ref.shape[0]
    return jnp.concatenate(
        [probes_ref[:, b * bs : (b + 1) * bs], jnp.broadcast_to(gradient[b : b + 1], (rows - count, bs))], axis=0
    )


def project_kernel(rows, latent_ref, responses_ref, prior_ref, probes_ref, map_ref, out_ref):
    blocks, bs = latent_ref.shape
    count = probes_ref.shape[0]
    probability, _, inv_diag = point_terms(latent_ref[...], prior_ref[...])
    gradient = responses_ref[...].astype(F32) - probability
    energy = jnp.zeros((rows, bs), F32)
    summed = jnp.zeros((rows, map_ref.shape[1]), F32)
    for b in range(0, blocks, PAIR):
        parts = []
        for c in range(b, b + PAIR):
            field = right_side_of(probes_ref, gradient, c, bs, rows)
            scaled = field * inv_diag[c : c + 1]
            energy += field * scaled
            parts.append(scaled.astype(BF16))
        summed += jnp.dot(
            jnp.concatenate(parts, axis=1), map_ref[b * bs : (b + PAIR) * bs], preferred_element_type=F32
        )
    out_ref[...] = summed
    out_ref[count + 1 : count + 2] = as_row(jnp.sum(energy, axis=1, keepdims=True), map_ref.shape[1])


def direction_kernel(
    rows, sums_ref, inner_ref, latent_ref, responses_ref, prior_ref, probes_ref, map_ref, dir_ref, msg_ref, grad_ref
):
    blocks, bs = latent_ref.shape
    count = probes_ref.shape[0]
    probability, _, inv_diag = point_terms(latent_ref[...], prior_ref[...])
    gradient = responses_ref[...].astype(F32) - probability
    coeffs = jnp.dot(sums_ref[...], inner_ref[...], precision=lax.Precision.HIGHEST).astype(BF16)
    for b in range(0, blocks, PAIR):
        correction = lax.dot_general(
            coeffs, map_ref[b * bs : (b + PAIR) * bs], (((1,), (1,)), ((), ())), preferred_element_type=F32
        )
        for c in range(b, b + PAIR):
            field = right_side_of(probes_ref, gradient, c, bs, rows)
            direction = (field + correction[:, (c - b) * bs : (c - b + 1) * bs]) * inv_diag[c : c + 1]
            dir_ref[c] = direction
            msg_ref[c] = direction[:count].astype(BF16)
            grad_ref[c : c + 1] = direction[count : count + 1]
    msg_ref[blocks] = grad_ref[...].astype(BF16)


def hessian_kernel(
    rows, ids_ref, factor_ref, far_ref, near_ref, own_ref, back_far_ref, back_near_ref, back_own_ref, curve_ref,
    around_ref, around_grad_ref, image_ref, total_ref, grad_ref,
):
    blocks, taps, bs, _ = factor_ref.shape
    count = around_ref.shape[1]
    tall = image_ref.shape[1]
    for i, ref in enumerate((far_ref, near_ref, own_ref)):
        around_ref[i * blocks : (i + 1) * blocks] = ref[:blocks]
        around_grad_ref[i * blocks : (i + 1) * blocks] = ref[blocks].astype(F32)
    total_ref[...] = jnp.zeros_like(total_ref)
    curve = jnp.zeros((rows, bs), F32)
    for b in range(blocks):
        image = jnp.zeros((tall, bs), F32)
        for k in range(taps):
            at = 2 * blocks + b if k == 0 else ids_ref[b, k - 1]
            last = jnp.broadcast_to(around_grad_ref[pl.ds(at, 1), :], (tall - count, bs)).astype(BF16)
            chosen = jnp.concatenate([around_ref[at], last], axis=0)
            image += lax.dot_general(
                chosen, factor_ref[b, k], (((1,), (1,)), ((), ())), preferred_element_type=F32
            )
        rounded = image.astype(BF16)
        image_ref[b] = rounded
        curve += (image * rounded.astype(F32))[:rows]
    curve_ref[...] = curve
    for b in range(blocks):
        rounded = image_ref[b]
        for k in range(taps):
            at = 2 * blocks + b if k == 0 else ids_ref[b, k - 1]
            back = jnp.dot(rounded, factor_ref[b, k], preferred_element_type=F32)
            total_ref[at] += back[:rows]
    for i, ref in enumerate((back_far_ref, back_near_ref)):
        for b in range(blocks):
            ref[b] = total_ref[i * blocks + b, :count].astype(BF16)
            grad_ref[b : b + 1] = total_ref[i * blocks + b, count : count + 1]
        ref[blocks] = grad_ref[...].astype(BF16)
    back_own_ref[...] = total_ref[2 * blocks :]


def combine_kernel(
    rows, own_ref, near_ref, far_ref, curve_ref, dir_ref, latent_ref, responses_ref, prior_ref, probes_ref, map_ref,
    hess_ref, out_ref,
):
    blocks, bs = latent_ref.shape
    count = probes_ref.shape[0]
    lanes = map_ref.shape[1]
    probability, weights, inv_diag = point_terms(latent_ref[...], prior_ref[...])
    gradient = responses_ref[...].astype(F32) - probability
    from_grad = near_ref[blocks].astype(F32) + far_ref[blocks].astype(F32)
    curve = curve_ref[...]
    cross = jnp.zeros((rows, bs), F32)
    square = jnp.zeros((rows, bs), F32)
    summed = jnp.zeros((rows, lanes), F32)
    for b in range(0, blocks, PAIR):
        parts = []
        for c in range(b, b + PAIR):
            came = jnp.concatenate(
                [
                    near_ref[c].astype(F32) + far_ref[c].astype(F32),
                    jnp.broadcast_to(from_grad[c : c + 1], (rows - count, bs)),
                ],
                axis=0,
            )
            direction = dir_ref[c]
            weighted = weights[c : c + 1] * direction
            hess = own_ref[c] + came + weighted
            hess_ref[c] = hess
            scaled = hess * inv_diag[c : c + 1]
            curve += weighted * direction
            cross += right_side_of(probes_ref, gradient, c, bs, rows) * scaled
            square += hess * scaled
            parts.append(scaled.astype(BF16))
        summed += jnp.dot(
            jnp.concatenate(parts, axis=1), map_ref[b * bs : (b + PAIR) * bs], preferred_element_type=F32
        )
    out_ref[...] = summed
    for i, acc in enumerate((curve, cross, square)):
        out_ref[count + 1 + i : count + 2 + i] = as_row(jnp.sum(acc, axis=1, keepdims=True), lanes)


def finish_kernel(
    rows, sums_ref, hess_sums_ref, inner_ref, dir_ref, hess_ref, latent_ref, responses_ref, prior_ref, probes_ref,
    map_ref, solution_ref, residual_ref, next_ref,
):
    blocks, bs = latent_ref.shape
    count = probes_ref.shape[0]
    probability, _, inv_diag = point_terms(latent_ref[...], prior_ref[...])
    gradient = responses_ref[...].astype(F32) - probability
    sums, hess_sums, inner = sums_ref[...], hess_sums_ref[...], inner_ref[...]
    column = lambda x, i: as_column(x[count + 1 + i : count + 2 + i], rows)
    coeffs = jnp.dot(sums, inner, precision=lax.Precision.HIGHEST).astype(BF16)
    plain = column(sums, 0)
    energy = plain + jnp.sum(coeffs.astype(F32) * sums, axis=1, keepdims=True)
    step = energy / column(hess_sums, 0)
    left = sums - step * hess_sums
    coeffs = jnp.dot(left, inner, precision=lax.Precision.HIGHEST).astype(BF16)
    plain_next = plain - 2.0 * step * column(hess_sums, 1) + step * step * column(hess_sums, 2)
    energy_next = plain_next + jnp.sum(coeffs.astype(F32) * left, axis=1, keepdims=True)
    ratio = energy_next / energy
    for b in range(0, blocks, PAIR):
        correction = lax.dot_general(
            coeffs, map_ref[b * bs : (b + PAIR) * bs], (((1,), (1,)), ((), ())), preferred_element_type=F32
        )
        for c in range(b, b + PAIR):
            at = slice(c * bs, (c + 1) * bs)
            direction = dir_ref[c]
            residual = right_side_of(probes_ref, gradient, c, bs, rows) - step * hess_ref[c]
            smoothed = (residual + correction[:, (c - b) * bs : (c - b + 1) * bs]) * inv_diag[c : c + 1]
            for ref, value in (
                (solution_ref, step * direction),
                (residual_ref, residual),
                (next_ref, smoothed + ratio * direction),
            ):
                ref[0:1, at] = value[count : count + 1]
                ref[1 : count + 1, at] = value[:count]


def call(kernel, outs, scratch=(), scalars=0, count=0, **kw):
    vmem = pl.BlockSpec(memory_space=pltpu.VMEM)
    smem = pl.BlockSpec(memory_space=pltpu.SMEM)
    shapes = tuple(jax.ShapeDtypeStruct(s, t) for s, t in outs)
    return pl.pallas_call(
        kernel,
        out_shape=shapes if len(shapes) > 1 else shapes[0],
        in_specs=[smem] * scalars + [vmem] * (count - scalars),
        out_specs=(vmem,) * len(shapes) if len(shapes) > 1 else vmem,
        scratch_shapes=scratch,
        compiler_params=pltpu.CompilerParams(vmem_limit_bytes=48 * 1024 * 1024),
    )


def body(latent, responses, probes, prior_diag, factor, cond_ids, inducing_map, inner_inverse):
    blocks, _, bs, _ = factor.shape
    count = probes.shape[0]
    inducing = inducing_map.shape[1]
    rows = count + 8
    tall = count + 16
    by_block = lambda x: x.reshape(blocks, bs)
    points = (by_block(latent), by_block(responses), by_block(prior_diag), probes, inducing_map)
    partial = call(functools.partial(project_kernel, rows), [((rows, inducing), F32)], count=5)(*points)
    sums = total(partial, "space")
    packed = (blocks + 1, count, bs)
    field = (blocks, rows, bs)
    direction, rounded = call(
        functools.partial(direction_kernel, rows), [(field, F32), (packed, BF16)], [pltpu.VMEM((blocks, bs), F32)], count=7
    )(sums, inner_inverse, *points)
    near = shifted(rounded, "space", 1)
    far = shifted(rounded, "space", 2)
    local_ids = cond_ids - (lax.axis_index("space") - 2) * blocks
    back_far, back_near, back_own, curve = call(
        functools.partial(hessian_kernel, rows),
        [(packed, BF16), (packed, BF16), (field, F32), ((rows, bs), F32)],
        [
            pltpu.VMEM((3 * blocks, count, bs), BF16),
            pltpu.VMEM((3 * blocks, bs), F32),
            pltpu.VMEM((blocks, tall, bs), BF16),
            pltpu.VMEM((3 * blocks, rows, bs), F32),
            pltpu.VMEM((blocks, bs), F32),
        ],
        scalars=1,
        count=5,
    )(local_ids, factor, far, near, rounded)
    from_near = shifted(back_near, "space", -1)
    from_far = shifted(back_far, "space", -2)
    hess, partial = call(
        functools.partial(combine_kernel, rows), [(field, F32), ((rows, inducing), F32)], count=10
    )(back_own, from_near, from_far, curve, direction, *points)
    hess_sums = total(partial, "space")
    whole = (count + 1, blocks * bs)
    return call(functools.partial(finish_kernel, rows), [(whole, F32)] * 3, count=10)(
        sums, hess_sums, inner_inverse, direction, hess, *points
    )


def solution(mesh):
    return jax.shard_map(
        body,
        mesh=mesh,
        in_specs=(
            P(("groups", "space")),
            P(("groups", "space")),
            P(None, ("groups", "space")),
            P(("groups", "space")),
            P(("groups", "space"), None, None, None),
            P(("groups", "space"), None),
            P(("groups", "space"), None),
            P("groups", None),
        ),
        out_specs=(
            P(None, ("groups", "space")),
            P(None, ("groups", "space")),
            P(None, ("groups", "space")),
        ),
        check_vma=False,
    )
```

```python
import functools

import jax
import jax.numpy as jnp
from jax import lax
from jax.experimental import pallas as pl
from jax.experimental.pallas import tpu as pltpu
from jax.sharding import PartitionSpec as P

F32, BF16 = jnp.float32, jnp.bfloat16
PAIR = 2
MAP_PARTS = 4
FACTOR_PARTS = 8


def shifted(block, axis, distance):
    devices = range(lax.axis_size(axis))
    route = [(i - distance, i) for i in devices if i - distance in devices]
    return lax.ppermute(block, axis, route)


def total(x, axis):
    n = lax.axis_size(axis)
    if n & (n - 1):
        return lax.psum(x, axis)
    step = 1
    while step < n:
        partners = [m * step for m in range(1, 4) if m * step < n]
        got = [lax.ppermute(x, axis, [(i, i ^ d) for i in range(n)]) for d in partners]
        for y in got:
            x = x + y
        step *= 4
    return x


def eye(rows, lanes):
    return lax.broadcasted_iota(jnp.int32, (rows, lanes), 0) == lax.broadcasted_iota(jnp.int32, (rows, lanes), 1)


def as_row(column, lanes):
    return jnp.sum(jnp.where(eye(column.shape[0], lanes), column, 0.0), axis=0, keepdims=True)


def as_column(row, rows):
    return jnp.sum(jnp.where(eye(rows, row.shape[1]), row, 0.0), axis=1, keepdims=True)


def right_side_of(probes_ref, gradient_ref, b, bs, rows):
    count = probes_ref.shape[0]
    return jnp.concatenate(
        [probes_ref[:, b * bs : (b + 1) * bs], jnp.broadcast_to(gradient_ref[b : b + 1], (rows - count, bs))], axis=0
    )


def project_kernel(
    rows, latent_hbm, responses_hbm, prior_hbm, probes_hbm, map_hbm, inner_hbm, out_ref, terms_ref, probes_ref, map_ref,
    inner_ref, latent_ref, responses_ref, prior_ref, sems,
):
    blocks, bs = latent_ref.shape
    count = probes_ref.shape[0]
    points = map_ref.shape[0]
    part = points // MAP_PARTS
    cut = lambda ref, i: ref.at[i * part : (i + 1) * part]
    pairs = [(latent_hbm, latent_ref), (responses_hbm, responses_ref), (prior_hbm, prior_ref), (probes_hbm, probes_ref)]
    pairs += [(cut(map_hbm, i), cut(map_ref, i)) for i in range(MAP_PARTS)] + [(inner_hbm, inner_ref)]
    copies = [pltpu.make_async_copy(a, b, sems.at[i]) for i, (a, b) in enumerate(pairs)]
    for copy in copies:
        copy.start()
    for copy in copies[:3]:
        copy.wait()
    probability = 1.0 / (1.0 + jnp.exp(-latent_ref[...]))
    weights = probability * (1.0 - probability)
    gradient_ref, weights_ref, inv_diag_ref = terms_ref.at[0], terms_ref.at[1], terms_ref.at[2]
    gradient_ref[...] = responses_ref[...].astype(F32) - probability
    weights_ref[...] = weights
    inv_diag_ref[...] = 1.0 / (weights + prior_ref[...])
    copies[3].wait()
    energy = jnp.zeros((rows, bs), F32)
    summed = jnp.zeros((rows, map_ref.shape[1]), F32)
    for b in range(0, blocks, PAIR):
        if b * bs % part == 0:
            copies[4 + b * bs // part].wait()
        parts = []
        for c in range(b, b + PAIR):
            field = right_side_of(probes_ref, gradient_ref, c, bs, rows)
            scaled = field * inv_diag_ref[c : c + 1]
            energy += field * scaled
            parts.append(scaled.astype(BF16))
        summed += jnp.dot(
            jnp.concatenate(parts, axis=1), map_ref[b * bs : (b + PAIR) * bs], preferred_element_type=F32
        )
    out_ref[...] = summed
    out_ref[count + 1 : count + 2] = as_row(jnp.sum(energy, axis=1, keepdims=True), map_ref.shape[1])
    copies[-1].wait()


def direction_kernel(
    rows, sums_ref, inner_ref, terms_ref, probes_ref, map_ref, dir_ref, msg_ref, product_ref, grad_ref
):
    _, blocks, bs = terms_ref.shape
    count = probes_ref.shape[0]
    gradient_ref, inv_diag_ref = terms_ref.at[0], terms_ref.at[2]
    product = jnp.dot(sums_ref[...], inner_ref[...], precision=lax.Precision.HIGHEST)
    product_ref[...] = product
    coeffs = product.astype(BF16)
    for b in range(0, blocks, PAIR):
        correction = lax.dot_general(
            coeffs, map_ref[b * bs : (b + PAIR) * bs], (((1,), (1,)), ((), ())), preferred_element_type=F32
        )
        for c in range(b, b + PAIR):
            field = right_side_of(probes_ref, gradient_ref, c, bs, rows)
            direction = (field + correction[:, (c - b) * bs : (c - b + 1) * bs]) * inv_diag_ref[c : c + 1]
            dir_ref[c] = direction
            msg_ref[c] = direction[:count].astype(BF16)
            grad_ref[c : c + 1] = direction[count : count + 1]
    msg_ref[blocks] = grad_ref[...].astype(BF16)


def hessian_kernel(
    rows, ids_ref, factor_hbm, far_ref, near_ref, own_ref, back_far_ref, back_near_ref, back_own_ref, curve_ref,
    around_ref, around_grad_ref, image_ref, total_ref, grad_ref, factor_ref, sems,
):
    blocks, taps, bs, _ = factor_ref.shape
    part = blocks // FACTOR_PARTS
    cut = lambda ref, i: ref.at[i * part : (i + 1) * part]
    copies = [
        pltpu.make_async_copy(cut(factor_hbm, i), cut(factor_ref, i), sems.at[i]) for i in range(FACTOR_PARTS)
    ]
    for copy in copies:
        copy.start()
    count = around_ref.shape[1]
    tall = image_ref.shape[1]
    for i, ref in enumerate((far_ref, near_ref, own_ref)):
        around_ref[i * blocks : (i + 1) * blocks] = ref[:blocks]
        around_grad_ref[i * blocks : (i + 1) * blocks] = ref[blocks].astype(F32)
    total_ref[...] = jnp.zeros_like(total_ref)
    curve = jnp.zeros((rows, bs), F32)
    for b in range(blocks):
        if b % part == 0:
            copies[b // part].wait()
        chosen = []
        for k in range(taps):
            at = 2 * blocks + b if k == 0 else ids_ref[b, k - 1]
            last = jnp.broadcast_to(around_grad_ref[pl.ds(at, 1), :], (tall - count, bs)).astype(BF16)
            chosen.append(jnp.concatenate([around_ref[at], last], axis=0))
        side_by_side = jnp.concatenate([factor_ref[b, k] for k in range(taps)], axis=1)
        image = lax.dot_general(
            jnp.concatenate(chosen, axis=1), side_by_side, (((1,), (1,)), ((), ())), preferred_element_type=F32
        )
        rounded = image.astype(BF16)
        image_ref[b] = rounded
        curve += (image * rounded.astype(F32))[:rows]
    curve_ref[...] = curve
    for b in range(blocks):
        side_by_side = jnp.concatenate([factor_ref[b, k] for k in range(taps)], axis=1)
        back = jnp.dot(image_ref[b], side_by_side, preferred_element_type=F32)
        for k in range(taps):
            at = 2 * blocks + b if k == 0 else ids_ref[b, k - 1]
            total_ref[at] += back[:rows, k * bs : (k + 1) * bs]
    for i, ref in enumerate((back_far_ref, back_near_ref)):
        for b in range(blocks):
            ref[b] = total_ref[i * blocks + b, :count].astype(BF16)
            grad_ref[b : b + 1] = total_ref[i * blocks + b, count : count + 1]
        ref[blocks] = grad_ref[...].astype(BF16)
    back_own_ref[...] = total_ref[2 * blocks :]


def combine_kernel(
    rows, own_ref, near_ref, far_ref, curve_ref, dir_ref, terms_ref, probes_ref, map_ref, hess_ref, out_ref
):
    _, blocks, bs = terms_ref.shape
    count = probes_ref.shape[0]
    lanes = map_ref.shape[1]
    gradient_ref, weights_ref, inv_diag_ref = terms_ref.at[0], terms_ref.at[1], terms_ref.at[2]
    from_grad = near_ref[blocks].astype(F32) + far_ref[blocks].astype(F32)
    curve = curve_ref[...]
    cross = jnp.zeros((rows, bs), F32)
    square = jnp.zeros((rows, bs), F32)
    summed = jnp.zeros((rows, lanes), F32)
    for b in range(0, blocks, PAIR):
        parts = []
        for c in range(b, b + PAIR):
            came = jnp.concatenate(
                [
                    near_ref[c].astype(F32) + far_ref[c].astype(F32),
                    jnp.broadcast_to(from_grad[c : c + 1], (rows - count, bs)),
                ],
                axis=0,
            )
            direction = dir_ref[c]
            weighted = weights_ref[c : c + 1] * direction
            hess = own_ref[c] + came + weighted
            hess_ref[c] = hess
            scaled = hess * inv_diag_ref[c : c + 1]
            curve += weighted * direction
            cross += right_side_of(probes_ref, gradient_ref, c, bs, rows) * scaled
            square += hess * scaled
            parts.append(scaled.astype(BF16))
        summed += jnp.dot(
            jnp.concatenate(parts, axis=1), map_ref[b * bs : (b + PAIR) * bs], preferred_element_type=F32
        )
    out_ref[...] = summed
    for i, acc in enumerate((curve, cross, square)):
        out_ref[count + 1 + i : count + 2 + i] = as_row(jnp.sum(acc, axis=1, keepdims=True), lanes)


def finish_kernel(
    rows, sums_ref, product_ref, hess_sums_ref, inner_ref, dir_ref, hess_ref, terms_ref, probes_ref, map_ref,
    solution_ref, residual_ref, next_ref,
):
    _, blocks, bs = terms_ref.shape
    count = probes_ref.shape[0]
    gradient_ref, inv_diag_ref = terms_ref.at[0], terms_ref.at[2]
    sums, product, hess_sums = sums_ref[...], product_ref[...], hess_sums_ref[...]
    column = lambda x, i: as_column(x[count + 1 + i : count + 2 + i], rows)
    coeffs = product.astype(BF16)
    plain = column(sums, 0)
    energy = plain + jnp.sum(coeffs.astype(F32) * sums, axis=1, keepdims=True)
    step = energy / column(hess_sums, 0)
    left = sums - step * hess_sums
    hess_product = jnp.dot(hess_sums, inner_ref[...], precision=lax.Precision.HIGHEST)
    coeffs = (product - step * hess_product).astype(BF16)
    plain_next = plain - 2.0 * step * column(hess_sums, 1) + step * step * column(hess_sums, 2)
    energy_next = plain_next + jnp.sum(coeffs.astype(F32) * left, axis=1, keepdims=True)
    ratio = energy_next / energy
    for b in range(0, blocks, PAIR):
        correction = lax.dot_general(
            coeffs, map_ref[b * bs : (b + PAIR) * bs], (((1,), (1,)), ((), ())), preferred_element_type=F32
        )
        for c in range(b, b + PAIR):
            at = slice(c * bs, (c + 1) * bs)
            direction = dir_ref[c]
            residual = right_side_of(probes_ref, gradient_ref, c, bs, rows) - step * hess_ref[c]
            smoothed = (residual + correction[:, (c - b) * bs : (c - b + 1) * bs]) * inv_diag_ref[c : c + 1]
            for ref, value in (
                (solution_ref, step * direction),
                (residual_ref, residual),
                (next_ref, smoothed + ratio * direction),
            ):
                ref[0:1, at] = value[count : count + 1]
                ref[1 : count + 1, at] = value[:count]


def call(kernel, ins, outs, scratch=(), limit=16, keep=True):
    spec = lambda space: pl.BlockSpec(memory_space=space)
    shapes = tuple((pltpu.VMEM if keep else jax.ShapeDtypeStruct)(s, t) for s, t in outs)
    specs = (spec(pltpu.VMEM),) * len(shapes)
    return pl.pallas_call(
        kernel,
        out_shape=shapes if len(shapes) > 1 else shapes[0],
        in_specs=[spec(space) for space in ins],
        out_specs=specs if len(shapes) > 1 else specs[0],
        scratch_shapes=scratch,
        compiler_params=pltpu.CompilerParams(vmem_limit_bytes=limit * 1024 * 1024),
    )


def in_hbm(x):
    return pltpu.with_memory_space_constraint(x, pltpu.HBM)


def body(latent, responses, probes, prior_diag, factor, cond_ids, inducing_map, inner_inverse):
    blocks, _, bs, _ = factor.shape
    count = probes.shape[0]
    rows, tall = count + 8, count + 16
    by_block = lambda x: x.reshape(blocks, bs)
    sum_shape = ((rows, inducing_map.shape[1]), F32)
    field = ((blocks, rows, bs), F32)
    packed = ((blocks + 1, count, bs), BF16)
    vmem, smem = pltpu.VMEM, pltpu.SMEM
    partial, terms, probes, inducing_map, inner_inverse = call(
        functools.partial(project_kernel, rows),
        [pl.ANY] * 6,
        [sum_shape, ((3, blocks, bs), F32), (probes.shape, F32), (inducing_map.shape, BF16), (inner_inverse.shape, F32)],
        [
            vmem((blocks, bs), F32),
            vmem((blocks, bs), jnp.int32),
            vmem((blocks, bs), F32),
            pltpu.SemaphoreType.DMA((5 + MAP_PARTS,)),
        ],
    )(*map(in_hbm, (by_block(latent), by_block(responses), by_block(prior_diag), probes, inducing_map, inner_inverse)))
    points = (terms, probes, inducing_map)
    sums = total(partial, "space")
    direction, rounded, product = call(
        functools.partial(direction_kernel, rows), [vmem] * 5, [field, packed, sum_shape], [vmem((blocks, bs), F32)]
    )(sums, inner_inverse, *points)
    near = shifted(rounded, "space", 1)
    far = shifted(rounded, "space", 2)
    local_ids = cond_ids - (lax.axis_index("space") - 2) * blocks
    back_far, back_near, back_own, curve = call(
        functools.partial(hessian_kernel, rows),
        [smem, pl.ANY] + [vmem] * 3,
        [packed, packed, field, ((rows, bs), F32)],
        [
            vmem((3 * blocks, count, bs), BF16),
            vmem((3 * blocks, bs), F32),
            vmem((blocks, tall, bs), BF16),
            vmem((3 * blocks, rows, bs), F32),
            vmem((blocks, bs), F32),
            vmem(factor.shape, BF16),
            pltpu.SemaphoreType.DMA((FACTOR_PARTS,)),
        ],
    )(local_ids, in_hbm(factor), far, near, rounded)
    from_near = shifted(back_near, "space", -1)
    from_far = shifted(back_far, "space", -2)
    hess, partial = call(functools.partial(combine_kernel, rows), [vmem] * 8, [field, sum_shape])(
        back_own, from_near, from_far, curve, direction, *points
    )
    hess_sums = total(partial, "space")
    whole = ((count + 1, blocks * bs), F32)
    return call(functools.partial(finish_kernel, rows), [vmem] * 9, [whole] * 3, keep=False)(
        sums, product, hess_sums, inner_inverse, direction, hess, *points
    )


def solution(mesh):
    return jax.shard_map(
        body,
        mesh=mesh,
        in_specs=(
            P(("groups", "space")),
            P(("groups", "space")),
            P(None, ("groups", "space")),
            P(("groups", "space")),
            P(("groups", "space"), None, None, None),
            P(("groups", "space"), None),
            P(("groups", "space"), None),
            P("groups", None),
        ),
        out_specs=(
            P(None, ("groups", "space")),
            P(None, ("groups", "space")),
            P(None, ("groups", "space")),
        ),
        check_vma=False,
    )
```

```python
import functools

import jax
import jax.numpy as jnp
from jax import lax
from jax.experimental import pallas as pl
from jax.experimental.pallas import tpu as pltpu
from jax.sharding import PartitionSpec as P

F32, BF16 = jnp.float32, jnp.bfloat16
PAIR = 2
MAP_PARTS = 4


def shifted(block, axis, distance):
    devices = range(lax.axis_size(axis))
    route = [(i - distance, i) for i in devices if i - distance in devices]
    return lax.ppermute(block, axis, route)


def write_message(msg_ref, x):
    top = x.shape[0] - 8
    tail = x[top:]
    high = tail.astype(BF16).astype(F32)
    middle = (tail - high).astype(BF16).astype(F32)
    low = tail - high - middle
    first = lax.broadcasted_iota(jnp.int32, tail.shape, 0) < 4
    msg_ref[:top] = x[:top].astype(BF16)
    msg_ref[top:] = jnp.concatenate([high, jnp.where(first, middle, pltpu.roll(low, 4, 0))], axis=0).astype(BF16)


def read_message(msg_ref):
    x = msg_ref[...].astype(F32)
    rest = x[-8:]
    first = lax.broadcasted_iota(jnp.int32, rest.shape, 0) < 4
    return jnp.concatenate([x[:-16], x[-16:-8] + jnp.where(first, rest + pltpu.roll(rest, 4, 0), 0.0)], axis=0)


def add_kernel(x_ref, *refs):
    *msg_refs, out_ref, msg_ref = refs
    x = x_ref[...]
    for ref in msg_refs:
        x = x + read_message(ref)
    out_ref[...] = x
    write_message(msg_ref, x)


def total(x, msg, axis):
    n = lax.axis_size(axis)
    if n & (n - 1):
        return lax.psum(x, axis)
    step = 1
    while step < n:
        partners = [m * step for m in range(1, 4) if m * step < n]
        got = [lax.ppermute(msg, axis, [(i, i ^ d) for i in range(n)]) for d in partners]
        x, msg = call(add_kernel, [pltpu.VMEM] * (1 + len(got)), [(x.shape, F32), (msg.shape, BF16)])(x, *got)
        step *= 4
    return x


def eye(rows, lanes):
    return lax.broadcasted_iota(jnp.int32, (rows, lanes), 0) == lax.broadcasted_iota(jnp.int32, (rows, lanes), 1)


def as_row(column, lanes):
    return jnp.sum(jnp.where(eye(column.shape[0], lanes), column, 0.0), axis=0, keepdims=True)


def as_column(row, rows):
    return jnp.sum(jnp.where(eye(rows, row.shape[1]), row, 0.0), axis=1, keepdims=True)


def right_side_of(probes_ref, gradient_ref, b, bs, rows):
    count = probes_ref.shape[0]
    return jnp.concatenate(
        [probes_ref[:, b * bs : (b + 1) * bs], jnp.broadcast_to(gradient_ref[b : b + 1], (rows - count, bs))], axis=0
    )


def project_kernel(
    rows, latent_hbm, responses_hbm, prior_hbm, probes_hbm, map_hbm, inner_hbm, out_ref, msg_ref, terms_ref, probes_ref,
    map_ref, inner_ref, latent_ref, responses_ref, prior_ref, sems,
):
    blocks, bs = latent_ref.shape
    count = probes_ref.shape[0]
    points = map_ref.shape[0]
    part = points // MAP_PARTS
    cut = lambda ref, i: ref.at[i * part : (i + 1) * part]
    pairs = [(latent_hbm, latent_ref), (responses_hbm, responses_ref), (prior_hbm, prior_ref), (probes_hbm, probes_ref)]
    pairs += [(cut(map_hbm, i), cut(map_ref, i)) for i in range(MAP_PARTS)] + [(inner_hbm, inner_ref)]
    copies = [pltpu.make_async_copy(a, b, sems.at[i]) for i, (a, b) in enumerate(pairs)]
    for copy in copies:
        copy.start()
    for copy in copies[:3]:
        copy.wait()
    probability = 1.0 / (1.0 + jnp.exp(-latent_ref[...]))
    weights = probability * (1.0 - probability)
    gradient_ref, weights_ref, inv_diag_ref = terms_ref.at[0], terms_ref.at[1], terms_ref.at[2]
    gradient_ref[...] = responses_ref[...].astype(F32) - probability
    weights_ref[...] = weights
    inv_diag_ref[...] = 1.0 / (weights + prior_ref[...])
    copies[3].wait()
    energy = jnp.zeros((rows, bs), F32)
    summed = jnp.zeros((rows, map_ref.shape[1]), F32)
    for b in range(0, blocks, PAIR):
        if b * bs % part == 0:
            copies[4 + b * bs // part].wait()
        parts = []
        for c in range(b, b + PAIR):
            field = right_side_of(probes_ref, gradient_ref, c, bs, rows)
            scaled = field * inv_diag_ref[c : c + 1]
            energy += field * scaled
            parts.append(scaled.astype(BF16))
        summed += jnp.dot(
            jnp.concatenate(parts, axis=1), map_ref[b * bs : (b + PAIR) * bs], preferred_element_type=F32
        )
    out_ref[...] = summed
    out_ref[count + 1 : count + 2] = as_row(jnp.sum(energy, axis=1, keepdims=True), map_ref.shape[1])
    write_message(msg_ref, out_ref[...])
    copies[-1].wait()


def direction_kernel(
    rows, sums_ref, inner_ref, terms_ref, probes_ref, map_ref, factor_hbm, dir_ref, msg_ref, product_ref, factor_ref,
    grad_ref, sem,
):
    copy = pltpu.make_async_copy(factor_hbm, factor_ref, sem)
    copy.start()
    _, blocks, bs = terms_ref.shape
    count = probes_ref.shape[0]
    gradient_ref, inv_diag_ref = terms_ref.at[0], terms_ref.at[2]
    product = jnp.dot(sums_ref[...], inner_ref[...], precision=lax.Precision.HIGHEST)
    product_ref[...] = product
    coeffs = product.astype(BF16)
    for b in range(0, blocks, PAIR):
        correction = lax.dot_general(
            coeffs, map_ref[b * bs : (b + PAIR) * bs], (((1,), (1,)), ((), ())), preferred_element_type=F32
        )
        for c in range(b, b + PAIR):
            field = right_side_of(probes_ref, gradient_ref, c, bs, rows)
            direction = (field + correction[:, (c - b) * bs : (c - b + 1) * bs]) * inv_diag_ref[c : c + 1]
            dir_ref[c] = direction
            msg_ref[c] = direction[:count].astype(BF16)
            grad_ref[c : c + 1] = direction[count : count + 1]
    msg_ref[blocks] = grad_ref[...].astype(BF16)
    copy.wait()


def hessian_kernel(
    rows, ids_ref, factor_ref, near_ref, far_ref, own_ref, back_far_ref, back_near_ref, back_own_ref, curve_ref,
    around_ref, around_grad_ref, image_ref, total_ref, grad_ref,
):
    blocks, taps, bs, _ = factor_ref.shape
    count = around_ref.shape[1]
    tall = image_ref.shape[1]
    for i, ref in enumerate((far_ref, near_ref, own_ref)):
        around_ref[i * blocks : (i + 1) * blocks] = ref[:blocks]
        around_grad_ref[i * blocks : (i + 1) * blocks] = ref[blocks].astype(F32)
    total_ref[...] = jnp.zeros_like(total_ref)
    curve = jnp.zeros((rows, bs), F32)
    for b in range(blocks):
        chosen = []
        for k in range(taps):
            at = 2 * blocks + b if k == 0 else ids_ref[b, k - 1]
            last = jnp.broadcast_to(around_grad_ref[pl.ds(at, 1), :], (tall - count, bs)).astype(BF16)
            chosen.append(jnp.concatenate([around_ref[at], last], axis=0))
        side_by_side = jnp.concatenate([factor_ref[b, k] for k in range(taps)], axis=1)
        image = lax.dot_general(
            jnp.concatenate(chosen, axis=1), side_by_side, (((1,), (1,)), ((), ())), preferred_element_type=F32
        )
        rounded = image.astype(BF16)
        image_ref[b] = rounded
        curve += (image * rounded.astype(F32))[:rows]
    curve_ref[...] = curve
    for b in range(blocks):
        side_by_side = jnp.concatenate([factor_ref[b, k] for k in range(taps)], axis=1)
        back = jnp.dot(image_ref[b], side_by_side, preferred_element_type=F32)
        for k in range(taps):
            at = 2 * blocks + b if k == 0 else ids_ref[b, k - 1]
            total_ref[at] += back[:rows, k * bs : (k + 1) * bs]
    for i, ref in enumerate((back_far_ref, back_near_ref)):
        for b in range(blocks):
            ref[b] = total_ref[i * blocks + b, :count].astype(BF16)
            grad_ref[b : b + 1] = total_ref[i * blocks + b, count : count + 1]
        ref[blocks] = grad_ref[...].astype(BF16)
    back_own_ref[...] = total_ref[2 * blocks :]


def combine_kernel(
    rows, own_ref, far_ref, near_ref, curve_ref, dir_ref, terms_ref, probes_ref, map_ref, hess_ref, out_ref, msg_ref
):
    _, blocks, bs = terms_ref.shape
    count = probes_ref.shape[0]
    lanes = map_ref.shape[1]
    gradient_ref, weights_ref, inv_diag_ref = terms_ref.at[0], terms_ref.at[1], terms_ref.at[2]
    from_grad = near_ref[blocks].astype(F32) + far_ref[blocks].astype(F32)
    curve = curve_ref[...]
    cross = jnp.zeros((rows, bs), F32)
    square = jnp.zeros((rows, bs), F32)
    summed = jnp.zeros((rows, lanes), F32)
    for b in range(0, blocks, PAIR):
        parts = []
        for c in range(b, b + PAIR):
            came = jnp.concatenate(
                [
                    near_ref[c].astype(F32) + far_ref[c].astype(F32),
                    jnp.broadcast_to(from_grad[c : c + 1], (rows - count, bs)),
                ],
                axis=0,
            )
            direction = dir_ref[c]
            weighted = weights_ref[c : c + 1] * direction
            hess = own_ref[c] + came + weighted
            hess_ref[c] = hess
            scaled = hess * inv_diag_ref[c : c + 1]
            curve += weighted * direction
            cross += right_side_of(probes_ref, gradient_ref, c, bs, rows) * scaled
            square += hess * scaled
            parts.append(scaled.astype(BF16))
        summed += jnp.dot(
            jnp.concatenate(parts, axis=1), map_ref[b * bs : (b + PAIR) * bs], preferred_element_type=F32
        )
    out_ref[...] = summed
    for i, acc in enumerate((curve, cross, square)):
        out_ref[count + 1 + i : count + 2 + i] = as_row(jnp.sum(acc, axis=1, keepdims=True), lanes)
    write_message(msg_ref, out_ref[...])


def finish_kernel(
    rows, sums_ref, product_ref, hess_sums_ref, inner_ref, dir_ref, hess_ref, terms_ref, probes_ref, map_ref,
    solution_ref, residual_ref, next_ref,
):
    _, blocks, bs = terms_ref.shape
    count = probes_ref.shape[0]
    gradient_ref, inv_diag_ref = terms_ref.at[0], terms_ref.at[2]
    sums, product, hess_sums = sums_ref[...], product_ref[...], hess_sums_ref[...]
    column = lambda x, i: as_column(x[count + 1 + i : count + 2 + i], rows)
    coeffs = product.astype(BF16)
    plain = column(sums, 0)
    energy = plain + jnp.sum(coeffs.astype(F32) * sums, axis=1, keepdims=True)
    step = energy / column(hess_sums, 0)
    left = sums - step * hess_sums
    hess_product = jnp.dot(hess_sums, inner_ref[...], precision=lax.Precision.HIGHEST)
    coeffs = (product - step * hess_product).astype(BF16)
    plain_next = plain - 2.0 * step * column(hess_sums, 1) + step * step * column(hess_sums, 2)
    energy_next = plain_next + jnp.sum(coeffs.astype(F32) * left, axis=1, keepdims=True)
    ratio = energy_next / energy
    for b in range(0, blocks, PAIR):
        correction = lax.dot_general(
            coeffs, map_ref[b * bs : (b + PAIR) * bs], (((1,), (1,)), ((), ())), preferred_element_type=F32
        )
        for c in range(b, b + PAIR):
            at = slice(c * bs, (c + 1) * bs)
            direction = dir_ref[c]
            residual = right_side_of(probes_ref, gradient_ref, c, bs, rows) - step * hess_ref[c]
            smoothed = (residual + correction[:, (c - b) * bs : (c - b + 1) * bs]) * inv_diag_ref[c : c + 1]
            for ref, value in (
                (solution_ref, step * direction),
                (residual_ref, residual),
                (next_ref, smoothed + ratio * direction),
            ):
                ref[0:1, at] = value[count : count + 1]
                ref[1 : count + 1, at] = value[:count]


def call(kernel, ins, outs, scratch=(), limit=16, keep=True):
    spec = lambda space: pl.BlockSpec(memory_space=space)
    shapes = tuple((pltpu.VMEM if keep else jax.ShapeDtypeStruct)(s, t) for s, t in outs)
    specs = (spec(pltpu.VMEM),) * len(shapes)
    return pl.pallas_call(
        kernel,
        out_shape=shapes if len(shapes) > 1 else shapes[0],
        in_specs=[spec(space) for space in ins],
        out_specs=specs if len(shapes) > 1 else specs[0],
        scratch_shapes=scratch,
        compiler_params=pltpu.CompilerParams(vmem_limit_bytes=limit * 1024 * 1024),
    )


def in_hbm(x):
    return pltpu.with_memory_space_constraint(x, pltpu.HBM)


def in_vmem(x):
    return pltpu.with_memory_space_constraint(x, pltpu.VMEM)


def body(latent, responses, probes, prior_diag, factor, cond_ids, inducing_map, inner_inverse):
    blocks, _, bs, _ = factor.shape
    count = probes.shape[0]
    rows, tall = count + 8, count + 16
    by_block = lambda x: x.reshape(blocks, bs)
    sum_shape = ((rows, inducing_map.shape[1]), F32)
    sum_msg = ((tall, inducing_map.shape[1]), BF16)
    field = ((blocks, rows, bs), F32)
    packed = ((blocks + 1, count, bs), BF16)
    vmem, smem = pltpu.VMEM, pltpu.SMEM
    partial, msg, terms, probes, inducing_map, inner_inverse = call(
        functools.partial(project_kernel, rows),
        [pl.ANY] * 6,
        [
            sum_shape,
            sum_msg,
            ((3, blocks, bs), F32),
            (probes.shape, F32),
            (inducing_map.shape, BF16),
            (inner_inverse.shape, F32),
        ],
        [
            vmem((blocks, bs), F32),
            vmem((blocks, bs), jnp.int32),
            vmem((blocks, bs), F32),
            pltpu.SemaphoreType.DMA((5 + MAP_PARTS,)),
        ],
    )(*map(in_hbm, (by_block(latent), by_block(responses), by_block(prior_diag), probes, inducing_map, inner_inverse)))
    points = (terms, probes, inducing_map)
    sums = total(partial, msg, "space")
    direction, rounded, product, factor = call(
        functools.partial(direction_kernel, rows),
        [vmem] * 5 + [pl.ANY],
        [field, packed, sum_shape, (factor.shape, BF16)],
        [vmem((blocks, bs), F32), pltpu.SemaphoreType.DMA],
    )(sums, inner_inverse, *points, in_hbm(factor))
    far = shifted(rounded, "space", 2)
    near = shifted(rounded, "space", 1)
    local_ids = cond_ids - (lax.axis_index("space") - 2) * blocks
    back_far, back_near, back_own, curve = call(
        functools.partial(hessian_kernel, rows),
        [smem] + [vmem] * 4,
        [packed, packed, field, ((rows, bs), F32)],
        [
            vmem((3 * blocks, count, bs), BF16),
            vmem((3 * blocks, bs), F32),
            vmem((blocks, tall, bs), BF16),
            vmem((3 * blocks, rows, bs), F32),
            vmem((blocks, bs), F32),
        ],
    )(local_ids, factor, near, far, rounded)
    from_far = shifted(back_far, "space", -2)
    from_near = shifted(back_near, "space", -1)
    hess, partial, msg = call(functools.partial(combine_kernel, rows), [vmem] * 8, [field, sum_shape, sum_msg])(
        back_own, from_far, from_near, curve, direction, *points
    )
    hess_sums = total(partial, msg, "space")
    whole = ((count + 1, blocks * bs), F32)
    return call(functools.partial(finish_kernel, rows), [vmem] * 9, [whole] * 3, keep=False)(
        *map(in_vmem, (sums, product, hess_sums, inner_inverse, direction, hess, *points))
    )


def solution(mesh):
    return jax.shard_map(
        body,
        mesh=mesh,
        in_specs=(
            P(("groups", "space")),
            P(("groups", "space")),
            P(None, ("groups", "space")),
            P(("groups", "space")),
            P(("groups", "space"), None, None, None),
            P(("groups", "space"), None),
            P(("groups", "space"), None),
            P("groups", None),
        ),
        out_specs=(
            P(None, ("groups", "space")),
            P(None, ("groups", "space")),
            P(None, ("groups", "space")),
        ),
        check_vma=False,
    )
```

```python
import functools

import jax
import jax.numpy as jnp
from jax import lax
from jax.experimental import pallas as pl
from jax.experimental.pallas import tpu as pltpu
from jax.sharding import PartitionSpec as P

F32, BF16 = jnp.float32, jnp.bfloat16
PAIR = 2
MAP_PARTS = 4


def shifted(block, axis, distance):
    devices = range(lax.axis_size(axis))
    route = [(i - distance, i) for i in devices if i - distance in devices]
    return lax.ppermute(block, axis, route)


def write_message(msg_ref, x):
    top = x.shape[0] - 8
    tail = x[top:]
    high = tail.astype(BF16).astype(F32)
    middle = (tail - high).astype(BF16).astype(F32)
    low = tail - high - middle
    first = lax.broadcasted_iota(jnp.int32, tail.shape, 0) < 4
    msg_ref[:top] = x[:top].astype(BF16)
    msg_ref[top:] = jnp.concatenate([high, jnp.where(first, middle, pltpu.roll(low, 4, 0))], axis=0).astype(BF16)


def read_message(msg_ref):
    x = msg_ref[...].astype(F32)
    rest = x[-8:]
    first = lax.broadcasted_iota(jnp.int32, rest.shape, 0) < 4
    return jnp.concatenate([x[:-16], x[-16:-8] + jnp.where(first, rest + pltpu.roll(rest, 4, 0), 0.0)], axis=0)


def add_kernel(count, x_ref, *refs):
    *in_refs, out_ref = refs[:count]
    x = x_ref[...]
    for ref in in_refs:
        x = x + read_message(ref)
    out_ref[...] = x
    for ref in refs[count:]:
        write_message(ref, x)


def total(x, msg, axis):
    n = lax.axis_size(axis)
    if n & (n - 1):
        return lax.psum(x, axis)
    step = 1
    while step < n:
        partners = [m * step for m in range(1, 4) if m * step < n]
        got = [lax.ppermute(msg, axis, [(i, i ^ d) for i in range(n)]) for d in partners]
        step *= 4
        add = functools.partial(add_kernel, len(got) + 1)
        ins = [pltpu.VMEM] * (len(got) + 1)
        if step < n:
            x, msg = call(add, ins, [(x.shape, F32), (msg.shape, BF16)])(x, *got)
        else:
            x = call(add, ins, [(x.shape, F32)])(x, *got)
    return x


def eye(rows, lanes):
    return lax.broadcasted_iota(jnp.int32, (rows, lanes), 0) == lax.broadcasted_iota(jnp.int32, (rows, lanes), 1)


def as_row(column, lanes):
    return jnp.sum(jnp.where(eye(column.shape[0], lanes), column, 0.0), axis=0, keepdims=True)


def as_column(row, rows):
    return jnp.sum(jnp.where(eye(rows, row.shape[1]), row, 0.0), axis=1, keepdims=True)


def right_side_of(probes_ref, gradient_ref, b, bs, rows):
    count = probes_ref.shape[0]
    return jnp.concatenate(
        [probes_ref[:, b * bs : (b + 1) * bs], jnp.broadcast_to(gradient_ref[b : b + 1], (rows - count, bs))], axis=0
    )


def project_kernel(
    rows, latent_hbm, responses_hbm, prior_hbm, probes_hbm, map_hbm, inner_hbm, out_ref, msg_ref, terms_ref, probes_ref,
    map_ref, inner_ref, latent_ref, responses_ref, prior_ref, sems,
):
    blocks, bs = latent_ref.shape
    count = probes_ref.shape[0]
    points = map_ref.shape[0]
    part = points // MAP_PARTS
    cut = lambda ref, i: ref.at[i * part : (i + 1) * part]
    pairs = [(latent_hbm, latent_ref), (responses_hbm, responses_ref), (prior_hbm, prior_ref), (probes_hbm, probes_ref)]
    pairs += [(cut(map_hbm, i), cut(map_ref, i)) for i in range(MAP_PARTS)] + [(inner_hbm, inner_ref)]
    copies = [pltpu.make_async_copy(a, b, sems.at[i]) for i, (a, b) in enumerate(pairs)]
    for copy in copies:
        copy.start()
    for copy in copies[:3]:
        copy.wait()
    probability = 1.0 / (1.0 + jnp.exp(-latent_ref[...]))
    weights = probability * (1.0 - probability)
    gradient_ref, weights_ref, inv_diag_ref = terms_ref.at[0], terms_ref.at[1], terms_ref.at[2]
    gradient_ref[...] = responses_ref[...].astype(F32) - probability
    weights_ref[...] = weights
    inv_diag_ref[...] = 1.0 / (weights + prior_ref[...])
    copies[3].wait()
    energy = jnp.zeros((rows, bs), F32)
    summed = jnp.zeros((rows, map_ref.shape[1]), F32)
    for b in range(0, blocks, PAIR):
        if b * bs % part == 0:
            copies[4 + b * bs // part].wait()
        parts = []
        for c in range(b, b + PAIR):
            field = right_side_of(probes_ref, gradient_ref, c, bs, rows)
            scaled = field * inv_diag_ref[c : c + 1]
            energy += field * scaled
            parts.append(scaled.astype(BF16))
        summed += jnp.dot(
            jnp.concatenate(parts, axis=1), map_ref[b * bs : (b + PAIR) * bs], preferred_element_type=F32
        )
    out_ref[...] = summed
    out_ref[count + 1 : count + 2] = as_row(jnp.sum(energy, axis=1, keepdims=True), map_ref.shape[1])
    write_message(msg_ref, out_ref[...])
    copies[-1].wait()


def direction_kernel(
    rows, sums_ref, inner_ref, terms_ref, probes_ref, map_ref, factor_hbm, dir_ref, msg_ref, product_ref, factor_ref,
    grad_ref, sem,
):
    copy = pltpu.make_async_copy(factor_hbm, factor_ref, sem)
    copy.start()
    _, blocks, bs = terms_ref.shape
    count = probes_ref.shape[0]
    gradient_ref, inv_diag_ref = terms_ref.at[0], terms_ref.at[2]
    product = jnp.dot(sums_ref[...], inner_ref[...], precision=lax.Precision.HIGHEST)
    product_ref[...] = product
    coeffs = product.astype(BF16)
    for b in range(0, blocks, PAIR):
        correction = lax.dot_general(
            coeffs, map_ref[b * bs : (b + PAIR) * bs], (((1,), (1,)), ((), ())), preferred_element_type=F32
        )
        for c in range(b, b + PAIR):
            field = right_side_of(probes_ref, gradient_ref, c, bs, rows)
            direction = (field + correction[:, (c - b) * bs : (c - b + 1) * bs]) * inv_diag_ref[c : c + 1]
            dir_ref[c] = direction
            msg_ref[c] = direction[:count].astype(BF16)
            grad_ref[c : c + 1] = direction[count : count + 1]
    msg_ref[blocks] = grad_ref[...].astype(BF16)
    copy.wait()


def hessian_kernel(
    rows, ids_ref, factor_ref, near_ref, far_ref, own_ref, back_far_ref, back_near_ref, back_own_ref, curve_ref,
    around_ref, around_grad_ref, image_ref, total_ref, grad_ref,
):
    blocks, taps, bs, _ = factor_ref.shape
    count = around_ref.shape[1]
    tall = image_ref.shape[1]
    for i, ref in enumerate((far_ref, near_ref, own_ref)):
        around_ref[i * blocks : (i + 1) * blocks] = ref[:blocks]
        around_grad_ref[i * blocks : (i + 1) * blocks] = ref[blocks].astype(F32)
    first = (lax.axis_index("space") - 2) * blocks
    total_ref[...] = jnp.zeros_like(total_ref)
    curve = jnp.zeros((rows, bs), F32)
    for b in range(blocks):
        chosen = []
        for k in range(taps):
            at = 2 * blocks + b if k == 0 else ids_ref[k - 1, b] - first
            last = jnp.broadcast_to(around_grad_ref[pl.ds(at, 1), :], (tall - count, bs)).astype(BF16)
            chosen.append(jnp.concatenate([around_ref[at], last], axis=0))
        side_by_side = jnp.concatenate([factor_ref[b, k] for k in range(taps)], axis=1)
        image = lax.dot_general(
            jnp.concatenate(chosen, axis=1), side_by_side, (((1,), (1,)), ((), ())), preferred_element_type=F32
        )
        rounded = image.astype(BF16)
        image_ref[b] = rounded
        curve += (image * rounded.astype(F32))[:rows]
    curve_ref[...] = curve
    for b in range(blocks):
        side_by_side = jnp.concatenate([factor_ref[b, k] for k in range(taps)], axis=1)
        back = jnp.dot(image_ref[b], side_by_side, preferred_element_type=F32)
        for k in range(taps):
            at = 2 * blocks + b if k == 0 else ids_ref[k - 1, b] - first
            total_ref[at] += back[:rows, k * bs : (k + 1) * bs]
    for i, ref in enumerate((back_far_ref, back_near_ref)):
        for b in range(blocks):
            ref[b] = total_ref[i * blocks + b, :count].astype(BF16)
            grad_ref[b : b + 1] = total_ref[i * blocks + b, count : count + 1]
        ref[blocks] = grad_ref[...].astype(BF16)
    back_own_ref[...] = total_ref[2 * blocks :]


def combine_kernel(
    rows, own_ref, far_ref, near_ref, curve_ref, dir_ref, terms_ref, probes_ref, map_ref, hess_ref, out_ref, msg_ref
):
    _, blocks, bs = terms_ref.shape
    count = probes_ref.shape[0]
    lanes = map_ref.shape[1]
    gradient_ref, weights_ref, inv_diag_ref = terms_ref.at[0], terms_ref.at[1], terms_ref.at[2]
    from_grad = near_ref[blocks].astype(F32) + far_ref[blocks].astype(F32)
    curve = curve_ref[...]
    cross = jnp.zeros((rows, bs), F32)
    square = jnp.zeros((rows, bs), F32)
    summed = jnp.zeros((rows, lanes), F32)
    for b in range(0, blocks, PAIR):
        parts = []
        for c in range(b, b + PAIR):
            came = jnp.concatenate(
                [
                    near_ref[c].astype(F32) + far_ref[c].astype(F32),
                    jnp.broadcast_to(from_grad[c : c + 1], (rows - count, bs)),
                ],
                axis=0,
            )
            direction = dir_ref[c]
            weighted = weights_ref[c : c + 1] * direction
            hess = own_ref[c] + came + weighted
            hess_ref[c] = hess
            scaled = hess * inv_diag_ref[c : c + 1]
            curve += weighted * direction
            cross += right_side_of(probes_ref, gradient_ref, c, bs, rows) * scaled
            square += hess * scaled
            parts.append(scaled.astype(BF16))
        summed += jnp.dot(
            jnp.concatenate(parts, axis=1), map_ref[b * bs : (b + PAIR) * bs], preferred_element_type=F32
        )
    out_ref[...] = summed
    for i, acc in enumerate((curve, cross, square)):
        out_ref[count + 1 + i : count + 2 + i] = as_row(jnp.sum(acc, axis=1, keepdims=True), lanes)
    write_message(msg_ref, out_ref[...])


def finish_kernel(
    rows, sums_ref, product_ref, hess_sums_ref, inner_ref, dir_ref, hess_ref, terms_ref, probes_ref, map_ref,
    solution_ref, residual_ref, next_ref,
):
    _, blocks, bs = terms_ref.shape
    count = probes_ref.shape[0]
    gradient_ref, inv_diag_ref = terms_ref.at[0], terms_ref.at[2]
    sums, product, hess_sums = sums_ref[...], product_ref[...], hess_sums_ref[...]
    column = lambda x, i: as_column(x[count + 1 + i : count + 2 + i], rows)
    coeffs = product.astype(BF16)
    plain = column(sums, 0)
    energy = plain + jnp.sum(coeffs.astype(F32) * sums, axis=1, keepdims=True)
    step = energy / column(hess_sums, 0)
    left = sums - step * hess_sums
    hess_product = jnp.dot(hess_sums, inner_ref[...], precision=lax.Precision.HIGHEST)
    coeffs = (product - step * hess_product).astype(BF16)
    plain_next = plain - 2.0 * step * column(hess_sums, 1) + step * step * column(hess_sums, 2)
    energy_next = plain_next + jnp.sum(coeffs.astype(F32) * left, axis=1, keepdims=True)
    ratio = energy_next / energy
    for b in range(0, blocks, PAIR):
        correction = lax.dot_general(
            coeffs, map_ref[b * bs : (b + PAIR) * bs], (((1,), (1,)), ((), ())), preferred_element_type=F32
        )
        for c in range(b, b + PAIR):
            at = slice(c * bs, (c + 1) * bs)
            direction = dir_ref[c]
            residual = right_side_of(probes_ref, gradient_ref, c, bs, rows) - step * hess_ref[c]
            smoothed = (residual + correction[:, (c - b) * bs : (c - b + 1) * bs]) * inv_diag_ref[c : c + 1]
            for ref, value in (
                (solution_ref, step * direction),
                (residual_ref, residual),
                (next_ref, smoothed + ratio * direction),
            ):
                ref[0:1, at] = value[count : count + 1]
                ref[1 : count + 1, at] = value[:count]


def call(kernel, ins, outs, scratch=(), limit=16, keep=True):
    spec = lambda space: pl.BlockSpec(memory_space=space)
    shapes = tuple((pltpu.VMEM if keep else jax.ShapeDtypeStruct)(s, t) for s, t in outs)
    specs = (spec(pltpu.VMEM),) * len(shapes)
    return pl.pallas_call(
        kernel,
        out_shape=shapes if len(shapes) > 1 else shapes[0],
        in_specs=[spec(space) for space in ins],
        out_specs=specs if len(shapes) > 1 else specs[0],
        scratch_shapes=scratch,
        compiler_params=pltpu.CompilerParams(vmem_limit_bytes=limit * 1024 * 1024),
    )


def in_hbm(x):
    return pltpu.with_memory_space_constraint(x, pltpu.HBM)


def in_vmem(x):
    return pltpu.with_memory_space_constraint(x, pltpu.VMEM)


def body(latent, responses, probes, prior_diag, factor, cond_ids, inducing_map, inner_inverse):
    blocks, _, bs, _ = factor.shape
    count = probes.shape[0]
    rows, tall = count + 8, count + 16
    by_block = lambda x: x.reshape(blocks, bs)
    sum_shape = ((rows, inducing_map.shape[1]), F32)
    sum_msg = ((tall, inducing_map.shape[1]), BF16)
    field = ((blocks, rows, bs), F32)
    packed = ((blocks + 1, count, bs), BF16)
    vmem, smem = pltpu.VMEM, pltpu.SMEM
    partial, msg, terms, probes, inducing_map, inner_inverse = call(
        functools.partial(project_kernel, rows),
        [pl.ANY] * 6,
        [
            sum_shape,
            sum_msg,
            ((3, blocks, bs), F32),
            (probes.shape, F32),
            (inducing_map.shape, BF16),
            (inner_inverse.shape, F32),
        ],
        [
            vmem((blocks, bs), F32),
            vmem((blocks, bs), jnp.int32),
            vmem((blocks, bs), F32),
            pltpu.SemaphoreType.DMA((5 + MAP_PARTS,)),
        ],
    )(*map(in_hbm, (by_block(latent), by_block(responses), by_block(prior_diag), probes, inducing_map, inner_inverse)))
    points = (terms, probes, inducing_map)
    sums = total(partial, msg, "space")
    direction, rounded, product, factor = call(
        functools.partial(direction_kernel, rows),
        [vmem] * 5 + [pl.ANY],
        [field, packed, sum_shape, (factor.shape, BF16)],
        [vmem((blocks, bs), F32), pltpu.SemaphoreType.DMA],
    )(sums, inner_inverse, *points, in_hbm(factor))
    far = shifted(rounded, "space", 2)
    near = shifted(rounded, "space", 1)
    back_far, back_near, back_own, curve = call(
        functools.partial(hessian_kernel, rows),
        [smem] + [vmem] * 4,
        [packed, packed, field, ((rows, bs), F32)],
        [
            vmem((3 * blocks, count, bs), BF16),
            vmem((3 * blocks, bs), F32),
            vmem((blocks, tall, bs), BF16),
            vmem((3 * blocks, rows, bs), F32),
            vmem((blocks, bs), F32),
        ],
    )(cond_ids.T, factor, near, far, rounded)
    from_far = shifted(back_far, "space", -2)
    from_near = shifted(back_near, "space", -1)
    hess, partial, msg = call(functools.partial(combine_kernel, rows), [vmem] * 8, [field, sum_shape, sum_msg])(
        back_own, from_far, from_near, curve, direction, *points
    )
    hess_sums = total(partial, msg, "space")
    whole = ((count + 1, blocks * bs), F32)
    return call(functools.partial(finish_kernel, rows), [vmem] * 9, [whole] * 3, keep=False)(
        *map(in_vmem, (sums, product, hess_sums, inner_inverse, direction, hess, *points))
    )


def solution(mesh):
    return jax.shard_map(
        body,
        mesh=mesh,
        in_specs=(
            P(("groups", "space")),
            P(("groups", "space")),
            P(None, ("groups", "space")),
            P(("groups", "space")),
            P(("groups", "space"), None, None, None),
            P(("groups", "space"), None),
            P(("groups", "space"), None),
            P("groups", None),
        ),
        out_specs=(
            P(None, ("groups", "space")),
            P(None, ("groups", "space")),
            P(None, ("groups", "space")),
        ),
        check_vma=False,
    )
```

```python
import functools

import jax
import jax.numpy as jnp
from jax import lax
from jax.experimental import pallas as pl
from jax.experimental.pallas import tpu as pltpu
from jax.sharding import PartitionSpec as P

F32, BF16 = jnp.float32, jnp.bfloat16
PAIR = 2
MAP_PARTS = 4


def shifted(block, axis, distance, parity):
    devices = range(lax.axis_size(axis))
    route = [(i - distance, i) for i in devices if i % 2 == parity and i - distance in devices]
    return lax.ppermute(block, axis, route)


def swapped(block, axis):
    return lax.ppermute(block, axis, [(i, i ^ 1) for i in range(lax.axis_size(axis))])


def is_even(axis):
    return lax.rem(lax.axis_index(axis), 2) == 0


def write_message(msg_ref, x):
    top = x.shape[0] - 8
    tail = x[top:]
    high = tail.astype(BF16).astype(F32)
    middle = (tail - high).astype(BF16).astype(F32)
    low = tail - high - middle
    first = lax.broadcasted_iota(jnp.int32, tail.shape, 0) < 4
    msg_ref[:top] = x[:top].astype(BF16)
    msg_ref[top:] = jnp.concatenate([high, jnp.where(first, middle, pltpu.roll(low, 4, 0))], axis=0).astype(BF16)


def read_message(msg_ref):
    x = msg_ref[...].astype(F32)
    rest = x[-8:]
    first = lax.broadcasted_iota(jnp.int32, rest.shape, 0) < 4
    return jnp.concatenate([x[:-16], x[-16:-8] + jnp.where(first, rest + pltpu.roll(rest, 4, 0), 0.0)], axis=0)


def add_kernel(count, held, x_ref, *refs):
    in_refs, (out_ref, *msg_refs) = refs[: count - 1], refs[count - 1 + held :]
    x = x_ref[...]
    for ref in in_refs:
        x = x + read_message(ref)
    out_ref[...] = x
    for ref in msg_refs:
        write_message(ref, x)


def total(x, msg, axis, held=()):
    n = lax.axis_size(axis)
    if n & (n - 1):
        return lax.psum(x, axis)
    step = 1
    while step < n:
        partners = [m * step for m in range(1, 4) if m * step < n]
        got = [lax.ppermute(msg, axis, [(i, i ^ d) for i in range(n)]) for d in partners]
        step *= 4
        add = functools.partial(add_kernel, len(got) + 1, len(held))
        ins = [pltpu.VMEM] * (len(got) + 1) + [pl.ANY] * len(held)
        if step < n:
            x, msg = call(add, ins, [(x.shape, F32), (msg.shape, BF16)])(x, *got, *held)
        else:
            x = call(add, ins, [(x.shape, F32)])(x, *got, *held)
        held = ()
    return x


def eye(rows, lanes):
    return lax.broadcasted_iota(jnp.int32, (rows, lanes), 0) == lax.broadcasted_iota(jnp.int32, (rows, lanes), 1)


def as_row(column, lanes):
    return jnp.sum(jnp.where(eye(column.shape[0], lanes), column, 0.0), axis=0, keepdims=True)


def as_column(row, rows):
    return jnp.sum(jnp.where(eye(rows, row.shape[1]), row, 0.0), axis=1, keepdims=True)


def right_side_of(probes_ref, gradient_ref, b, bs, rows):
    count = probes_ref.shape[0]
    return jnp.concatenate(
        [probes_ref[:, b * bs : (b + 1) * bs], jnp.broadcast_to(gradient_ref[b : b + 1], (rows - count, bs))], axis=0
    )


def project_kernel(
    rows, latent_hbm, responses_hbm, prior_hbm, probes_hbm, map_hbm, inner_hbm, out_ref, msg_ref, terms_ref, probes_ref,
    map_ref, inner_ref, latent_ref, responses_ref, prior_ref, sems,
):
    blocks, bs = latent_ref.shape
    count = probes_ref.shape[0]
    points = map_ref.shape[0]
    part = points // MAP_PARTS
    cut = lambda ref, i: ref.at[i * part : (i + 1) * part]
    pairs = [(latent_hbm, latent_ref), (responses_hbm, responses_ref), (prior_hbm, prior_ref), (probes_hbm, probes_ref)]
    pairs += [(cut(map_hbm, i), cut(map_ref, i)) for i in range(MAP_PARTS)] + [(inner_hbm, inner_ref)]
    copies = [pltpu.make_async_copy(a, b, sems.at[i]) for i, (a, b) in enumerate(pairs)]
    for copy in copies:
        copy.start()
    for copy in copies[:3]:
        copy.wait()
    probability = 1.0 / (1.0 + jnp.exp(-latent_ref[...]))
    weights = probability * (1.0 - probability)
    gradient_ref, weights_ref, inv_diag_ref = terms_ref.at[0], terms_ref.at[1], terms_ref.at[2]
    gradient_ref[...] = responses_ref[...].astype(F32) - probability
    weights_ref[...] = weights
    inv_diag_ref[...] = 1.0 / (weights + prior_ref[...])
    copies[3].wait()
    energy = jnp.zeros((rows, bs), F32)
    summed = jnp.zeros((rows, map_ref.shape[1]), F32)
    for b in range(0, blocks, PAIR):
        if b * bs % part == 0:
            copies[4 + b * bs // part].wait()
        parts = []
        for c in range(b, b + PAIR):
            field = right_side_of(probes_ref, gradient_ref, c, bs, rows)
            scaled = field * inv_diag_ref[c : c + 1]
            energy += field * scaled
            parts.append(scaled.astype(BF16))
        summed += jnp.dot(
            jnp.concatenate(parts, axis=1), map_ref[b * bs : (b + PAIR) * bs], preferred_element_type=F32
        )
    out_ref[...] = summed
    out_ref[count + 1 : count + 2] = as_row(jnp.sum(energy, axis=1, keepdims=True), map_ref.shape[1])
    write_message(msg_ref, out_ref[...])
    copies[-1].wait()


def direction_kernel(
    rows, sums_ref, inner_ref, terms_ref, probes_ref, map_ref, dir_ref, msg_ref, product_ref, grad_ref
):
    _, blocks, bs = terms_ref.shape
    count = probes_ref.shape[0]
    gradient_ref, inv_diag_ref = terms_ref.at[0], terms_ref.at[2]
    product = jnp.dot(sums_ref[...], inner_ref[...], precision=lax.Precision.HIGHEST)
    product_ref[...] = product
    coeffs = product.astype(BF16)
    for b in range(0, blocks, PAIR):
        correction = lax.dot_general(
            coeffs, map_ref[b * bs : (b + PAIR) * bs], (((1,), (1,)), ((), ())), preferred_element_type=F32
        )
        for c in range(b, b + PAIR):
            field = right_side_of(probes_ref, gradient_ref, c, bs, rows)
            direction = (field + correction[:, (c - b) * bs : (c - b + 1) * bs]) * inv_diag_ref[c : c + 1]
            dir_ref[c] = direction
            msg_ref[c] = direction[:count].astype(BF16)
            grad_ref[c : c + 1] = direction[count : count + 1]
    msg_ref[blocks] = grad_ref[...].astype(BF16)


def load_kernel(factor_hbm, after_ref, factor_ref, sem):
    copy = pltpu.make_async_copy(factor_hbm, factor_ref, sem)
    copy.start()
    copy.wait()


def tall_block(refs, grads, at, tall):
    probe_rows = refs[at]
    last = jnp.broadcast_to(grads[pl.ds(at, 1), :], (tall - probe_rows.shape[0], probe_rows.shape[1]))
    return jnp.concatenate([probe_rows, last.astype(BF16)], axis=0)


def own_image_kernel(tall, own_ref, factor_ref, image_ref, again_ref, grad_ref):
    blocks = factor_ref.shape[0]
    again_ref[...] = own_ref[...]
    grad_ref[...] = own_ref[blocks].astype(F32)
    for b in range(blocks):
        image_ref[b] = lax.dot_general(
            tall_block(own_ref, grad_ref, b, tall),
            factor_ref[b, 0],
            (((1,), (1,)), ((), ())),
            preferred_element_type=F32,
        )


def pass_on_kernel(own_ref, far_ref, out_ref):
    @pl.when(is_even("space"))
    def _():
        out_ref[...] = own_ref[...]

    @pl.when(jnp.logical_not(is_even("space")))
    def _():
        out_ref[...] = far_ref[...]


def join_kernel(back_far_ref, got_ref, out_ref):
    out_ref[...] = (back_far_ref[...].astype(F32) + got_ref[...].astype(F32)).astype(BF16)


def own_back_kernel(rows, image_ref, factor_ref, out_ref):
    for b in range(factor_ref.shape[0]):
        out_ref[b] = jnp.dot(image_ref[b], factor_ref[b, 0], preferred_element_type=F32)[:rows]


def hessian_kernel(
    rows, ids_ref, factor_ref, own_image_ref, near_ref, far_even_ref, far_odd_ref, own_ref, back_far_ref, back_near_ref,
    back_own_ref, curve_ref, image_ref, around_ref, around_grad_ref, total_ref, grad_ref,
):
    blocks, taps, bs, _ = factor_ref.shape
    count = around_ref.shape[1]
    tall = image_ref.shape[1]
    for i, refs in enumerate(((far_even_ref, far_odd_ref), (near_ref,), (own_ref,))):
        at = slice(i * blocks, (i + 1) * blocks)
        around_ref[at] = functools.reduce(jnp.add, [ref[:blocks] for ref in refs])
        around_grad_ref[at] = functools.reduce(jnp.add, [ref[blocks].astype(F32) for ref in refs])
    first = (lax.axis_index("space") - 2) * blocks
    total_ref[...] = jnp.zeros_like(total_ref)
    curve = jnp.zeros((rows, bs), F32)
    ids = lambda b, k: ids_ref[k - 1, b] - first
    side_by_side = lambda b: jnp.concatenate([factor_ref[b, k] for k in range(1, taps)], axis=1)
    for b in range(blocks):
        chosen = [tall_block(around_ref, around_grad_ref, ids(b, k), tall) for k in range(1, taps)]
        image = own_image_ref[b] + lax.dot_general(
            jnp.concatenate(chosen, axis=1), side_by_side(b), (((1,), (1,)), ((), ())), preferred_element_type=F32
        )
        rounded = image.astype(BF16)
        image_ref[b] = rounded
        curve += (image * rounded.astype(F32))[:rows]
    curve_ref[...] = curve
    for b in range(blocks):
        back = jnp.dot(image_ref[b], side_by_side(b), preferred_element_type=F32)
        for k in range(1, taps):
            total_ref[ids(b, k)] += back[:rows, (k - 1) * bs : k * bs]
    for i, ref in enumerate((back_far_ref, back_near_ref)):
        for b in range(blocks):
            ref[b] = total_ref[i * blocks + b, :count].astype(BF16)
            grad_ref[b : b + 1] = total_ref[i * blocks + b, count : count + 1]
        ref[blocks] = grad_ref[...].astype(BF16)
    back_own_ref[...] = total_ref[2 * blocks :]


def combine_kernel(
    rows, own_ref, own_back_ref, even_ref, odd_ref, mate_ref, curve_ref, dir_ref, terms_ref, probes_ref, map_ref,
    hess_ref, out_ref, msg_ref,
):
    _, blocks, bs = terms_ref.shape
    count = probes_ref.shape[0]
    lanes = map_ref.shape[1]
    gradient_ref, weights_ref, inv_diag_ref = terms_ref.at[0], terms_ref.at[1], terms_ref.at[2]
    own_part = jnp.where(is_even("space"), 1.0, 0.0)
    arrived = lambda c: even_ref[c].astype(F32) + odd_ref[c].astype(F32) + own_part * mate_ref[c].astype(F32)
    from_grad = arrived(blocks)
    curve = curve_ref[...]
    cross = jnp.zeros((rows, bs), F32)
    square = jnp.zeros((rows, bs), F32)
    summed = jnp.zeros((rows, lanes), F32)
    for b in range(0, blocks, PAIR):
        parts = []
        for c in range(b, b + PAIR):
            came = jnp.concatenate(
                [
                    arrived(c),
                    jnp.broadcast_to(from_grad[c : c + 1], (rows - count, bs)),
                ],
                axis=0,
            )
            direction = dir_ref[c]
            weighted = weights_ref[c : c + 1] * direction
            hess = own_ref[c] + own_back_ref[c] + came + weighted
            hess_ref[c] = hess
            scaled = hess * inv_diag_ref[c : c + 1]
            curve += weighted * direction
            cross += right_side_of(probes_ref, gradient_ref, c, bs, rows) * scaled
            square += hess * scaled
            parts.append(scaled.astype(BF16))
        summed += jnp.dot(
            jnp.concatenate(parts, axis=1), map_ref[b * bs : (b + PAIR) * bs], preferred_element_type=F32
        )
    out_ref[...] = summed
    for i, acc in enumerate((curve, cross, square)):
        out_ref[count + 1 + i : count + 2 + i] = as_row(jnp.sum(acc, axis=1, keepdims=True), lanes)
    write_message(msg_ref, out_ref[...])


def finish_kernel(
    rows, sums_ref, product_ref, hess_sums_ref, inner_ref, dir_ref, hess_ref, terms_ref, probes_ref, map_ref,
    solution_ref, residual_ref, next_ref,
):
    _, blocks, bs = terms_ref.shape
    count = probes_ref.shape[0]
    gradient_ref, inv_diag_ref = terms_ref.at[0], terms_ref.at[2]
    sums, product, hess_sums = sums_ref[...], product_ref[...], hess_sums_ref[...]
    column = lambda x, i: as_column(x[count + 1 + i : count + 2 + i], rows)
    coeffs = product.astype(BF16)
    plain = column(sums, 0)
    energy = plain + jnp.sum(coeffs.astype(F32) * sums, axis=1, keepdims=True)
    step = energy / column(hess_sums, 0)
    left = sums - step * hess_sums
    hess_product = jnp.dot(hess_sums, inner_ref[...], precision=lax.Precision.HIGHEST)
    coeffs = (product - step * hess_product).astype(BF16)
    plain_next = plain - 2.0 * step * column(hess_sums, 1) + step * step * column(hess_sums, 2)
    energy_next = plain_next + jnp.sum(coeffs.astype(F32) * left, axis=1, keepdims=True)
    ratio = energy_next / energy
    for b in range(0, blocks, PAIR):
        correction = lax.dot_general(
            coeffs, map_ref[b * bs : (b + PAIR) * bs], (((1,), (1,)), ((), ())), preferred_element_type=F32
        )
        for c in range(b, b + PAIR):
            at = slice(c * bs, (c + 1) * bs)
            direction = dir_ref[c]
            residual = right_side_of(probes_ref, gradient_ref, c, bs, rows) - step * hess_ref[c]
            smoothed = (residual + correction[:, (c - b) * bs : (c - b + 1) * bs]) * inv_diag_ref[c : c + 1]
            for ref, value in (
                (solution_ref, step * direction),
                (residual_ref, residual),
                (next_ref, smoothed + ratio * direction),
            ):
                ref[0:1, at] = value[count : count + 1]
                ref[1 : count + 1, at] = value[:count]


def call(kernel, ins, outs, scratch=(), limit=16, keep=True):
    spec = lambda space: pl.BlockSpec(memory_space=space)
    shapes = tuple((pltpu.VMEM if keep else jax.ShapeDtypeStruct)(s, t) for s, t in outs)
    specs = (spec(pltpu.VMEM),) * len(shapes)
    return pl.pallas_call(
        kernel,
        out_shape=shapes if len(shapes) > 1 else shapes[0],
        in_specs=[spec(space) for space in ins],
        out_specs=specs if len(shapes) > 1 else specs[0],
        scratch_shapes=scratch,
        compiler_params=pltpu.CompilerParams(vmem_limit_bytes=limit * 1024 * 1024),
    )


def in_hbm(x):
    return pltpu.with_memory_space_constraint(x, pltpu.HBM)


def in_vmem(x):
    return pltpu.with_memory_space_constraint(x, pltpu.VMEM)


def body(latent, responses, probes, prior_diag, factor, cond_ids, inducing_map, inner_inverse):
    blocks, _, bs, _ = factor.shape
    count = probes.shape[0]
    rows, tall = count + 8, count + 16
    by_block = lambda x: x.reshape(blocks, bs)
    sum_shape = ((rows, inducing_map.shape[1]), F32)
    sum_msg = ((tall, inducing_map.shape[1]), BF16)
    field = ((blocks, rows, bs), F32)
    packed = ((blocks + 1, count, bs), BF16)
    vmem, smem = pltpu.VMEM, pltpu.SMEM
    partial, msg, terms, probes, inducing_map, inner_inverse = call(
        functools.partial(project_kernel, rows),
        [pl.ANY] * 6,
        [
            sum_shape,
            sum_msg,
            ((3, blocks, bs), F32),
            (probes.shape, F32),
            (inducing_map.shape, BF16),
            (inner_inverse.shape, F32),
        ],
        [
            vmem((blocks, bs), F32),
            vmem((blocks, bs), jnp.int32),
            vmem((blocks, bs), F32),
            pltpu.SemaphoreType.DMA((5 + MAP_PARTS,)),
        ],
    )(*map(in_hbm, (by_block(latent), by_block(responses), by_block(prior_diag), probes, inducing_map, inner_inverse)))
    points = (terms, probes, inducing_map)
    factor = call(load_kernel, [pl.ANY] * 2, [(factor.shape, BF16)], [pltpu.SemaphoreType.DMA])(in_hbm(factor), msg)
    sums = total(partial, msg, "space", (factor,))
    direction, rounded, product = call(
        functools.partial(direction_kernel, rows), [vmem] * 5, [field, packed, sum_shape], [vmem((blocks, bs), F32)]
    )(sums, inner_inverse, *points)
    far_odd = shifted(rounded, "space", 2, 1)
    own_image, again = call(
        functools.partial(own_image_kernel, tall), [vmem] * 2, [((blocks, tall, bs), F32), packed], [vmem((blocks, bs), F32)]
    )(rounded, factor)
    far_even = shifted(again, "space", 2, 0)
    near = swapped(call(pass_on_kernel, [vmem] * 2, [packed])(rounded, far_odd), "space")
    back_far, back_near, back_own, curve, image = call(
        functools.partial(hessian_kernel, rows),
        [smem] + [vmem] * 6,
        [packed, packed, field, ((rows, bs), F32), ((blocks, tall, bs), BF16)],
        [
            vmem((3 * blocks, count, bs), BF16),
            vmem((3 * blocks, bs), F32),
            vmem((3 * blocks, rows, bs), F32),
            vmem((blocks, bs), F32),
        ],
    )(cond_ids.T, factor, own_image, near, far_even, far_odd, rounded)
    mate = swapped(back_near, "space")
    from_even = shifted(back_far, "space", -2, 0)
    from_odd = shifted(call(join_kernel, [vmem] * 2, [packed])(back_far, mate), "space", -2, 1)
    own_back = call(functools.partial(own_back_kernel, rows), [vmem] * 2, [field])(image, factor)
    hess, partial, msg = call(functools.partial(combine_kernel, rows), [vmem] * 10, [field, sum_shape, sum_msg])(
        back_own, own_back, from_even, from_odd, mate, curve, direction, *points
    )
    hess_sums = total(partial, msg, "space")
    whole = ((count + 1, blocks * bs), F32)
    return call(functools.partial(finish_kernel, rows), [vmem] * 9, [whole] * 3, keep=False)(
        *map(in_vmem, (sums, product, hess_sums, inner_inverse, direction, hess, *points))
    )


def solution(mesh):
    return jax.shard_map(
        body,
        mesh=mesh,
        in_specs=(
            P(("groups", "space")),
            P(("groups", "space")),
            P(None, ("groups", "space")),
            P(("groups", "space")),
            P(("groups", "space"), None, None, None),
            P(("groups", "space"), None),
            P(("groups", "space"), None),
            P("groups", None),
        ),
        out_specs=(
            P(None, ("groups", "space")),
            P(None, ("groups", "space")),
            P(None, ("groups", "space")),
        ),
        check_vma=False,
    )
```

```python
import functools

import jax
import jax.numpy as jnp
from jax import lax
from jax.experimental import pallas as pl
from jax.experimental.pallas import tpu as pltpu
from jax.sharding import PartitionSpec as P

F32, BF16 = jnp.float32, jnp.bfloat16
PAIR = 2
MAP_PARTS = 4
OUT_PARTS = 4


def shifted(block, axis, distance, parity):
    devices = range(lax.axis_size(axis))
    route = [(i - distance, i) for i in devices if i % 2 == parity and i - distance in devices]
    return lax.ppermute(block, axis, route)


def swapped(block, axis):
    return lax.ppermute(block, axis, [(i, i ^ 1) for i in range(lax.axis_size(axis))])


def is_even(axis):
    return lax.rem(lax.axis_index(axis), 2) == 0


def write_message(msg_ref, x):
    top, half = x.shape[0] - 8, x.shape[1] // 2
    value, beside = x[top:, :half], x[top:, half:]
    high = value.astype(BF16).astype(F32)
    middle = (value - high).astype(BF16).astype(F32)
    low = value - high - middle
    row = lax.broadcasted_iota(jnp.int32, value.shape, 0)
    left = jnp.where(row < 4, high, pltpu.roll(low, 3, 0))
    right = jnp.where(row < 1, beside, middle)
    msg_ref[...] = jnp.concatenate([x[:top], jnp.concatenate([left, right], axis=1)], axis=0).astype(BF16)


def read_message(msg_ref):
    x = msg_ref[...].astype(F32)
    top, half = x.shape[0] - 8, x.shape[1] // 2
    left, right = x[top:, :half], x[top:, half:]
    row = lax.broadcasted_iota(jnp.int32, left.shape, 0)
    left = jnp.where(row < 1, left, left + right + pltpu.roll(left, 5, 0))
    return jnp.concatenate([x[:top], jnp.concatenate([left, right], axis=1)], axis=0)


def add_kernel(count, held, x_ref, *refs):
    in_refs, (out_ref, *msg_refs) = refs[: count - 1], refs[count - 1 + held :]
    x = x_ref[...]
    for ref in in_refs:
        x = x + read_message(ref)
    out_ref[...] = x
    for ref in msg_refs:
        write_message(ref, x)


def total(x, msg, axis, beside=()):
    n = lax.axis_size(axis)
    made = ()
    if n & (n - 1):
        for work in beside:
            made = work(msg, *made)
        return lax.psum(x, axis), made
    step = 1
    while step < n:
        partners = [m * step for m in range(1, 4) if m * step < n]
        got = [lax.ppermute(msg, axis, [(i, i ^ d) for i in range(n)]) for d in partners]
        step *= 4
        last = step >= n
        held = ()
        while beside and (last or not held):
            work, *beside = beside
            made = held = work(msg, *made)
        add = functools.partial(add_kernel, len(got) + 1, len(held))
        ins = [pltpu.VMEM] * (len(got) + 1) + [pl.ANY] * len(held)
        outs = [(x.shape, F32)] + [(msg.shape, BF16)] * (not last)
        x, *rest = jax.tree.leaves(call(add, ins, outs)(x, *got, *held))
        msg = rest[0] if rest else None
    return x, made


def eye(rows, lanes):
    return lax.broadcasted_iota(jnp.int32, (rows, lanes), 0) == lax.broadcasted_iota(jnp.int32, (rows, lanes), 1)


def as_row(column, lanes):
    return jnp.sum(jnp.where(eye(column.shape[0], lanes), column, 0.0), axis=0, keepdims=True)


def as_column(row, rows):
    return jnp.sum(jnp.where(eye(rows, row.shape[1]), row, 0.0), axis=1, keepdims=True)


def project_kernel(
    latent_hbm, responses_hbm, prior_hbm, probes_hbm, map_hbm, out_ref, msg_ref, terms_ref, field_ref, map_ref, latent_ref,
    responses_ref, prior_ref, probes_ref, sems,
):
    blocks, bs = latent_ref.shape
    rows = out_ref.shape[0]
    count = probes_ref.shape[0]
    part = map_ref.shape[0] // MAP_PARTS
    cut = lambda ref, i: ref.at[i * part : (i + 1) * part]
    pairs = [(latent_hbm, latent_ref), (responses_hbm, responses_ref), (prior_hbm, prior_ref), (probes_hbm, probes_ref)]
    pairs += [(cut(map_hbm, i), cut(map_ref, i)) for i in range(MAP_PARTS)]
    copies = [pltpu.make_async_copy(a, b, sems.at[i]) for i, (a, b) in enumerate(pairs)]
    for copy in copies:
        copy.start()
    for copy in copies[:3]:
        copy.wait()
    probability = 1.0 / (1.0 + jnp.exp(-latent_ref[...]))
    weights = probability * (1.0 - probability)
    gradient = responses_ref[...].astype(F32) - probability
    inv_diag = 1.0 / (weights + prior_ref[...])
    terms_ref[0] = weights
    terms_ref[1] = inv_diag
    copies[3].wait()
    energy = jnp.zeros((rows, bs), F32)
    scaled = []
    for b in range(blocks):
        at = slice(b * bs, (b + 1) * bs)
        last = jnp.broadcast_to(gradient[b : b + 1], (rows - count, bs))
        field = pltpu.roll(jnp.concatenate([probes_ref[:, at], last], axis=0), 1, 0)
        field_ref[b] = field
        scaled.append(field * inv_diag[b : b + 1])
        energy += field * scaled[-1]
    summed = jnp.zeros(out_ref.shape, F32)
    for b in range(0, blocks, PAIR):
        if b * bs % part == 0:
            copies[4 + b * bs // part].wait()
        both = jnp.concatenate([scaled[b + i].astype(BF16) for i in range(PAIR)], axis=1)
        summed += jnp.dot(both, map_ref[b * bs : (b + PAIR) * bs], preferred_element_type=F32)
    out_ref[...] = summed
    out_ref[count + 1 : count + 2] = as_row(jnp.sum(energy, axis=1, keepdims=True), out_ref.shape[1])
    write_message(msg_ref, out_ref[...])


def direction_kernel(sums_ref, inner_ref, terms_ref, field_ref, map_ref, dir_ref, msg_ref, product_ref, last_ref):
    blocks, _, bs = field_ref.shape
    count = msg_ref.shape[1]
    inv_diag_ref = terms_ref.at[1]
    product = jnp.dot(sums_ref[...], inner_ref[...], precision=lax.Precision.HIGH)
    product_ref[...] = product
    coeffs = product.astype(BF16)
    for b in range(0, blocks, PAIR):
        correction = lax.dot_general(
            coeffs, map_ref[b * bs : (b + PAIR) * bs], (((1,), (1,)), ((), ())), preferred_element_type=F32
        )
        for c in range(b, b + PAIR):
            direction = (field_ref[c] + correction[:, (c - b) * bs : (c - b + 1) * bs]) * inv_diag_ref[c : c + 1]
            dir_ref[c] = direction
            msg_ref[c] = direction[:count].astype(BF16)
            last_ref[c : c + 1] = direction[count : count + 1]
    msg_ref[blocks] = last_ref[...].astype(BF16)


def load_kernel(factor_hbm, inner_hbm, after_ref, factor_ref, inner_ref, sems):
    copies = [
        pltpu.make_async_copy(factor_hbm, factor_ref, sems.at[0]),
        pltpu.make_async_copy(inner_hbm, inner_ref, sems.at[1]),
    ]
    for copy in copies:
        copy.start()
    for copy in copies:
        copy.wait()


def turn_kernel(factor_ref, after_ref, turned_ref):
    blocks, taps, bs, _ = factor_ref.shape
    for b in range(blocks):
        for k in range(taps):
            turned_ref[b, k * bs : (k + 1) * bs] = factor_ref[b, k].T


def tall_block(refs, lasts, at, tall):
    most = refs[at]
    last = jnp.broadcast_to(lasts[pl.ds(at, 1), :], (tall - most.shape[0], most.shape[1]))
    return jnp.concatenate([most, last.astype(BF16)], axis=0)


def own_image_kernel(tall, own_ref, turned_ref, image_ref, again_ref, zeros_ref, last_ref):
    blocks, bs = last_ref.shape
    again_ref[...] = own_ref[...]
    zeros_ref[...] = jnp.zeros_like(zeros_ref)
    last_ref[...] = own_ref[blocks].astype(F32)
    for b in range(blocks):
        image_ref[b] = jnp.dot(tall_block(own_ref, last_ref, b, tall), turned_ref[b, :bs], preferred_element_type=F32)


def pass_on_kernel(own_ref, far_ref, out_ref):
    @pl.when(is_even("space"))
    def _():
        out_ref[...] = own_ref[...]

    @pl.when(jnp.logical_not(is_even("space")))
    def _():
        out_ref[...] = far_ref[...]


def join_kernel(back_far_ref, got_ref, out_ref):
    out_ref[...] = (back_far_ref[...].astype(F32) + got_ref[...].astype(F32)).astype(BF16)


def own_back_kernel(rows, image_ref, factor_ref, out_ref):
    for b in range(factor_ref.shape[0]):
        out_ref[b] = jnp.dot(image_ref[b], factor_ref[b, 0], preferred_element_type=F32)[:rows]


def hessian_kernel(
    rows, ids_ref, factor_ref, turned_ref, own_image_ref, near_ref, far_even_ref, far_odd_ref, own_ref, zeros_ref,
    back_far_ref, back_near_ref, total_ref, curve_ref, image_ref, around_ref, around_last_ref, last_ref,
):
    blocks, taps, bs, _ = factor_ref.shape
    count = around_ref.shape[1]
    tall = image_ref.shape[1]
    for i, refs in enumerate(((far_even_ref, far_odd_ref), (near_ref,), (own_ref,))):
        at = slice(i * blocks, (i + 1) * blocks)
        around_ref[at] = functools.reduce(jnp.add, [ref[:blocks] for ref in refs])
        around_last_ref[at] = functools.reduce(jnp.add, [ref[blocks].astype(F32) for ref in refs])
    first = (lax.axis_index("space") - 2) * blocks
    curve = jnp.zeros((rows, bs), F32)
    ids = lambda b, k: ids_ref[k - 1, b] - first
    side_by_side = lambda b: jnp.concatenate([factor_ref[b, k] for k in range(1, taps)], axis=1)
    for b in range(blocks):
        chosen = [tall_block(around_ref, around_last_ref, ids(b, k), tall) for k in range(1, taps)]
        image = own_image_ref[b] + jnp.dot(
            jnp.concatenate(chosen, axis=1), turned_ref[b, bs:], preferred_element_type=F32
        )
        rounded = image.astype(BF16)
        image_ref[b] = rounded
        curve += (image * rounded.astype(F32))[:rows]
    curve_ref[...] = curve
    for b in range(blocks):
        back = jnp.dot(image_ref[b], side_by_side(b), preferred_element_type=F32)
        for k in range(1, taps):
            total_ref[ids(b, k)] += back[:rows, (k - 1) * bs : k * bs]
    for i, ref in enumerate((back_far_ref, back_near_ref)):
        for b in range(blocks):
            ref[b] = total_ref[i * blocks + b, :count].astype(BF16)
            last_ref[b : b + 1] = total_ref[i * blocks + b, count : count + 1]
        ref[blocks] = last_ref[...].astype(BF16)


def combine_kernel(
    own_ref, own_back_ref, even_ref, odd_ref, mate_ref, curve_ref, dir_ref, terms_ref, field_ref, map_ref, hess_ref,
    out_ref, msg_ref,
):
    blocks, rows, bs = field_ref.shape
    count = mate_ref.shape[1]
    weights_ref, inv_diag_ref = terms_ref.at[0], terms_ref.at[1]
    own_part = jnp.where(is_even("space"), 1.0, 0.0)
    arrived = lambda c: even_ref[c].astype(F32) + odd_ref[c].astype(F32) + own_part * mate_ref[c].astype(F32)
    from_last = arrived(blocks)
    curve = curve_ref[...]
    cross = jnp.zeros((rows, bs), F32)
    square = jnp.zeros((rows, bs), F32)
    summed = jnp.zeros(out_ref.shape, F32)
    for b in range(0, blocks, PAIR):
        parts = []
        for c in range(b, b + PAIR):
            last = jnp.broadcast_to(from_last[c : c + 1], (rows - count, bs))
            direction = dir_ref[c]
            weighted = weights_ref[c : c + 1] * direction
            hess = own_ref[2 * blocks + c] + own_back_ref[c] + jnp.concatenate([arrived(c), last], axis=0) + weighted
            hess_ref[c] = hess
            scaled = hess * inv_diag_ref[c : c + 1]
            curve += weighted * direction
            cross += field_ref[c] * scaled
            square += hess * scaled
            parts.append(scaled.astype(BF16))
        summed += jnp.dot(
            jnp.concatenate(parts, axis=1), map_ref[b * bs : (b + PAIR) * bs], preferred_element_type=F32
        )
    out_ref[...] = summed
    for i, acc in enumerate((curve, cross, square)):
        out_ref[count + 1 + i : count + 2 + i] = as_row(jnp.sum(acc, axis=1, keepdims=True), out_ref.shape[1])
    write_message(msg_ref, out_ref[...])


def finish_kernel(
    sums_ref, product_ref, hess_sums_ref, inner_ref, dir_ref, hess_ref, terms_ref, field_ref, map_ref, solution_hbm,
    residual_hbm, next_hbm, solution_ref, residual_ref, next_ref, sems,
):
    blocks, rows, bs = field_ref.shape
    whole = solution_ref.shape[0]
    inv_diag_ref = terms_ref.at[1]
    sums, product, hess_sums = sums_ref[...], product_ref[...], hess_sums_ref[...]
    column = lambda x, i: as_column(x[whole + i : whole + i + 1], rows)
    coeffs = product.astype(BF16)
    plain = column(sums, 0)
    energy = plain + jnp.sum(coeffs.astype(F32) * sums, axis=1, keepdims=True)
    step = energy / column(hess_sums, 0)
    left = sums - step * hess_sums
    hess_product = jnp.dot(hess_sums, inner_ref[...], precision=lax.Precision.HIGH)
    coeffs = (product - step * hess_product).astype(BF16)
    plain_next = plain - 2.0 * step * column(hess_sums, 1) + step * step * column(hess_sums, 2)
    energy_next = plain_next + jnp.sum(coeffs.astype(F32) * left, axis=1, keepdims=True)
    ratio = energy_next / energy
    part = blocks // OUT_PARTS
    copies = []

    def send(i, ref, hbm):
        at = pl.ds(i * part * bs, part * bs)
        copies.append(pltpu.make_async_copy(ref.at[:, at], hbm.at[:, at], sems.at[len(copies)]))
        copies[-1].start()

    residual_of = lambda c: field_ref[c] - step * hess_ref[c]
    for i in range(OUT_PARTS):
        for c in range(i * part, (i + 1) * part):
            at = slice(c * bs, (c + 1) * bs)
            solution_ref[:, at] = (step * dir_ref[c])[:whole]
            residual_ref[:, at] = residual_of(c)[:whole]
        send(i, solution_ref, solution_hbm)
        send(i, residual_ref, residual_hbm)
    for i in range(OUT_PARTS):
        for b in range(i * part, (i + 1) * part, PAIR):
            correction = lax.dot_general(
                coeffs, map_ref[b * bs : (b + PAIR) * bs], (((1,), (1,)), ((), ())), preferred_element_type=F32
            )
            for c in range(b, b + PAIR):
                smoothed = (residual_of(c) + correction[:, (c - b) * bs : (c - b + 1) * bs]) * inv_diag_ref[c : c + 1]
                next_ref[:, c * bs : (c + 1) * bs] = (smoothed + ratio * dir_ref[c])[:whole]
        send(i, next_ref, next_hbm)
    for copy in copies:
        copy.wait()


def call(kernel, ins, outs, scratch=(), limit=16, keep=True, aliases={}):
    spec = lambda space: pl.BlockSpec(memory_space=space)
    shapes = tuple((pltpu.VMEM if keep else jax.ShapeDtypeStruct)(s, t) for s, t in outs)
    specs = (spec(pltpu.VMEM if keep else pl.ANY),) * len(shapes)
    return pl.pallas_call(
        kernel,
        out_shape=shapes if len(shapes) > 1 else shapes[0],
        in_specs=[spec(space) for space in ins],
        out_specs=specs if len(shapes) > 1 else specs[0],
        scratch_shapes=scratch,
        input_output_aliases=aliases,
        compiler_params=pltpu.CompilerParams(vmem_limit_bytes=limit * 1024 * 1024),
    )


def in_hbm(x):
    return pltpu.with_memory_space_constraint(x, pltpu.HBM)


def in_vmem(x):
    return pltpu.with_memory_space_constraint(x, pltpu.VMEM)


def body(latent, responses, probes, prior_diag, factor, cond_ids, inducing_map, inner_inverse):
    blocks, _, bs, _ = factor.shape
    count = probes.shape[0]
    rows, tall = count + 8, count + 16
    by_block = lambda x: x.reshape(blocks, bs)
    sum_shape = ((rows, inducing_map.shape[1]), F32)
    sum_msg = ((rows, inducing_map.shape[1]), BF16)
    field = ((blocks, rows, bs), F32)
    packed = ((blocks + 1, count, bs), BF16)
    vmem, smem = pltpu.VMEM, pltpu.SMEM
    partial, msg, terms, right_side, inducing_map = call(
        project_kernel,
        [pl.ANY] * 5,
        [sum_shape, sum_msg, ((2, blocks, bs), F32), field, (inducing_map.shape, BF16)],
        [
            vmem((blocks, bs), F32),
            vmem((blocks, bs), jnp.int32),
            vmem((blocks, bs), F32),
            vmem(probes.shape, F32),
            pltpu.SemaphoreType.DMA((4 + MAP_PARTS,)),
        ],
    )(*map(in_hbm, (by_block(latent), by_block(responses), by_block(prior_diag), probes, inducing_map)))
    points = (terms, right_side, inducing_map)

    def load(msg):
        outs = [(factor.shape, BF16), (inner_inverse.shape, F32)]
        return call(load_kernel, [pl.ANY] * 3, outs, [pltpu.SemaphoreType.DMA((2,))])(
            in_hbm(factor), in_hbm(inner_inverse), msg
        )

    def turn(msg, loaded, inner):
        shape = (blocks, factor.shape[1] * bs, bs)
        return loaded, inner, call(turn_kernel, [vmem, pl.ANY], [(shape, BF16)])(loaded, msg)

    sums, (factor, inner_inverse, turned) = total(partial, msg, "space", [load, turn])
    direction, rounded, product = call(
        direction_kernel, [vmem] * 5, [field, packed, sum_shape], [vmem((blocks, bs), F32)]
    )(sums, inner_inverse, *points)
    far_odd = shifted(rounded, "space", 2, 1)
    around = ((3 * blocks, rows, bs), F32)
    own_image, again, zeros = call(
        functools.partial(own_image_kernel, tall),
        [vmem] * 2,
        [((blocks, tall, bs), F32), packed, around],
        [vmem((blocks, bs), F32)],
    )(rounded, turned)
    far_even = shifted(again, "space", 2, 0)
    near = swapped(call(pass_on_kernel, [vmem] * 2, [packed])(rounded, far_odd), "space")
    back_far, back_near, back_own, curve, image = call(
        functools.partial(hessian_kernel, rows),
        [smem] + [vmem] * 8,
        [packed, packed, around, ((rows, bs), F32), ((blocks, tall, bs), BF16)],
        [vmem((3 * blocks, count, bs), BF16), vmem((3 * blocks, bs), F32), vmem((blocks, bs), F32)],
        aliases={8: 2},
    )(cond_ids.T, factor, turned, own_image, near, far_even, far_odd, rounded, zeros)
    mate = swapped(back_near, "space")
    from_even = shifted(back_far, "space", -2, 0)
    from_odd = shifted(call(join_kernel, [vmem] * 2, [packed])(back_far, mate), "space", -2, 1)
    own_back = call(functools.partial(own_back_kernel, rows), [vmem] * 2, [field])(image, factor)
    hess, partial, msg = call(combine_kernel, [vmem] * 10, [field, sum_shape, sum_msg])(
        back_own, own_back, from_even, from_odd, mate, curve, direction, *points
    )
    hess_sums, _ = total(partial, msg, "space")
    whole = ((count + 1, blocks * bs), F32)
    scratch = [vmem(*whole)] * 3 + [pltpu.SemaphoreType.DMA((3 * OUT_PARTS,))]
    return call(finish_kernel, [vmem] * 9, [whole] * 3, scratch, keep=False)(
        *map(in_vmem, (sums, product, hess_sums, inner_inverse, direction, hess, *points))
    )


def solution(mesh):
    return jax.shard_map(
        body,
        mesh=mesh,
        in_specs=(
            P(("groups", "space")),
            P(("groups", "space")),
            P(None, ("groups", "space")),
            P(("groups", "space")),
            P(("groups", "space"), None, None, None),
            P(("groups", "space"), None),
            P(("groups", "space"), None),
            P("groups", None),
        ),
        out_specs=(
            P(None, ("groups", "space")),
            P(None, ("groups", "space")),
            P(None, ("groups", "space")),
        ),
        check_vma=False,
    )
```

```python
import functools

import jax
import jax.numpy as jnp
from jax import lax
from jax.experimental import pallas as pl
from jax.experimental.pallas import tpu as pltpu
from jax.sharding import PartitionSpec as P

F32, BF16 = jnp.float32, jnp.bfloat16
PAIR = 2
MAP_PARTS = 4
OUT_PARTS = 4


def shifted(block, axis, distance, parity):
    devices = range(lax.axis_size(axis))
    route = [(i - distance, i) for i in devices if i % 2 == parity and i - distance in devices]
    return lax.ppermute(block, axis, route)


def swapped(block, axis):
    return lax.ppermute(block, axis, [(i, i ^ 1) for i in range(lax.axis_size(axis))])


def is_even(axis):
    return lax.rem(lax.axis_index(axis), 2) == 0


def write_message(msg_ref, x):
    top, half = x.shape[0] - 8, x.shape[1] // 2
    value, beside = x[top:, :half], x[top:, half:]
    high = value.astype(BF16).astype(F32)
    middle = (value - high).astype(BF16).astype(F32)
    low = value - high - middle
    row = lax.broadcasted_iota(jnp.int32, value.shape, 0)
    left = jnp.where(row < 4, high, pltpu.roll(low, 3, 0))
    right = jnp.where(row < 1, beside, middle)
    msg_ref[...] = jnp.concatenate([x[:top], jnp.concatenate([left, right], axis=1)], axis=0).astype(BF16)


def read_message(msg_ref):
    x = msg_ref[...].astype(F32)
    top, half = x.shape[0] - 8, x.shape[1] // 2
    left, right = x[top:, :half], x[top:, half:]
    row = lax.broadcasted_iota(jnp.int32, left.shape, 0)
    left = jnp.where(row < 1, left, left + right + pltpu.roll(left, 5, 0))
    return jnp.concatenate([x[:top], jnp.concatenate([left, right], axis=1)], axis=0)


def add_kernel(count, held, x_ref, *refs):
    in_refs, (out_ref, *msg_refs) = refs[: count - 1], refs[count - 1 + held :]
    x = x_ref[...]
    for ref in in_refs:
        x = x + (ref[...] if ref.dtype == F32 else read_message(ref))
    out_ref[...] = x
    for ref in msg_refs:
        write_message(ref, x)


def rounds_of(n):
    rounds = [(1,)] + [(3,)] * (n > 2)
    step = 4
    while step < n:
        rounds.append(tuple((m * step) ^ 1 for m in range(1, 4) if m * step < n))
        step *= 4
    return rounds


def total(x, axis, beside=()):
    n = lax.axis_size(axis)
    made = ()
    if n & (n - 1):
        for work in beside:
            made = work(x, *made)
        return lax.psum(x, axis), made
    rounds = rounds_of(n)
    msg = x
    for i, partners in enumerate(rounds):
        got = [lax.ppermute(msg, axis, [(j, j ^ d) for j in range(n)]) for d in partners]
        last = i + 1 == len(rounds)
        held = ()
        while beside and (last or (i > 0 and not held)):
            work, *beside = beside
            made = held = work(msg, *made)
        add = functools.partial(add_kernel, len(got) + 1, len(held))
        ins = [pltpu.VMEM] * (len(got) + 1) + [pl.ANY] * len(held)
        outs = [(x.shape, F32)] + [(x.shape, BF16)] * (not last)
        x, *rest = jax.tree.leaves(call(add, ins, outs)(x, *got, *held))
        msg = rest[0] if rest else None
    return x, made


def eye(rows, lanes):
    return lax.broadcasted_iota(jnp.int32, (rows, lanes), 0) == lax.broadcasted_iota(jnp.int32, (rows, lanes), 1)


def as_row(column, lanes):
    return jnp.sum(jnp.where(eye(column.shape[0], lanes), column, 0.0), axis=0, keepdims=True)


def as_column(row, rows):
    return jnp.sum(jnp.where(eye(rows, row.shape[1]), row, 0.0), axis=1, keepdims=True)


def project_kernel(
    latent_hbm, responses_hbm, prior_hbm, probes_hbm, map_hbm, out_ref, terms_ref, field_ref, map_ref, latent_ref,
    responses_ref, prior_ref, probes_ref, sems,
):
    blocks, bs = latent_ref.shape
    rows = out_ref.shape[0]
    count = probes_ref.shape[0]
    part = map_ref.shape[0] // MAP_PARTS
    cut = lambda ref, i: ref.at[i * part : (i + 1) * part]
    pairs = [(latent_hbm, latent_ref), (responses_hbm, responses_ref), (prior_hbm, prior_ref), (probes_hbm, probes_ref)]
    pairs += [(cut(map_hbm, i), cut(map_ref, i)) for i in range(MAP_PARTS)]
    copies = [pltpu.make_async_copy(a, b, sems.at[i]) for i, (a, b) in enumerate(pairs)]
    for copy in copies:
        copy.start()
    for copy in copies[:3]:
        copy.wait()
    probability = 1.0 / (1.0 + jnp.exp(-latent_ref[...]))
    weights = probability * (1.0 - probability)
    gradient = responses_ref[...].astype(F32) - probability
    inv_diag = 1.0 / (weights + prior_ref[...])
    terms_ref[0] = weights
    terms_ref[1] = inv_diag
    copies[3].wait()
    energy = jnp.zeros((rows, bs), F32)
    scaled = []
    for b in range(blocks):
        at = slice(b * bs, (b + 1) * bs)
        last = jnp.broadcast_to(gradient[b : b + 1], (rows - count, bs))
        field = pltpu.roll(jnp.concatenate([probes_ref[:, at], last], axis=0), 1, 0)
        field_ref[b] = field
        scaled.append(field * inv_diag[b : b + 1])
        energy += field * scaled[-1]
    summed = jnp.zeros(out_ref.shape, F32)
    for b in range(0, blocks, PAIR):
        if b * bs % part == 0:
            copies[4 + b * bs // part].wait()
        both = jnp.concatenate([scaled[b + i].astype(BF16) for i in range(PAIR)], axis=1)
        summed += jnp.dot(both, map_ref[b * bs : (b + PAIR) * bs], preferred_element_type=F32)
    out_ref[...] = summed
    out_ref[count + 1 : count + 2] = as_row(jnp.sum(energy, axis=1, keepdims=True), out_ref.shape[1])


def direction_kernel(sums_ref, inner_ref, terms_ref, field_ref, map_ref, dir_ref, msg_ref, product_ref, last_ref):
    blocks, _, bs = field_ref.shape
    count = msg_ref.shape[1]
    inv_diag_ref = terms_ref.at[1]
    product = jnp.dot(sums_ref[...], inner_ref[...], precision=lax.Precision.HIGH)
    product_ref[...] = product
    coeffs = product.astype(BF16)
    for b in range(0, blocks, PAIR):
        correction = lax.dot_general(
            coeffs, map_ref[b * bs : (b + PAIR) * bs], (((1,), (1,)), ((), ())), preferred_element_type=F32
        )
        for c in range(b, b + PAIR):
            direction = (field_ref[c] + correction[:, (c - b) * bs : (c - b + 1) * bs]) * inv_diag_ref[c : c + 1]
            dir_ref[c] = direction
            msg_ref[c] = direction[:count].astype(BF16)
            last_ref[c : c + 1] = direction[count : count + 1]
    msg_ref[blocks] = last_ref[...].astype(BF16)


def load_kernel(factor_hbm, inner_hbm, after_ref, factor_ref, inner_ref, sems):
    copies = [
        pltpu.make_async_copy(factor_hbm, factor_ref, sems.at[0]),
        pltpu.make_async_copy(inner_hbm, inner_ref, sems.at[1]),
    ]
    for copy in copies:
        copy.start()
    for copy in copies:
        copy.wait()


def turn_kernel(factor_ref, after_ref, turned_ref):
    blocks, taps, bs, _ = factor_ref.shape
    for b in range(blocks):
        for k in range(taps):
            turned_ref[b, k * bs : (k + 1) * bs] = factor_ref[b, k].T


def tall_block(refs, lasts, at, tall):
    most = refs[at]
    last = jnp.broadcast_to(lasts[pl.ds(at, 1), :], (tall - most.shape[0], most.shape[1]))
    return jnp.concatenate([most, last.astype(BF16)], axis=0)


def own_image_kernel(tall, own_ref, turned_ref, image_ref, again_ref, zeros_ref, last_ref):
    blocks, bs = last_ref.shape
    again_ref[...] = own_ref[...]
    zeros_ref[...] = jnp.zeros_like(zeros_ref)
    last_ref[...] = own_ref[blocks].astype(F32)
    for b in range(blocks):
        image_ref[b] = jnp.dot(tall_block(own_ref, last_ref, b, tall), turned_ref[b, :bs], preferred_element_type=F32)


def pass_on_kernel(own_ref, far_ref, out_ref):
    @pl.when(is_even("space"))
    def _():
        out_ref[...] = own_ref[...]

    @pl.when(jnp.logical_not(is_even("space")))
    def _():
        out_ref[...] = far_ref[...]


def join_kernel(back_far_ref, got_ref, out_ref):
    out_ref[...] = (back_far_ref[...].astype(F32) + got_ref[...].astype(F32)).astype(BF16)


def own_back_kernel(rows, image_ref, factor_ref, out_ref):
    for b in range(factor_ref.shape[0]):
        out_ref[b] = jnp.dot(image_ref[b], factor_ref[b, 0], preferred_element_type=F32)[:rows]


def hessian_kernel(
    rows, ids_ref, factor_ref, turned_ref, own_image_ref, near_ref, far_even_ref, far_odd_ref, own_ref, zeros_ref,
    back_far_ref, back_near_ref, total_ref, curve_ref, image_ref, around_ref, around_last_ref, last_ref,
):
    blocks, taps, bs, _ = factor_ref.shape
    count = around_ref.shape[1]
    tall = image_ref.shape[1]
    for i, refs in enumerate(((far_even_ref, far_odd_ref), (near_ref,), (own_ref,))):
        at = slice(i * blocks, (i + 1) * blocks)
        around_ref[at] = functools.reduce(jnp.add, [ref[:blocks] for ref in refs])
        around_last_ref[at] = functools.reduce(jnp.add, [ref[blocks].astype(F32) for ref in refs])
    first = (lax.axis_index("space") - 2) * blocks
    curve = jnp.zeros((rows, bs), F32)
    ids = lambda b, k: ids_ref[k - 1, b] - first
    side_by_side = lambda b: jnp.concatenate([factor_ref[b, k] for k in range(1, taps)], axis=1)
    for b in range(blocks):
        chosen = [tall_block(around_ref, around_last_ref, ids(b, k), tall) for k in range(1, taps)]
        image = own_image_ref[b] + jnp.dot(
            jnp.concatenate(chosen, axis=1), turned_ref[b, bs:], preferred_element_type=F32
        )
        rounded = image.astype(BF16)
        image_ref[b] = rounded
        curve += (image * rounded.astype(F32))[:rows]
    curve_ref[...] = curve
    for b in range(blocks):
        back = jnp.dot(image_ref[b], side_by_side(b), preferred_element_type=F32)
        for k in range(1, taps):
            total_ref[ids(b, k)] += back[:rows, (k - 1) * bs : k * bs]
    for i, ref in enumerate((back_far_ref, back_near_ref)):
        for b in range(blocks):
            ref[b] = total_ref[i * blocks + b, :count].astype(BF16)
            last_ref[b : b + 1] = total_ref[i * blocks + b, count : count + 1]
        ref[blocks] = last_ref[...].astype(BF16)


def combine_kernel(
    own_ref, own_back_ref, even_ref, odd_ref, mate_ref, curve_ref, dir_ref, terms_ref, field_ref, map_ref, hess_ref,
    out_ref,
):
    blocks, rows, bs = field_ref.shape
    count = mate_ref.shape[1]
    weights_ref, inv_diag_ref = terms_ref.at[0], terms_ref.at[1]
    own_part = jnp.where(is_even("space"), 1.0, 0.0)
    arrived = lambda c: even_ref[c].astype(F32) + odd_ref[c].astype(F32) + own_part * mate_ref[c].astype(F32)
    from_last = arrived(blocks)
    curve = curve_ref[...]
    cross = jnp.zeros((rows, bs), F32)
    square = jnp.zeros((rows, bs), F32)
    summed = jnp.zeros(out_ref.shape, F32)
    for b in range(0, blocks, PAIR):
        parts = []
        for c in range(b, b + PAIR):
            last = jnp.broadcast_to(from_last[c : c + 1], (rows - count, bs))
            direction = dir_ref[c]
            weighted = weights_ref[c : c + 1] * direction
            hess = own_ref[2 * blocks + c] + own_back_ref[c] + jnp.concatenate([arrived(c), last], axis=0) + weighted
            hess_ref[c] = hess
            scaled = hess * inv_diag_ref[c : c + 1]
            curve += weighted * direction
            cross += field_ref[c] * scaled
            square += hess * scaled
            parts.append(scaled.astype(BF16))
        summed += jnp.dot(
            jnp.concatenate(parts, axis=1), map_ref[b * bs : (b + PAIR) * bs], preferred_element_type=F32
        )
    out_ref[...] = summed
    for i, acc in enumerate((curve, cross, square)):
        out_ref[count + 1 + i : count + 2 + i] = as_row(jnp.sum(acc, axis=1, keepdims=True), out_ref.shape[1])


def finish_kernel(
    sums_ref, product_ref, hess_sums_ref, inner_ref, dir_ref, hess_ref, terms_ref, field_ref, map_ref, solution_hbm,
    residual_hbm, next_hbm, solution_ref, residual_ref, next_ref, sems,
):
    blocks, rows, bs = field_ref.shape
    whole = solution_ref.shape[0]
    inv_diag_ref = terms_ref.at[1]
    sums, product, hess_sums = sums_ref[...], product_ref[...], hess_sums_ref[...]
    column = lambda x, i: as_column(x[whole + i : whole + i + 1], rows)
    coeffs = product.astype(BF16)
    plain = column(sums, 0)
    energy = plain + jnp.sum(coeffs.astype(F32) * sums, axis=1, keepdims=True)
    step = energy / column(hess_sums, 0)
    left = sums - step * hess_sums
    hess_product = jnp.dot(hess_sums, inner_ref[...], precision=lax.Precision.HIGH)
    coeffs = (product - step * hess_product).astype(BF16)
    plain_next = plain - 2.0 * step * column(hess_sums, 1) + step * step * column(hess_sums, 2)
    energy_next = plain_next + jnp.sum(coeffs.astype(F32) * left, axis=1, keepdims=True)
    ratio = energy_next / energy
    part = blocks // OUT_PARTS
    copies = []

    def send(i, ref, hbm):
        at = pl.ds(i * part * bs, part * bs)
        copies.append(pltpu.make_async_copy(ref.at[:, at], hbm.at[:, at], sems.at[len(copies)]))
        copies[-1].start()

    residual_of = lambda c: field_ref[c] - step * hess_ref[c]
    for i in range(OUT_PARTS):
        for c in range(i * part, (i + 1) * part):
            at = slice(c * bs, (c + 1) * bs)
            solution_ref[:, at] = (step * dir_ref[c])[:whole]
            residual_ref[:, at] = residual_of(c)[:whole]
        send(i, solution_ref, solution_hbm)
        send(i, residual_ref, residual_hbm)
    for i in range(OUT_PARTS):
        for b in range(i * part, (i + 1) * part, PAIR):
            correction = lax.dot_general(
                coeffs, map_ref[b * bs : (b + PAIR) * bs], (((1,), (1,)), ((), ())), preferred_element_type=F32
            )
            for c in range(b, b + PAIR):
                smoothed = (residual_of(c) + correction[:, (c - b) * bs : (c - b + 1) * bs]) * inv_diag_ref[c : c + 1]
                next_ref[:, c * bs : (c + 1) * bs] = (smoothed + ratio * dir_ref[c])[:whole]
        send(i, next_ref, next_hbm)
    for copy in copies:
        copy.wait()


def call(kernel, ins, outs, scratch=(), limit=16, keep=True, aliases={}):
    spec = lambda space: pl.BlockSpec(memory_space=space)
    shapes = tuple((pltpu.VMEM if keep else jax.ShapeDtypeStruct)(s, t) for s, t in outs)
    specs = (spec(pltpu.VMEM if keep else pl.ANY),) * len(shapes)
    return pl.pallas_call(
        kernel,
        out_shape=shapes if len(shapes) > 1 else shapes[0],
        in_specs=[spec(space) for space in ins],
        out_specs=specs if len(shapes) > 1 else specs[0],
        scratch_shapes=scratch,
        input_output_aliases=aliases,
        compiler_params=pltpu.CompilerParams(vmem_limit_bytes=limit * 1024 * 1024),
    )


def in_hbm(x):
    return pltpu.with_memory_space_constraint(x, pltpu.HBM)


def in_vmem(x):
    return pltpu.with_memory_space_constraint(x, pltpu.VMEM)


def body(latent, responses, probes, prior_diag, factor, cond_ids, inducing_map, inner_inverse):
    blocks, _, bs, _ = factor.shape
    count = probes.shape[0]
    rows, tall = count + 8, count + 16
    by_block = lambda x: x.reshape(blocks, bs)
    sum_shape = ((rows, inducing_map.shape[1]), F32)
    field = ((blocks, rows, bs), F32)
    packed = ((blocks + 1, count, bs), BF16)
    vmem, smem = pltpu.VMEM, pltpu.SMEM
    partial, terms, right_side, inducing_map = call(
        project_kernel,
        [pl.ANY] * 5,
        [sum_shape, ((2, blocks, bs), F32), field, (inducing_map.shape, BF16)],
        [
            vmem((blocks, bs), F32),
            vmem((blocks, bs), jnp.int32),
            vmem((blocks, bs), F32),
            vmem(probes.shape, F32),
            pltpu.SemaphoreType.DMA((4 + MAP_PARTS,)),
        ],
    )(*map(in_hbm, (by_block(latent), by_block(responses), by_block(prior_diag), probes, inducing_map)))
    points = (terms, right_side, inducing_map)

    def load(msg):
        outs = [(factor.shape, BF16), (inner_inverse.shape, F32)]
        return call(load_kernel, [pl.ANY] * 3, outs, [pltpu.SemaphoreType.DMA((2,))])(
            in_hbm(factor), in_hbm(inner_inverse), msg
        )

    def turn(msg, loaded, inner):
        shape = (blocks, factor.shape[1] * bs, bs)
        return loaded, inner, call(turn_kernel, [vmem, pl.ANY], [(shape, BF16)])(loaded, msg)

    sums, (factor, inner_inverse, turned) = total(partial, "space", [load, turn])
    direction, rounded, product = call(
        direction_kernel, [vmem] * 5, [field, packed, sum_shape], [vmem((blocks, bs), F32)]
    )(sums, inner_inverse, *points)
    far_odd = shifted(rounded, "space", 2, 1)
    around = ((3 * blocks, rows, bs), F32)
    own_image, again, zeros = call(
        functools.partial(own_image_kernel, tall),
        [vmem] * 2,
        [((blocks, tall, bs), F32), packed, around],
        [vmem((blocks, bs), F32)],
    )(rounded, turned)
    far_even = shifted(again, "space", 2, 0)
    near = swapped(call(pass_on_kernel, [vmem] * 2, [packed])(rounded, far_odd), "space")
    back_far, back_near, back_own, curve, image = call(
        functools.partial(hessian_kernel, rows),
        [smem] + [vmem] * 8,
        [packed, packed, around, ((rows, bs), F32), ((blocks, tall, bs), BF16)],
        [vmem((3 * blocks, count, bs), BF16), vmem((3 * blocks, bs), F32), vmem((blocks, bs), F32)],
        aliases={8: 2},
    )(cond_ids.T, factor, turned, own_image, near, far_even, far_odd, rounded, zeros)
    mate = swapped(back_near, "space")
    from_even = shifted(back_far, "space", -2, 0)
    from_odd = shifted(call(join_kernel, [vmem] * 2, [packed])(back_far, mate), "space", -2, 1)
    own_back = call(functools.partial(own_back_kernel, rows), [vmem] * 2, [field])(image, factor)
    hess, partial = call(combine_kernel, [vmem] * 10, [field, sum_shape])(
        back_own, own_back, from_even, from_odd, mate, curve, direction, *points
    )
    hess_sums, _ = total(partial, "space")
    whole = ((count + 1, blocks * bs), F32)
    scratch = [vmem(*whole)] * 3 + [pltpu.SemaphoreType.DMA((3 * OUT_PARTS,))]
    return call(finish_kernel, [vmem] * 9, [whole] * 3, scratch, keep=False)(
        *map(in_vmem, (sums, product, hess_sums, inner_inverse, direction, hess, *points))
    )


def solution(mesh):
    return jax.shard_map(
        body,
        mesh=mesh,
        in_specs=(
            P(("groups", "space")),
            P(("groups", "space")),
            P(None, ("groups", "space")),
            P(("groups", "space")),
            P(("groups", "space"), None, None, None),
            P(("groups", "space"), None),
            P(("groups", "space"), None),
            P("groups", None),
        ),
        out_specs=(
            P(None, ("groups", "space")),
            P(None, ("groups", "space")),
            P(None, ("groups", "space")),
        ),
        check_vma=False,
    )
```

```python
import functools

import jax
import jax.numpy as jnp
from jax import lax
from jax.experimental import pallas as pl
from jax.experimental.pallas import tpu as pltpu
from jax.sharding import PartitionSpec as P

F32, BF16 = jnp.float32, jnp.bfloat16
PAIR = 2
MAP_PARTS = 4
OUT_PARTS = 4


def sent(block, axis, distance, parities=(0, 1)):
    devices = range(lax.axis_size(axis))
    return lax.ppermute(block, axis, [(i, i + distance) for i in devices if i % 2 in parities and i + distance in devices])


def swapped(block, axis):
    return lax.ppermute(block, axis, [(i, i ^ 1) for i in range(lax.axis_size(axis))])


def is_even(axis):
    return lax.rem(lax.axis_index(axis), 2) == 0


def write_message(msg_ref, x):
    top, half = x.shape[0] - 8, x.shape[1] // 2
    value, beside = x[top:, :half], x[top:, half:]
    high = value.astype(BF16).astype(F32)
    middle = (value - high).astype(BF16).astype(F32)
    low = value - high - middle
    row = lax.broadcasted_iota(jnp.int32, value.shape, 0)
    left = jnp.where(row < 4, high, pltpu.roll(low, 3, 0))
    right = jnp.where(row < 1, beside, middle)
    msg_ref[...] = jnp.concatenate([x[:top], jnp.concatenate([left, right], axis=1)], axis=0).astype(BF16)


def read_message(msg_ref):
    x = msg_ref[...].astype(F32)
    top, half = x.shape[0] - 8, x.shape[1] // 2
    left, right = x[top:, :half], x[top:, half:]
    row = lax.broadcasted_iota(jnp.int32, left.shape, 0)
    left = jnp.where(row < 1, left, left + right + pltpu.roll(left, 5, 0))
    return jnp.concatenate([x[:top], jnp.concatenate([left, right], axis=1)], axis=0)


def add_kernel(count, held, x_ref, *refs):
    in_refs, (out_ref, *msg_refs) = refs[: count - 1], refs[count - 1 + held :]
    x = x_ref[...]
    for ref in in_refs:
        x = x + (ref[...] if ref.dtype == F32 else read_message(ref))
    out_ref[...] = x
    for ref in msg_refs:
        write_message(ref, x)


def rounds_of(n):
    rounds = [(1,)] + [(3,)] * (n > 2)
    step = 4
    while step < n:
        rounds.append(tuple((m * step) ^ 1 for m in range(1, 4) if m * step < n))
        step *= 4
    return rounds


def total(x, axis, beside=None):
    n = lax.axis_size(axis)
    if n & (n - 1):
        return lax.psum(x, axis), beside(x) if beside else ()
    rounds = rounds_of(n)
    msg = x
    for i, partners in enumerate(rounds):
        got = [lax.ppermute(msg, axis, [(j, j ^ d) for j in range(n)]) for d in partners]
        last = i + 1 == len(rounds)
        held = beside(msg) if beside and last else ()
        add = functools.partial(add_kernel, len(got) + 1, len(held))
        ins = [pltpu.VMEM] * (len(got) + 1) + [pl.ANY] * len(held)
        outs = [(x.shape, F32)] + [(x.shape, BF16)] * (not last)
        x, *rest = jax.tree.leaves(call(add, ins, outs)(x, *got, *held))
        msg = rest[0] if rest else None
    return x, held


def eye(rows, lanes):
    return lax.broadcasted_iota(jnp.int32, (rows, lanes), 0) == lax.broadcasted_iota(jnp.int32, (rows, lanes), 1)


def as_row(column, lanes):
    return jnp.sum(jnp.where(eye(column.shape[0], lanes), column, 0.0), axis=0, keepdims=True)


def as_column(row, rows):
    return jnp.sum(jnp.where(eye(rows, row.shape[1]), row, 0.0), axis=1, keepdims=True)


def project_kernel(
    latent_hbm, responses_hbm, prior_hbm, probes_hbm, map_hbm, out_ref, terms_ref, field_ref, map_ref, latent_ref,
    responses_ref, prior_ref, probes_ref, sems,
):
    blocks, bs = latent_ref.shape
    rows = out_ref.shape[0]
    count = probes_ref.shape[0]
    part = map_ref.shape[0] // MAP_PARTS
    cut = lambda ref, i: ref.at[i * part : (i + 1) * part]
    pairs = [(latent_hbm, latent_ref), (responses_hbm, responses_ref), (prior_hbm, prior_ref), (probes_hbm, probes_ref)]
    pairs += [(cut(map_hbm, i), cut(map_ref, i)) for i in range(MAP_PARTS)]
    copies = [pltpu.make_async_copy(a, b, sems.at[i]) for i, (a, b) in enumerate(pairs)]
    for copy in copies:
        copy.start()
    for copy in copies[:3]:
        copy.wait()
    probability = 1.0 / (1.0 + jnp.exp(-latent_ref[...]))
    weights = probability * (1.0 - probability)
    gradient = responses_ref[...].astype(F32) - probability
    inv_diag = 1.0 / (weights + prior_ref[...])
    terms_ref[0] = weights
    terms_ref[1] = inv_diag
    copies[3].wait()
    energy = jnp.zeros((rows, bs), F32)
    scaled = []
    for b in range(blocks):
        at = slice(b * bs, (b + 1) * bs)
        last = jnp.broadcast_to(gradient[b : b + 1], (rows - count, bs))
        field = pltpu.roll(jnp.concatenate([probes_ref[:, at], last], axis=0), 1, 0)
        field_ref[b] = field
        scaled.append(field * inv_diag[b : b + 1])
        energy += field * scaled[-1]
    summed = jnp.zeros(out_ref.shape, F32)
    for b in range(0, blocks, PAIR):
        if b * bs % part == 0:
            copies[4 + b * bs // part].wait()
        both = jnp.concatenate([scaled[b + i].astype(BF16) for i in range(PAIR)], axis=1)
        summed += jnp.dot(both, map_ref[b * bs : (b + PAIR) * bs], preferred_element_type=F32)
    out_ref[...] = summed
    out_ref[count + 1 : count + 2] = as_row(jnp.sum(energy, axis=1, keepdims=True), out_ref.shape[1])


def direction_kernel(sums_ref, inner_ref, terms_ref, field_ref, map_ref, dir_ref, msg_ref, product_ref, last_ref):
    blocks, _, bs = field_ref.shape
    count = msg_ref.shape[1]
    inv_diag_ref = terms_ref.at[1]
    product = jnp.dot(sums_ref[...], inner_ref[...], precision=lax.Precision.HIGH)
    product_ref[...] = product
    coeffs = product.astype(BF16)
    for b in range(0, blocks, PAIR):
        correction = lax.dot_general(
            coeffs, map_ref[b * bs : (b + PAIR) * bs], (((1,), (1,)), ((), ())), preferred_element_type=F32
        )
        for c in range(b, b + PAIR):
            direction = (field_ref[c] + correction[:, (c - b) * bs : (c - b + 1) * bs]) * inv_diag_ref[c : c + 1]
            dir_ref[c] = direction
            msg_ref[c] = direction[:count].astype(BF16)
            last_ref[c : c + 1] = direction[count : count + 1]
    msg_ref[blocks] = last_ref[...].astype(BF16)


def load_kernel(factor_hbm, inner_hbm, after_ref, factor_ref, inner_ref, sems):
    copies = [
        pltpu.make_async_copy(factor_hbm, factor_ref, sems.at[0]),
        pltpu.make_async_copy(inner_hbm, inner_ref, sems.at[1]),
    ]
    for copy in copies:
        copy.start()
    for copy in copies:
        copy.wait()


def turn_kernel(factor_ref, after_ref, turned_ref):
    blocks, taps, bs, _ = factor_ref.shape
    for b in range(blocks):
        for k in range(taps):
            turned_ref[b, k * bs : (k + 1) * bs] = factor_ref[b, k].T


def tall_block(refs, lasts, at, tall):
    most = refs[at]
    last = jnp.broadcast_to(lasts[pl.ds(at, 1), :], (tall - most.shape[0], most.shape[1]))
    return jnp.concatenate([most, last.astype(BF16)], axis=0)


def own_image_kernel(tall, own_ref, turned_ref, image_ref, zeros_ref, last_ref):
    blocks, bs = last_ref.shape
    zeros_ref[...] = jnp.zeros_like(zeros_ref)
    last_ref[...] = own_ref[blocks].astype(F32)
    for b in range(blocks):
        image_ref[b] = jnp.dot(tall_block(own_ref, last_ref, b, tall), turned_ref[b, :bs], preferred_element_type=F32)


def pass_on_kernel(near_ref, after_ref, out_ref):
    out_ref[...] = near_ref[...]


def join_kernel(back_far_ref, got_ref, out_ref):
    out_ref[...] = (back_far_ref[...].astype(F32) + got_ref[...].astype(F32)).astype(BF16)


def own_back_kernel(rows, image_ref, factor_ref, total_ref, curve_ref, dir_ref, terms_ref, base_ref, curve_out_ref):
    blocks = factor_ref.shape[0]
    curve = curve_ref[...]
    for b in range(blocks):
        direction = dir_ref[b]
        weighted = terms_ref[0, b : b + 1] * direction
        curve += weighted * direction
        back = jnp.dot(image_ref[b], factor_ref[b, 0], preferred_element_type=F32)[:rows]
        base_ref[b] = total_ref[2 * blocks + b] + back + weighted
    curve_out_ref[...] = curve


def hessian_kernel(
    rows, ids_ref, factor_ref, turned_ref, own_image_ref, near_ref, far_even_ref, far_odd_ref, own_ref, zeros_ref,
    back_far_ref, back_near_ref, total_ref, curve_ref, image_ref, around_ref, around_last_ref, last_ref,
):
    blocks, taps, bs, _ = factor_ref.shape
    count = around_ref.shape[1]
    tall = image_ref.shape[1]
    for i, refs in enumerate(((far_even_ref, far_odd_ref), (near_ref,), (own_ref,))):
        at = slice(i * blocks, (i + 1) * blocks)
        around_ref[at] = functools.reduce(jnp.add, [ref[:blocks] for ref in refs])
        around_last_ref[at] = functools.reduce(jnp.add, [ref[blocks].astype(F32) for ref in refs])
    first = (lax.axis_index("space") - 2) * blocks
    curve = jnp.zeros((rows, bs), F32)
    ids = lambda b, k: ids_ref[k - 1, b] - first
    side_by_side = lambda b: jnp.concatenate([factor_ref[b, k] for k in range(1, taps)], axis=1)
    for b in range(blocks):
        chosen = [tall_block(around_ref, around_last_ref, ids(b, k), tall) for k in range(1, taps)]
        image = own_image_ref[b] + jnp.dot(
            jnp.concatenate(chosen, axis=1), turned_ref[b, bs:], preferred_element_type=F32
        )
        rounded = image.astype(BF16)
        image_ref[b] = rounded
        curve += (image * rounded.astype(F32))[:rows]
    curve_ref[...] = curve
    for b in range(blocks):
        back = jnp.dot(image_ref[b], side_by_side(b), preferred_element_type=F32)
        for k in range(1, taps):
            total_ref[ids(b, k)] += back[:rows, (k - 1) * bs : k * bs]
    for i, ref in enumerate((back_far_ref, back_near_ref)):
        for b in range(blocks):
            ref[b] = total_ref[i * blocks + b, :count].astype(BF16)
            last_ref[b : b + 1] = total_ref[i * blocks + b, count : count + 1]
        ref[blocks] = last_ref[...].astype(BF16)


def combine_kernel(
    base_ref, even_ref, odd_ref, mate_ref, curve_ref, terms_ref, field_ref, map_ref, hess_ref, out_ref
):
    blocks, rows, bs = field_ref.shape
    count = mate_ref.shape[1]
    inv_diag_ref = terms_ref.at[1]
    own_part = jnp.where(is_even("space"), 1.0, 0.0)
    arrived = lambda c: even_ref[c].astype(F32) + odd_ref[c].astype(F32) + own_part * mate_ref[c].astype(F32)
    from_last = arrived(blocks)
    cross = jnp.zeros((rows, bs), F32)
    square = jnp.zeros((rows, bs), F32)
    summed = jnp.zeros(out_ref.shape, F32)
    for b in range(0, blocks, PAIR):
        parts = []
        for c in range(b, b + PAIR):
            last = jnp.broadcast_to(from_last[c : c + 1], (rows - count, bs))
            hess = base_ref[c] + jnp.concatenate([arrived(c), last], axis=0)
            hess_ref[c] = hess
            scaled = hess * inv_diag_ref[c : c + 1]
            cross += field_ref[c] * scaled
            square += hess * scaled
            parts.append(scaled.astype(BF16))
        summed += jnp.dot(
            jnp.concatenate(parts, axis=1), map_ref[b * bs : (b + PAIR) * bs], preferred_element_type=F32
        )
    out_ref[...] = summed
    for i, acc in enumerate((curve_ref[...], cross, square)):
        out_ref[count + 1 + i : count + 2 + i] = as_row(jnp.sum(acc, axis=1, keepdims=True), out_ref.shape[1])


def finish_kernel(
    sums_ref, product_ref, hess_sums_ref, inner_ref, dir_ref, hess_ref, terms_ref, field_ref, map_ref, solution_hbm,
    residual_hbm, next_hbm, solution_ref, residual_ref, next_ref, sems,
):
    blocks, rows, bs = field_ref.shape
    whole = solution_ref.shape[0]
    inv_diag_ref = terms_ref.at[1]
    sums, product, hess_sums = sums_ref[...], product_ref[...], hess_sums_ref[...]
    column = lambda x, i: as_column(x[whole + i : whole + i + 1], rows)
    coeffs = product.astype(BF16)
    plain = column(sums, 0)
    energy = plain + jnp.sum(coeffs.astype(F32) * sums, axis=1, keepdims=True)
    step = energy / column(hess_sums, 0)
    left = sums - step * hess_sums
    hess_product = jnp.dot(hess_sums, inner_ref[...], precision=lax.Precision.HIGH)
    coeffs = (product - step * hess_product).astype(BF16)
    plain_next = plain - 2.0 * step * column(hess_sums, 1) + step * step * column(hess_sums, 2)
    energy_next = plain_next + jnp.sum(coeffs.astype(F32) * left, axis=1, keepdims=True)
    ratio = energy_next / energy
    part = blocks // OUT_PARTS
    copies = []

    def send(i, ref, hbm):
        at = pl.ds(i * part * bs, part * bs)
        copies.append(pltpu.make_async_copy(ref.at[:, at], hbm.at[:, at], sems.at[len(copies)]))
        copies[-1].start()

    residual_of = lambda c: field_ref[c] - step * hess_ref[c]
    for i in range(OUT_PARTS):
        for c in range(i * part, (i + 1) * part):
            at = slice(c * bs, (c + 1) * bs)
            solution_ref[:, at] = (step * dir_ref[c])[:whole]
            residual_ref[:, at] = residual_of(c)[:whole]
        send(i, solution_ref, solution_hbm)
        send(i, residual_ref, residual_hbm)
    for i in range(OUT_PARTS):
        for b in range(i * part, (i + 1) * part, PAIR):
            correction = lax.dot_general(
                coeffs, map_ref[b * bs : (b + PAIR) * bs], (((1,), (1,)), ((), ())), preferred_element_type=F32
            )
            for c in range(b, b + PAIR):
                smoothed = (residual_of(c) + correction[:, (c - b) * bs : (c - b + 1) * bs]) * inv_diag_ref[c : c + 1]
                next_ref[:, c * bs : (c + 1) * bs] = (smoothed + ratio * dir_ref[c])[:whole]
        send(i, next_ref, next_hbm)
    for copy in copies:
        copy.wait()


def call(kernel, ins, outs, scratch=(), limit=16, keep=True, aliases={}):
    spec = lambda space: pl.BlockSpec(memory_space=space)
    shapes = tuple((pltpu.VMEM if keep else jax.ShapeDtypeStruct)(s, t) for s, t in outs)
    specs = (spec(pltpu.VMEM if keep else pl.ANY),) * len(shapes)
    return pl.pallas_call(
        kernel,
        out_shape=shapes if len(shapes) > 1 else shapes[0],
        in_specs=[spec(space) for space in ins],
        out_specs=specs if len(shapes) > 1 else specs[0],
        scratch_shapes=scratch,
        input_output_aliases=aliases,
        compiler_params=pltpu.CompilerParams(vmem_limit_bytes=limit * 1024 * 1024),
    )


def in_hbm(x):
    return pltpu.with_memory_space_constraint(x, pltpu.HBM)


def in_vmem(x):
    return pltpu.with_memory_space_constraint(x, pltpu.VMEM)


def body(latent, responses, probes, prior_diag, factor, cond_ids, inducing_map, inner_inverse):
    blocks, _, bs, _ = factor.shape
    count = probes.shape[0]
    rows, tall = count + 8, count + 16
    by_block = lambda x: x.reshape(blocks, bs)
    sum_shape = ((rows, inducing_map.shape[1]), F32)
    field = ((blocks, rows, bs), F32)
    packed = ((blocks + 1, count, bs), BF16)
    vmem, smem = pltpu.VMEM, pltpu.SMEM
    partial, terms, right_side, inducing_map = call(
        project_kernel,
        [pl.ANY] * 5,
        [sum_shape, ((2, blocks, bs), F32), field, (inducing_map.shape, BF16)],
        [
            vmem((blocks, bs), F32),
            vmem((blocks, bs), jnp.int32),
            vmem((blocks, bs), F32),
            vmem(probes.shape, F32),
            pltpu.SemaphoreType.DMA((4 + MAP_PARTS,)),
        ],
    )(*map(in_hbm, (by_block(latent), by_block(responses), by_block(prior_diag), probes, inducing_map)))
    points = (terms, right_side, inducing_map)

    def load(msg):
        outs = [(factor.shape, BF16), (inner_inverse.shape, F32)]
        return call(load_kernel, [pl.ANY] * 3, outs, [pltpu.SemaphoreType.DMA((2,))])(
            in_hbm(factor), in_hbm(inner_inverse), msg
        )

    sums, (factor, inner_inverse) = total(partial, "space", load)
    direction, rounded, product = call(
        direction_kernel, [vmem] * 5, [field, packed, sum_shape], [vmem((blocks, bs), F32)]
    )(sums, inner_inverse, *points)
    near = sent(rounded, "space", 1)
    far_even = sent(rounded, "space", 2, (0,))
    turned = call(turn_kernel, [vmem, pl.ANY], [((blocks, factor.shape[1] * bs, bs), BF16)])(factor, rounded)
    around = ((3 * blocks, rows, bs), F32)
    own_image, zeros = call(
        functools.partial(own_image_kernel, tall),
        [vmem] * 2,
        [((blocks, tall, bs), F32), around],
        [vmem((blocks, bs), F32)],
    )(rounded, turned)
    far_odd = sent(call(pass_on_kernel, [vmem, pl.ANY], [packed])(near, own_image), "space", 1, (0,))
    back_far, back_near, back_own, curve, image = call(
        functools.partial(hessian_kernel, rows),
        [smem] + [vmem] * 8,
        [packed, packed, around, ((rows, bs), F32), ((blocks, tall, bs), BF16)],
        [vmem((3 * blocks, count, bs), BF16), vmem((3 * blocks, bs), F32), vmem((blocks, bs), F32)],
        aliases={8: 2},
    )(cond_ids.T, factor, turned, own_image, near, far_even, far_odd, rounded, zeros)
    mate = swapped(back_near, "space")
    from_even = sent(back_far, "space", -2, (0,))
    from_odd = sent(call(join_kernel, [vmem] * 2, [packed])(back_far, mate), "space", -2, (1,))
    base, curve = call(functools.partial(own_back_kernel, rows), [vmem] * 6, [field, ((rows, bs), F32)])(
        image, factor, back_own, curve, direction, terms
    )
    hess, partial = call(combine_kernel, [vmem] * 8, [field, sum_shape])(base, from_even, from_odd, mate, curve, *points)
    hess_sums, _ = total(partial, "space")
    whole = ((count + 1, blocks * bs), F32)
    scratch = [vmem(*whole)] * 3 + [pltpu.SemaphoreType.DMA((3 * OUT_PARTS,))]
    return call(finish_kernel, [vmem] * 9, [whole] * 3, scratch, keep=False)(
        *map(in_vmem, (sums, product, hess_sums, inner_inverse, direction, hess, *points))
    )


def solution(mesh):
    return jax.shard_map(
        body,
        mesh=mesh,
        in_specs=(
            P(("groups", "space")),
            P(("groups", "space")),
            P(None, ("groups", "space")),
            P(("groups", "space")),
            P(("groups", "space"), None, None, None),
            P(("groups", "space"), None),
            P(("groups", "space"), None),
            P("groups", None),
        ),
        out_specs=(
            P(None, ("groups", "space")),
            P(None, ("groups", "space")),
            P(None, ("groups", "space")),
        ),
        check_vma=False,
    )
```

```python
import functools

import jax
import jax.numpy as jnp
from jax import lax
from jax.experimental import pallas as pl
from jax.experimental.pallas import tpu as pltpu
from jax.sharding import PartitionSpec as P

F32, BF16 = jnp.float32, jnp.bfloat16
PAIR = 2
MAP_PARTS = 4
OUT_PARTS = 4


def sent(block, axis, distance, parities=(0, 1)):
    devices = range(lax.axis_size(axis))
    return lax.ppermute(block, axis, [(i, i + distance) for i in devices if i % 2 in parities and i + distance in devices])


def swapped(block, axis):
    return lax.ppermute(block, axis, [(i, i ^ 1) for i in range(lax.axis_size(axis))])


def is_even(axis):
    return lax.rem(lax.axis_index(axis), 2) == 0


def write_message(msg_ref, x):
    top, half = x.shape[0] - 8, x.shape[1] // 2
    value, beside = x[top:, :half], x[top:, half:]
    high = value.astype(BF16).astype(F32)
    middle = (value - high).astype(BF16).astype(F32)
    low = value - high - middle
    row = lax.broadcasted_iota(jnp.int32, value.shape, 0)
    left = jnp.where(row < 4, high, pltpu.roll(low, 3, 0))
    right = jnp.where(row < 1, beside, middle)
    msg_ref[...] = jnp.concatenate([x[:top], jnp.concatenate([left, right], axis=1)], axis=0).astype(BF16)


def read_message(msg_ref):
    x = msg_ref[...].astype(F32)
    top, half = x.shape[0] - 8, x.shape[1] // 2
    left, right = x[top:, :half], x[top:, half:]
    row = lax.broadcasted_iota(jnp.int32, left.shape, 0)
    left = jnp.where(row < 1, left, left + right + pltpu.roll(left, 5, 0))
    return jnp.concatenate([x[:top], jnp.concatenate([left, right], axis=1)], axis=0)


def add_kernel(count, held, x_ref, *refs):
    in_refs, (out_ref, *msg_refs) = refs[: count - 1], refs[count - 1 + held :]
    x = x_ref[...]
    for ref in in_refs:
        x = x + (ref[...] if ref.dtype == F32 else read_message(ref))
    out_ref[...] = x
    for ref in msg_refs:
        write_message(ref, x)


def rounds_of(n):
    rounds = [(1,)] + [(3,)] * (n > 2)
    step = 4
    while step < n:
        rounds.append(tuple((m * step) ^ 1 for m in range(1, 4) if m * step < n))
        step *= 4
    return rounds


def total(x, axis, beside=None):
    n = lax.axis_size(axis)
    if n & (n - 1):
        return lax.psum(x, axis), beside(x) if beside else ()
    rounds = rounds_of(n)
    msg = x
    for i, partners in enumerate(rounds):
        got = [lax.ppermute(msg, axis, [(j, j ^ d) for j in range(n)]) for d in partners]
        last = i + 1 == len(rounds)
        held = beside(msg) if beside and last else ()
        add = functools.partial(add_kernel, len(got) + 1, len(held))
        ins = [pltpu.VMEM] * (len(got) + 1) + [pl.ANY] * len(held)
        outs = [(x.shape, F32)] + [(x.shape, BF16)] * (not last)
        x, *rest = jax.tree.leaves(call(add, ins, outs)(x, *got, *held))
        msg = rest[0] if rest else None
    return x, held


def eye(rows, lanes):
    return lax.broadcasted_iota(jnp.int32, (rows, lanes), 0) == lax.broadcasted_iota(jnp.int32, (rows, lanes), 1)


def as_row(column, lanes):
    return jnp.sum(jnp.where(eye(column.shape[0], lanes), column, 0.0), axis=0, keepdims=True)


def as_column(row, rows):
    return jnp.sum(jnp.where(eye(rows, row.shape[1]), row, 0.0), axis=1, keepdims=True)


def project_kernel(
    latent_hbm, responses_hbm, prior_hbm, probes_hbm, map_hbm, out_ref, terms_ref, field_ref, map_ref, latent_ref,
    responses_ref, prior_ref, probes_ref, sems,
):
    blocks, bs = latent_ref.shape
    rows = out_ref.shape[0]
    count = probes_ref.shape[0]
    part = map_ref.shape[0] // MAP_PARTS
    cut = lambda ref, i: ref.at[i * part : (i + 1) * part]
    pairs = [(latent_hbm, latent_ref), (responses_hbm, responses_ref), (prior_hbm, prior_ref), (probes_hbm, probes_ref)]
    pairs += [(cut(map_hbm, i), cut(map_ref, i)) for i in range(MAP_PARTS)]
    copies = [pltpu.make_async_copy(a, b, sems.at[i]) for i, (a, b) in enumerate(pairs)]
    for copy in copies:
        copy.start()
    for copy in copies[:3]:
        copy.wait()
    probability = 1.0 / (1.0 + jnp.exp(-latent_ref[...]))
    weights = probability * (1.0 - probability)
    gradient = responses_ref[...].astype(F32) - probability
    inv_diag = 1.0 / (weights + prior_ref[...])
    terms_ref[0] = weights
    terms_ref[1] = inv_diag
    copies[3].wait()
    energy = jnp.zeros((rows, bs), F32)
    scaled = []
    for b in range(blocks):
        at = slice(b * bs, (b + 1) * bs)
        last = jnp.broadcast_to(gradient[b : b + 1], (rows - count, bs))
        field = pltpu.roll(jnp.concatenate([probes_ref[:, at], last], axis=0), 1, 0)
        field_ref[b] = field
        scaled.append(field * inv_diag[b : b + 1])
        energy += field * scaled[-1]
    summed = jnp.zeros(out_ref.shape, F32)
    for b in range(0, blocks, PAIR):
        if b * bs % part == 0:
            copies[4 + b * bs // part].wait()
        both = jnp.concatenate([scaled[b + i].astype(BF16) for i in range(PAIR)], axis=1)
        summed += jnp.dot(both, map_ref[b * bs : (b + PAIR) * bs], preferred_element_type=F32)
    out_ref[...] = summed
    out_ref[count + 1 : count + 2] = as_row(jnp.sum(energy, axis=1, keepdims=True), out_ref.shape[1])


def direction_kernel(sums_ref, inner_ref, terms_ref, field_ref, map_ref, dir_ref, msg_ref, product_ref, last_ref):
    blocks, _, bs = field_ref.shape
    count = msg_ref.shape[1]
    inv_diag_ref = terms_ref.at[1]
    product = jnp.dot(sums_ref[...], inner_ref[...], precision=lax.Precision.HIGH)
    product_ref[...] = product
    coeffs = product.astype(BF16)
    for b in range(0, blocks, PAIR):
        correction = lax.dot_general(
            coeffs, map_ref[b * bs : (b + PAIR) * bs], (((1,), (1,)), ((), ())), preferred_element_type=F32
        )
        for c in range(b, b + PAIR):
            direction = (field_ref[c] + correction[:, (c - b) * bs : (c - b + 1) * bs]) * inv_diag_ref[c : c + 1]
            dir_ref[c] = direction
            msg_ref[c] = direction[:count].astype(BF16)
            last_ref[c : c + 1] = direction[count : count + 1]
    msg_ref[blocks] = last_ref[...].astype(BF16)


def load_kernel(factor_hbm, inner_hbm, after_ref, factor_ref, inner_ref, sems):
    copies = [
        pltpu.make_async_copy(factor_hbm, factor_ref, sems.at[0]),
        pltpu.make_async_copy(inner_hbm, inner_ref, sems.at[1]),
    ]
    for copy in copies:
        copy.start()
    for copy in copies:
        copy.wait()


def turn_kernel(factor_ref, after_ref, turned_ref):
    blocks, taps, bs, _ = factor_ref.shape
    for b in range(blocks):
        for k in range(taps):
            turned_ref[b, k * bs : (k + 1) * bs] = factor_ref[b, k].T


def tall_block(refs, lasts, at, tall):
    most = refs[at]
    last = jnp.broadcast_to(lasts[pl.ds(at, 1), :], (tall - most.shape[0], most.shape[1]))
    return jnp.concatenate([most, last.astype(BF16)], axis=0)


def own_image_kernel(tall, own_ref, turned_ref, image_ref, zeros_ref, last_ref):
    blocks, bs = last_ref.shape
    zeros_ref[...] = jnp.zeros_like(zeros_ref)
    last_ref[...] = own_ref[blocks].astype(F32)
    for b in range(blocks):
        image_ref[b] = jnp.dot(tall_block(own_ref, last_ref, b, tall), turned_ref[b, :bs], preferred_element_type=F32)


def pass_on_kernel(own_ref, far_ref, after_ref, out_ref):
    @pl.when(is_even("space"))
    def _():
        out_ref[...] = own_ref[...]

    @pl.when(jnp.logical_not(is_even("space")))
    def _():
        out_ref[...] = far_ref[...]


def join_kernel(back_far_ref, got_ref, out_ref):
    out_ref[...] = (back_far_ref[...].astype(F32) + got_ref[...].astype(F32)).astype(BF16)


def own_back_kernel(rows, image_ref, factor_ref, total_ref, curve_ref, dir_ref, terms_ref, base_ref, curve_out_ref):
    blocks = factor_ref.shape[0]
    curve = curve_ref[...]
    for b in range(blocks):
        direction = dir_ref[b]
        weighted = terms_ref[0, b : b + 1] * direction
        curve += weighted * direction
        back = jnp.dot(image_ref[b], factor_ref[b, 0], preferred_element_type=F32)[:rows]
        base_ref[b] = total_ref[2 * blocks + b] + back + weighted
    curve_out_ref[...] = curve


def hessian_kernel(
    rows, ids_ref, factor_ref, turned_ref, own_image_ref, near_ref, far_even_ref, far_odd_ref, own_ref, zeros_ref,
    back_far_ref, back_near_ref, total_ref, curve_ref, image_ref, around_ref, around_last_ref, last_ref,
):
    blocks, taps, bs, _ = factor_ref.shape
    count = around_ref.shape[1]
    tall = image_ref.shape[1]
    for i, refs in enumerate(((far_even_ref, far_odd_ref), (near_ref,), (own_ref,))):
        at = slice(i * blocks, (i + 1) * blocks)
        around_ref[at] = functools.reduce(jnp.add, [ref[:blocks] for ref in refs])
        around_last_ref[at] = functools.reduce(jnp.add, [ref[blocks].astype(F32) for ref in refs])
    first = (lax.axis_index("space") - 2) * blocks
    curve = jnp.zeros((rows, bs), F32)
    ids = lambda b, k: ids_ref[k - 1, b] - first
    side_by_side = lambda b: jnp.concatenate([factor_ref[b, k] for k in range(1, taps)], axis=1)
    for b in range(blocks):
        chosen = [tall_block(around_ref, around_last_ref, ids(b, k), tall) for k in range(1, taps)]
        image = own_image_ref[b] + jnp.dot(
            jnp.concatenate(chosen, axis=1), turned_ref[b, bs:], preferred_element_type=F32
        )
        rounded = image.astype(BF16)
        image_ref[b] = rounded
        curve += (image * rounded.astype(F32))[:rows]
    curve_ref[...] = curve
    for b in range(blocks):
        back = jnp.dot(image_ref[b], side_by_side(b), preferred_element_type=F32)
        for k in range(1, taps):
            total_ref[ids(b, k)] += back[:rows, (k - 1) * bs : k * bs]
    for i, ref in enumerate((back_far_ref, back_near_ref)):
        for b in range(blocks):
            ref[b] = total_ref[i * blocks + b, :count].astype(BF16)
            last_ref[b : b + 1] = total_ref[i * blocks + b, count : count + 1]
        ref[blocks] = last_ref[...].astype(BF16)


def combine_kernel(
    base_ref, even_ref, odd_ref, mate_ref, curve_ref, terms_ref, field_ref, map_ref, hess_ref, out_ref
):
    blocks, rows, bs = field_ref.shape
    count = mate_ref.shape[1]
    inv_diag_ref = terms_ref.at[1]
    own_part = jnp.where(is_even("space"), 1.0, 0.0)
    arrived = lambda c: even_ref[c].astype(F32) + odd_ref[c].astype(F32) + own_part * mate_ref[c].astype(F32)
    from_last = arrived(blocks)
    cross = jnp.zeros((rows, bs), F32)
    square = jnp.zeros((rows, bs), F32)
    summed = jnp.zeros(out_ref.shape, F32)
    for b in range(0, blocks, PAIR):
        parts = []
        for c in range(b, b + PAIR):
            last = jnp.broadcast_to(from_last[c : c + 1], (rows - count, bs))
            hess = base_ref[c] + jnp.concatenate([arrived(c), last], axis=0)
            hess_ref[c] = hess
            scaled = hess * inv_diag_ref[c : c + 1]
            cross += field_ref[c] * scaled
            square += hess * scaled
            parts.append(scaled.astype(BF16))
        summed += jnp.dot(
            jnp.concatenate(parts, axis=1), map_ref[b * bs : (b + PAIR) * bs], preferred_element_type=F32
        )
    out_ref[...] = summed
    for i, acc in enumerate((curve_ref[...], cross, square)):
        out_ref[count + 1 + i : count + 2 + i] = as_row(jnp.sum(acc, axis=1, keepdims=True), out_ref.shape[1])


def finish_kernel(
    sums_ref, product_ref, hess_sums_ref, inner_ref, dir_ref, hess_ref, terms_ref, field_ref, map_ref, solution_hbm,
    residual_hbm, next_hbm, solution_ref, residual_ref, next_ref, sems,
):
    blocks, rows, bs = field_ref.shape
    whole = solution_ref.shape[0]
    inv_diag_ref = terms_ref.at[1]
    sums, product, hess_sums = sums_ref[...], product_ref[...], hess_sums_ref[...]
    column = lambda x, i: as_column(x[whole + i : whole + i + 1], rows)
    coeffs = product.astype(BF16)
    plain = column(sums, 0)
    energy = plain + jnp.sum(coeffs.astype(F32) * sums, axis=1, keepdims=True)
    step = energy / column(hess_sums, 0)
    left = sums - step * hess_sums
    hess_product = jnp.dot(hess_sums, inner_ref[...], precision=lax.Precision.HIGH)
    coeffs = (product - step * hess_product).astype(BF16)
    plain_next = plain - 2.0 * step * column(hess_sums, 1) + step * step * column(hess_sums, 2)
    energy_next = plain_next + jnp.sum(coeffs.astype(F32) * left, axis=1, keepdims=True)
    ratio = energy_next / energy
    part = blocks // OUT_PARTS
    copies = []

    def send(i, ref, hbm):
        at = pl.ds(i * part * bs, part * bs)
        copies.append(pltpu.make_async_copy(ref.at[:, at], hbm.at[:, at], sems.at[len(copies)]))
        copies[-1].start()

    residual_of = lambda c: field_ref[c] - step * hess_ref[c]
    for i in range(OUT_PARTS):
        for c in range(i * part, (i + 1) * part):
            at = slice(c * bs, (c + 1) * bs)
            solution_ref[:, at] = (step * dir_ref[c])[:whole]
            residual_ref[:, at] = residual_of(c)[:whole]
        send(i, solution_ref, solution_hbm)
        send(i, residual_ref, residual_hbm)
    for i in range(OUT_PARTS):
        for b in range(i * part, (i + 1) * part, PAIR):
            correction = lax.dot_general(
                coeffs, map_ref[b * bs : (b + PAIR) * bs], (((1,), (1,)), ((), ())), preferred_element_type=F32
            )
            for c in range(b, b + PAIR):
                smoothed = (residual_of(c) + correction[:, (c - b) * bs : (c - b + 1) * bs]) * inv_diag_ref[c : c + 1]
                next_ref[:, c * bs : (c + 1) * bs] = (smoothed + ratio * dir_ref[c])[:whole]
        send(i, next_ref, next_hbm)
    for copy in copies:
        copy.wait()


def call(kernel, ins, outs, scratch=(), limit=16, keep=True, aliases={}):
    spec = lambda space: pl.BlockSpec(memory_space=space)
    shapes = tuple((pltpu.VMEM if keep else jax.ShapeDtypeStruct)(s, t) for s, t in outs)
    specs = (spec(pltpu.VMEM if keep else pl.ANY),) * len(shapes)
    return pl.pallas_call(
        kernel,
        out_shape=shapes if len(shapes) > 1 else shapes[0],
        in_specs=[spec(space) for space in ins],
        out_specs=specs if len(shapes) > 1 else specs[0],
        scratch_shapes=scratch,
        input_output_aliases=aliases,
        compiler_params=pltpu.CompilerParams(vmem_limit_bytes=limit * 1024 * 1024),
    )


def in_hbm(x):
    return pltpu.with_memory_space_constraint(x, pltpu.HBM)


def in_vmem(x):
    return pltpu.with_memory_space_constraint(x, pltpu.VMEM)


def body(latent, responses, probes, prior_diag, factor, cond_ids, inducing_map, inner_inverse):
    blocks, _, bs, _ = factor.shape
    count = probes.shape[0]
    rows, tall = count + 8, count + 16
    by_block = lambda x: x.reshape(blocks, bs)
    sum_shape = ((rows, inducing_map.shape[1]), F32)
    field = ((blocks, rows, bs), F32)
    packed = ((blocks + 1, count, bs), BF16)
    vmem, smem = pltpu.VMEM, pltpu.SMEM
    partial, terms, right_side, inducing_map = call(
        project_kernel,
        [pl.ANY] * 5,
        [sum_shape, ((2, blocks, bs), F32), field, (inducing_map.shape, BF16)],
        [
            vmem((blocks, bs), F32),
            vmem((blocks, bs), jnp.int32),
            vmem((blocks, bs), F32),
            vmem(probes.shape, F32),
            pltpu.SemaphoreType.DMA((4 + MAP_PARTS,)),
        ],
    )(*map(in_hbm, (by_block(latent), by_block(responses), by_block(prior_diag), probes, inducing_map)))
    points = (terms, right_side, inducing_map)

    def load(msg):
        outs = [(factor.shape, BF16), (inner_inverse.shape, F32)]
        return call(load_kernel, [pl.ANY] * 3, outs, [pltpu.SemaphoreType.DMA((2,))])(
            in_hbm(factor), in_hbm(inner_inverse), msg
        )

    sums, (factor, inner_inverse) = total(partial, "space", load)
    direction, rounded, product = call(
        direction_kernel, [vmem] * 5, [field, packed, sum_shape], [vmem((blocks, bs), F32)]
    )(sums, inner_inverse, *points)
    far_odd = sent(rounded, "space", 2, (1,))
    far_even = sent(rounded, "space", 2, (0,))
    turned = call(turn_kernel, [vmem, pl.ANY], [((blocks, factor.shape[1] * bs, bs), BF16)])(factor, rounded)
    around = ((3 * blocks, rows, bs), F32)
    own_image, zeros = call(
        functools.partial(own_image_kernel, tall),
        [vmem] * 2,
        [((blocks, tall, bs), F32), around],
        [vmem((blocks, bs), F32)],
    )(rounded, turned)
    near = swapped(call(pass_on_kernel, [vmem, vmem, pl.ANY], [packed])(rounded, far_odd, own_image), "space")
    back_far, back_near, back_own, curve, image = call(
        functools.partial(hessian_kernel, rows),
        [smem] + [vmem] * 8,
        [packed, packed, around, ((rows, bs), F32), ((blocks, tall, bs), BF16)],
        [vmem((3 * blocks, count, bs), BF16), vmem((3 * blocks, bs), F32), vmem((blocks, bs), F32)],
        aliases={8: 2},
    )(cond_ids.T, factor, turned, own_image, near, far_even, far_odd, rounded, zeros)
    mate = swapped(back_near, "space")
    from_even = sent(back_far, "space", -2, (0,))
    from_odd = sent(call(join_kernel, [vmem] * 2, [packed])(back_far, mate), "space", -2, (1,))
    base, curve = call(functools.partial(own_back_kernel, rows), [vmem] * 6, [field, ((rows, bs), F32)])(
        image, factor, back_own, curve, direction, terms
    )
    hess, partial = call(combine_kernel, [vmem] * 8, [field, sum_shape])(base, from_even, from_odd, mate, curve, *points)
    hess_sums, _ = total(partial, "space")
    whole = ((count + 1, blocks * bs), F32)
    scratch = [vmem(*whole)] * 3 + [pltpu.SemaphoreType.DMA((3 * OUT_PARTS,))]
    return call(finish_kernel, [vmem] * 9, [whole] * 3, scratch, keep=False)(
        *map(in_vmem, (sums, product, hess_sums, inner_inverse, direction, hess, *points))
    )


def solution(mesh):
    return jax.shard_map(
        body,
        mesh=mesh,
        in_specs=(
            P(("groups", "space")),
            P(("groups", "space")),
            P(None, ("groups", "space")),
            P(("groups", "space")),
            P(("groups", "space"), None, None, None),
            P(("groups", "space"), None),
            P(("groups", "space"), None),
            P("groups", None),
        ),
        out_specs=(
            P(None, ("groups", "space")),
            P(None, ("groups", "space")),
            P(None, ("groups", "space")),
        ),
        check_vma=False,
    )
```

```python
import functools

import jax
import jax.numpy as jnp
from jax import lax
from jax.experimental import pallas as pl
from jax.experimental.pallas import tpu as pltpu
from jax.sharding import PartitionSpec as P

F32, BF16 = jnp.float32, jnp.bfloat16
PAIR = 2
MAP_PARTS = 4
OUT_PARTS = 4


def sent(block, axis, distance, parities=(0, 1)):
    devices = range(lax.axis_size(axis))
    return lax.ppermute(block, axis, [(i, i + distance) for i in devices if i % 2 in parities and i + distance in devices])


def swapped(block, axis):
    return lax.ppermute(block, axis, [(i, i ^ 1) for i in range(lax.axis_size(axis))])


def is_even(axis):
    return lax.rem(lax.axis_index(axis), 2) == 0


def write_message(msg_ref, x):
    top, half = x.shape[0] - 8, x.shape[1] // 2
    value, beside = x[top:, :half], x[top:, half:]
    high = value.astype(BF16).astype(F32)
    middle = (value - high).astype(BF16).astype(F32)
    low = value - high - middle
    row = lax.broadcasted_iota(jnp.int32, value.shape, 0)
    left = jnp.where(row < 4, high, pltpu.roll(low, 3, 0))
    right = jnp.where(row < 1, beside, middle)
    msg_ref[...] = jnp.concatenate([x[:top], jnp.concatenate([left, right], axis=1)], axis=0).astype(BF16)


def read_message(msg_ref):
    x = msg_ref[...].astype(F32)
    top, half = x.shape[0] - 8, x.shape[1] // 2
    left, right = x[top:, :half], x[top:, half:]
    row = lax.broadcasted_iota(jnp.int32, left.shape, 0)
    left = jnp.where(row < 1, left, left + right + pltpu.roll(left, 5, 0))
    return jnp.concatenate([x[:top], jnp.concatenate([left, right], axis=1)], axis=0)


def add_kernel(count, held, x_ref, *refs):
    in_refs, (out_ref, *msg_refs) = refs[: count - 1], refs[count - 1 + held :]
    x = x_ref[...]
    for ref in in_refs:
        x = x + (ref[...] if ref.dtype == F32 else read_message(ref))
    out_ref[...] = x
    for ref in msg_refs:
        write_message(ref, x)


def rounds_of(n):
    rounds = [(1,)] + [(3,)] * (n > 2)
    step = 4
    while step < n:
        rounds.append(tuple((m * step) ^ 1 for m in range(1, 4) if m * step < n))
        step *= 4
    return rounds


def total(x, axis, beside=()):
    n = lax.axis_size(axis)
    if n & (n - 1):
        return lax.psum(x, axis), [work(x) for work in beside]
    rounds = rounds_of(n)
    made, todo, msg = [], list(beside), x
    for i, partners in enumerate(rounds):
        got = [lax.ppermute(msg, axis, [(j, j ^ d) for j in range(n)]) for d in partners]
        last = i + 1 == len(rounds)
        held = ()
        while len(todo) >= max(len(rounds) - i, 1):
            made.append(todo.pop(0)(msg))
            held += made[-1]
        add = functools.partial(add_kernel, len(got) + 1, len(held))
        ins = [pltpu.VMEM] * (len(got) + 1) + [pl.ANY] * len(held)
        outs = [(x.shape, F32)] + [(x.shape, BF16)] * (not last)
        x, *rest = jax.tree.leaves(call(add, ins, outs)(x, *got, *held))
        msg = rest[0] if rest else None
    return x, made


def eye(rows, lanes):
    return lax.broadcasted_iota(jnp.int32, (rows, lanes), 0) == lax.broadcasted_iota(jnp.int32, (rows, lanes), 1)


def as_row(column, lanes):
    return jnp.sum(jnp.where(eye(column.shape[0], lanes), column, 0.0), axis=0, keepdims=True)


def as_column(row, rows):
    return jnp.sum(jnp.where(eye(rows, row.shape[1]), row, 0.0), axis=1, keepdims=True)


def project_kernel(
    latent_hbm, responses_hbm, prior_hbm, probes_hbm, map_hbm, out_ref, terms_ref, field_ref, map_ref, latent_ref,
    responses_ref, prior_ref, probes_ref, sems,
):
    blocks, bs = latent_ref.shape
    rows = out_ref.shape[0]
    count = probes_ref.shape[0]
    part = map_ref.shape[0] // MAP_PARTS
    cut = lambda ref, i: ref.at[i * part : (i + 1) * part]
    pairs = [(latent_hbm, latent_ref), (responses_hbm, responses_ref), (prior_hbm, prior_ref), (probes_hbm, probes_ref)]
    pairs += [(cut(map_hbm, i), cut(map_ref, i)) for i in range(MAP_PARTS)]
    copies = [pltpu.make_async_copy(a, b, sems.at[i]) for i, (a, b) in enumerate(pairs)]
    for copy in copies:
        copy.start()
    for copy in copies[:3]:
        copy.wait()
    probability = 1.0 / (1.0 + jnp.exp(-latent_ref[...]))
    weights = probability * (1.0 - probability)
    gradient = responses_ref[...].astype(F32) - probability
    inv_diag = 1.0 / (weights + prior_ref[...])
    terms_ref[0] = weights
    terms_ref[1] = inv_diag
    copies[3].wait()
    energy = jnp.zeros((rows, bs), F32)
    scaled = []
    for b in range(blocks):
        at = slice(b * bs, (b + 1) * bs)
        last = jnp.broadcast_to(gradient[b : b + 1], (rows - count, bs))
        field = pltpu.roll(jnp.concatenate([probes_ref[:, at], last], axis=0), 1, 0)
        field_ref[b] = field
        scaled.append(field * inv_diag[b : b + 1])
        energy += field * scaled[-1]
    summed = jnp.zeros(out_ref.shape, F32)
    for b in range(0, blocks, PAIR):
        if b * bs % part == 0:
            copies[4 + b * bs // part].wait()
        both = jnp.concatenate([scaled[b + i].astype(BF16) for i in range(PAIR)], axis=1)
        summed += jnp.dot(both, map_ref[b * bs : (b + PAIR) * bs], preferred_element_type=F32)
    out_ref[...] = summed
    out_ref[count + 1 : count + 2] = as_row(jnp.sum(energy, axis=1, keepdims=True), out_ref.shape[1])


def direction_kernel(sums_ref, inner_ref, terms_ref, field_ref, map_ref, dir_ref, msg_ref, product_ref, last_ref):
    blocks, _, bs = field_ref.shape
    count = msg_ref.shape[1]
    inv_diag_ref = terms_ref.at[1]
    product = jnp.dot(sums_ref[...], inner_ref[...], precision=lax.Precision.HIGH)
    product_ref[...] = product
    coeffs = product.astype(BF16)
    for b in range(0, blocks, PAIR):
        correction = jnp.dot(coeffs, map_ref[:, b * bs : (b + PAIR) * bs], preferred_element_type=F32)
        for c in range(b, b + PAIR):
            direction = (field_ref[c] + correction[:, (c - b) * bs : (c - b + 1) * bs]) * inv_diag_ref[c : c + 1]
            dir_ref[c] = direction
            msg_ref[c] = direction[:count].astype(BF16)
            last_ref[c : c + 1] = direction[count : count + 1]
    msg_ref[blocks] = last_ref[...].astype(BF16)


def turn_map_kernel(map_ref, after_ref, turned_ref):
    points, inducing = map_ref.shape
    for i in range(0, points, inducing):
        turned_ref[:, i : i + inducing] = map_ref[i : i + inducing].T


def load_kernel(factor_hbm, inner_hbm, after_ref, factor_ref, inner_ref, sems):
    copies = [
        pltpu.make_async_copy(factor_hbm, factor_ref, sems.at[0]),
        pltpu.make_async_copy(inner_hbm, inner_ref, sems.at[1]),
    ]
    for copy in copies:
        copy.start()
    for copy in copies:
        copy.wait()


def turn_kernel(factor_ref, after_ref, turned_ref):
    blocks, taps, bs, _ = factor_ref.shape
    for b in range(blocks):
        for k in range(1, taps):
            turned_ref[b, (k - 1) * bs : k * bs] = factor_ref[b, k].T


def tall_block(refs, lasts, at, tall):
    most = refs[at]
    last = jnp.broadcast_to(lasts[pl.ds(at, 1), :], (tall - most.shape[0], most.shape[1]))
    return jnp.concatenate([most, last.astype(BF16)], axis=0)


def own_image_kernel(tall, own_ref, factor_ref, image_ref, again_ref, zeros_ref, last_ref):
    blocks, bs = last_ref.shape
    again_ref[...] = own_ref[...]
    zeros_ref[...] = jnp.zeros_like(zeros_ref)
    last_ref[...] = own_ref[blocks].astype(F32)
    for b in range(blocks):
        image_ref[b] = lax.dot_general(
            tall_block(own_ref, last_ref, b, tall),
            factor_ref[b, 0],
            (((1,), (1,)), ((), ())),
            preferred_element_type=F32,
        )


def pass_on_kernel(own_ref, far_ref, after_ref, out_ref):
    @pl.when(is_even("space"))
    def _():
        out_ref[...] = own_ref[...]

    @pl.when(jnp.logical_not(is_even("space")))
    def _():
        out_ref[...] = far_ref[...]


def join_kernel(back_far_ref, got_ref, out_ref):
    out_ref[...] = (back_far_ref[...].astype(F32) + got_ref[...].astype(F32)).astype(BF16)


def own_back_kernel(rows, image_ref, factor_ref, total_ref, curve_ref, dir_ref, terms_ref, base_ref, curve_out_ref):
    blocks = factor_ref.shape[0]
    curve = curve_ref[...]
    for b in range(blocks):
        direction = dir_ref[b]
        weighted = terms_ref[0, b : b + 1] * direction
        curve += weighted * direction
        back = jnp.dot(image_ref[b], factor_ref[b, 0], preferred_element_type=F32)[:rows]
        base_ref[b] = total_ref[2 * blocks + b] + back + weighted
    curve_out_ref[...] = curve


def hessian_kernel(
    rows, ids_ref, factor_ref, turned_ref, own_image_ref, near_ref, far_even_ref, far_odd_ref, own_ref, zeros_ref,
    back_far_ref, back_near_ref, total_ref, curve_ref, image_ref, around_ref, around_last_ref, last_ref,
):
    blocks, taps, bs, _ = factor_ref.shape
    count = around_ref.shape[1]
    tall = image_ref.shape[1]
    for i, refs in enumerate(((far_even_ref, far_odd_ref), (near_ref,), (own_ref,))):
        at = slice(i * blocks, (i + 1) * blocks)
        around_ref[at] = functools.reduce(jnp.add, [ref[:blocks] for ref in refs])
        around_last_ref[at] = functools.reduce(jnp.add, [ref[blocks].astype(F32) for ref in refs])
    first = (lax.axis_index("space") - 2) * blocks
    curve = jnp.zeros((rows, bs), F32)
    ids = lambda b, k: ids_ref[k - 1, b] - first
    side_by_side = lambda b: jnp.concatenate([factor_ref[b, k] for k in range(1, taps)], axis=1)
    for b in range(blocks):
        chosen = [tall_block(around_ref, around_last_ref, ids(b, k), tall) for k in range(1, taps)]
        image = own_image_ref[b] + jnp.dot(
            jnp.concatenate(chosen, axis=1), turned_ref[b], preferred_element_type=F32
        )
        rounded = image.astype(BF16)
        image_ref[b] = rounded
        curve += (image * rounded.astype(F32))[:rows]
    curve_ref[...] = curve
    for b in range(blocks):
        back = jnp.dot(image_ref[b], side_by_side(b), preferred_element_type=F32)
        for k in range(1, taps):
            total_ref[ids(b, k)] += back[:rows, (k - 1) * bs : k * bs]
    for i, ref in enumerate((back_far_ref, back_near_ref)):
        for b in range(blocks):
            ref[b] = total_ref[i * blocks + b, :count].astype(BF16)
            last_ref[b : b + 1] = total_ref[i * blocks + b, count : count + 1]
        ref[blocks] = last_ref[...].astype(BF16)


def combine_kernel(
    base_ref, even_ref, odd_ref, mate_ref, curve_ref, terms_ref, field_ref, map_ref, hess_ref, out_ref
):
    blocks, rows, bs = field_ref.shape
    count = mate_ref.shape[1]
    inv_diag_ref = terms_ref.at[1]
    own_part = jnp.where(is_even("space"), 1.0, 0.0)
    arrived = lambda c: even_ref[c].astype(F32) + odd_ref[c].astype(F32) + own_part * mate_ref[c].astype(F32)
    from_last = arrived(blocks)
    cross = jnp.zeros((rows, bs), F32)
    square = jnp.zeros((rows, bs), F32)
    summed = jnp.zeros(out_ref.shape, F32)
    for b in range(0, blocks, PAIR):
        parts = []
        for c in range(b, b + PAIR):
            last = jnp.broadcast_to(from_last[c : c + 1], (rows - count, bs))
            hess = base_ref[c] + jnp.concatenate([arrived(c), last], axis=0)
            hess_ref[c] = hess
            scaled = hess * inv_diag_ref[c : c + 1]
            cross += field_ref[c] * scaled
            square += hess * scaled
            parts.append(scaled.astype(BF16))
        summed += jnp.dot(
            jnp.concatenate(parts, axis=1), map_ref[b * bs : (b + PAIR) * bs], preferred_element_type=F32
        )
    out_ref[...] = summed
    for i, acc in enumerate((curve_ref[...], cross, square)):
        out_ref[count + 1 + i : count + 2 + i] = as_row(jnp.sum(acc, axis=1, keepdims=True), out_ref.shape[1])


def finish_kernel(
    sums_ref, product_ref, hess_sums_ref, inner_ref, dir_ref, hess_ref, terms_ref, field_ref, map_ref, solution_hbm,
    residual_hbm, next_hbm, solution_ref, residual_ref, next_ref, sems,
):
    blocks, rows, bs = field_ref.shape
    whole = solution_ref.shape[0]
    inv_diag_ref = terms_ref.at[1]
    sums, product, hess_sums = sums_ref[...], product_ref[...], hess_sums_ref[...]
    column = lambda x, i: as_column(x[whole + i : whole + i + 1], rows)
    coeffs = product.astype(BF16)
    plain = column(sums, 0)
    energy = plain + jnp.sum(coeffs.astype(F32) * sums, axis=1, keepdims=True)
    step = energy / column(hess_sums, 0)
    left = sums - step * hess_sums
    hess_product = jnp.dot(hess_sums, inner_ref[...], precision=lax.Precision.HIGH)
    coeffs = (product - step * hess_product).astype(BF16)
    plain_next = plain - 2.0 * step * column(hess_sums, 1) + step * step * column(hess_sums, 2)
    energy_next = plain_next + jnp.sum(coeffs.astype(F32) * left, axis=1, keepdims=True)
    ratio = energy_next / energy
    part = blocks // OUT_PARTS
    copies = []

    def send(i, ref, hbm):
        at = pl.ds(i * part * bs, part * bs)
        copies.append(pltpu.make_async_copy(ref.at[:, at], hbm.at[:, at], sems.at[len(copies)]))
        copies[-1].start()

    residual_of = lambda c: field_ref[c] - step * hess_ref[c]
    for i in range(OUT_PARTS):
        for c in range(i * part, (i + 1) * part):
            at = slice(c * bs, (c + 1) * bs)
            solution_ref[:, at] = (step * dir_ref[c])[:whole]
            residual_ref[:, at] = residual_of(c)[:whole]
        send(i, solution_ref, solution_hbm)
        send(i, residual_ref, residual_hbm)
    for i in range(OUT_PARTS):
        for b in range(i * part, (i + 1) * part, PAIR):
            correction = jnp.dot(coeffs, map_ref[:, b * bs : (b + PAIR) * bs], preferred_element_type=F32)
            for c in range(b, b + PAIR):
                smoothed = (residual_of(c) + correction[:, (c - b) * bs : (c - b + 1) * bs]) * inv_diag_ref[c : c + 1]
                next_ref[:, c * bs : (c + 1) * bs] = (smoothed + ratio * dir_ref[c])[:whole]
        send(i, next_ref, next_hbm)
    for copy in copies:
        copy.wait()


def call(kernel, ins, outs, scratch=(), limit=16, keep=True, aliases={}):
    spec = lambda space: pl.BlockSpec(memory_space=space)
    shapes = tuple((pltpu.VMEM if keep else jax.ShapeDtypeStruct)(s, t) for s, t in outs)
    specs = (spec(pltpu.VMEM if keep else pl.ANY),) * len(shapes)
    return pl.pallas_call(
        kernel,
        out_shape=shapes if len(shapes) > 1 else shapes[0],
        in_specs=[spec(space) for space in ins],
        out_specs=specs if len(shapes) > 1 else specs[0],
        scratch_shapes=scratch,
        input_output_aliases=aliases,
        compiler_params=pltpu.CompilerParams(vmem_limit_bytes=limit * 1024 * 1024),
    )


def in_hbm(x):
    return pltpu.with_memory_space_constraint(x, pltpu.HBM)


def in_vmem(x):
    return pltpu.with_memory_space_constraint(x, pltpu.VMEM)


def body(latent, responses, probes, prior_diag, factor, cond_ids, inducing_map, inner_inverse):
    blocks, _, bs, _ = factor.shape
    count = probes.shape[0]
    rows, tall = count + 8, count + 16
    by_block = lambda x: x.reshape(blocks, bs)
    sum_shape = ((rows, inducing_map.shape[1]), F32)
    field = ((blocks, rows, bs), F32)
    packed = ((blocks + 1, count, bs), BF16)
    vmem, smem = pltpu.VMEM, pltpu.SMEM
    partial, terms, right_side, inducing_map = call(
        project_kernel,
        [pl.ANY] * 5,
        [sum_shape, ((2, blocks, bs), F32), field, (inducing_map.shape, BF16)],
        [
            vmem((blocks, bs), F32),
            vmem((blocks, bs), jnp.int32),
            vmem((blocks, bs), F32),
            vmem(probes.shape, F32),
            pltpu.SemaphoreType.DMA((4 + MAP_PARTS,)),
        ],
    )(*map(in_hbm, (by_block(latent), by_block(responses), by_block(prior_diag), probes, inducing_map)))
    points = (terms, right_side, inducing_map)

    def load(msg):
        outs = [(factor.shape, BF16), (inner_inverse.shape, F32)]
        return call(load_kernel, [pl.ANY] * 3, outs, [pltpu.SemaphoreType.DMA((2,))])(
            in_hbm(factor), in_hbm(inner_inverse), msg
        )

    def turn_map(msg):
        return (call(turn_map_kernel, [vmem, pl.ANY], [(inducing_map.shape[::-1], BF16)])(inducing_map, msg),)

    sums, ((turned_map,), (factor, inner_inverse)) = total(partial, "space", [turn_map, load])
    direction, rounded, product = call(
        direction_kernel, [vmem] * 5, [field, packed, sum_shape], [vmem((blocks, bs), F32)]
    )(sums, inner_inverse, terms, right_side, turned_map)
    far_odd = sent(rounded, "space", 2, (1,))
    around = ((3 * blocks, rows, bs), F32)
    own_image, again, zeros = call(
        functools.partial(own_image_kernel, tall),
        [vmem] * 2,
        [((blocks, tall, bs), F32), packed, around],
        [vmem((blocks, bs), F32)],
    )(rounded, factor)
    far_even = sent(again, "space", 2, (0,))
    shape = (blocks, (factor.shape[1] - 1) * bs, bs)
    turned = call(turn_kernel, [vmem, pl.ANY], [(shape, BF16)])(factor, own_image)
    near = swapped(call(pass_on_kernel, [vmem, vmem, pl.ANY], [packed])(rounded, far_odd, turned), "space")
    back_far, back_near, back_own, curve, image = call(
        functools.partial(hessian_kernel, rows),
        [smem] + [vmem] * 8,
        [packed, packed, around, ((rows, bs), F32), ((blocks, tall, bs), BF16)],
        [vmem((3 * blocks, count, bs), BF16), vmem((3 * blocks, bs), F32), vmem((blocks, bs), F32)],
        aliases={8: 2},
    )(cond_ids.T, factor, turned, own_image, near, far_even, far_odd, rounded, zeros)
    mate = swapped(back_near, "space")
    from_even = sent(back_far, "space", -2, (0,))
    from_odd = sent(call(join_kernel, [vmem] * 2, [packed])(back_far, mate), "space", -2, (1,))
    base, curve = call(functools.partial(own_back_kernel, rows), [vmem] * 6, [field, ((rows, bs), F32)])(
        image, factor, back_own, curve, direction, terms
    )
    hess, partial = call(combine_kernel, [vmem] * 8, [field, sum_shape])(base, from_even, from_odd, mate, curve, *points)
    hess_sums, _ = total(partial, "space")
    whole = ((count + 1, blocks * bs), F32)
    scratch = [vmem(*whole)] * 3 + [pltpu.SemaphoreType.DMA((3 * OUT_PARTS,))]
    return call(finish_kernel, [vmem] * 9, [whole] * 3, scratch, keep=False)(
        *map(in_vmem, (sums, product, hess_sums, inner_inverse, direction, hess, terms, right_side, turned_map))
    )


def solution(mesh):
    return jax.shard_map(
        body,
        mesh=mesh,
        in_specs=(
            P(("groups", "space")),
            P(("groups", "space")),
            P(None, ("groups", "space")),
            P(("groups", "space")),
            P(("groups", "space"), None, None, None),
            P(("groups", "space"), None),
            P(("groups", "space"), None),
            P("groups", None),
        ),
        out_specs=(
            P(None, ("groups", "space")),
            P(None, ("groups", "space")),
            P(None, ("groups", "space")),
        ),
        check_vma=False,
    )
```

```python
import functools

import jax
import jax.numpy as jnp
from jax import lax
from jax.experimental import pallas as pl
from jax.experimental.pallas import tpu as pltpu
from jax.sharding import PartitionSpec as P

F32, BF16 = jnp.float32, jnp.bfloat16
PAIR = 2
MAP_PARTS = 4
OUT_PARTS = 4


def sent(block, axis, distance, parities=(0, 1)):
    devices = range(lax.axis_size(axis))
    return lax.ppermute(block, axis, [(i, i + distance) for i in devices if i % 2 in parities and i + distance in devices])


def swapped(block, axis):
    return lax.ppermute(block, axis, [(i, i ^ 1) for i in range(lax.axis_size(axis))])


def is_even(axis):
    return lax.rem(lax.axis_index(axis), 2) == 0


def write_message(msg_ref, x):
    top, half = x.shape[0] - 8, x.shape[1] // 2
    value, beside = x[top:, :half], x[top:, half:]
    high = value.astype(BF16).astype(F32)
    middle = (value - high).astype(BF16).astype(F32)
    low = value - high - middle
    row = lax.broadcasted_iota(jnp.int32, value.shape, 0)
    left = jnp.where(row < 4, high, pltpu.roll(low, 3, 0))
    right = jnp.where(row < 1, beside, middle)
    msg_ref[...] = jnp.concatenate([x[:top], jnp.concatenate([left, right], axis=1)], axis=0).astype(BF16)


def read_message(msg_ref):
    x = msg_ref[...].astype(F32)
    top, half = x.shape[0] - 8, x.shape[1] // 2
    left, right = x[top:, :half], x[top:, half:]
    row = lax.broadcasted_iota(jnp.int32, left.shape, 0)
    left = jnp.where(row < 1, left, left + right + pltpu.roll(left, 5, 0))
    return jnp.concatenate([x[:top], jnp.concatenate([left, right], axis=1)], axis=0)


def add_kernel(count, held, x_ref, *refs):
    in_refs, (out_ref, *msg_refs) = refs[: count - 1], refs[count - 1 + held :]
    x = x_ref[...]
    for ref in in_refs:
        x = x + (ref[...] if ref.dtype == F32 else read_message(ref))
    out_ref[...] = x
    for ref in msg_refs:
        write_message(ref, x)


def rounds_of(n):
    rounds = [(1,)] + [(3,)] * (n > 2)
    step = 4
    while step < n:
        rounds.append(tuple((m * step) ^ 1 for m in range(1, 4) if m * step < n))
        step *= 4
    return rounds


def total(x, axis, beside=()):
    n = lax.axis_size(axis)
    if n & (n - 1):
        return lax.psum(x, axis), [work(x) for work in beside]
    rounds = rounds_of(n)
    made, todo, msg = [], list(beside), x
    for i, partners in enumerate(rounds):
        got = [lax.ppermute(msg, axis, [(j, j ^ d) for j in range(n)]) for d in partners]
        last = i + 1 == len(rounds)
        held = ()
        while len(todo) >= max(len(rounds) - i, 1):
            made.append(todo.pop(0)(msg))
            held += made[-1]
        add = functools.partial(add_kernel, len(got) + 1, len(held))
        ins = [pltpu.VMEM] * (len(got) + 1) + [pl.ANY] * len(held)
        outs = [(x.shape, F32)] + [(x.shape, BF16)] * (not last)
        x, *rest = jax.tree.leaves(call(add, ins, outs)(x, *got, *held))
        msg = rest[0] if rest else None
    return x, made


def eye(rows, lanes):
    return lax.broadcasted_iota(jnp.int32, (rows, lanes), 0) == lax.broadcasted_iota(jnp.int32, (rows, lanes), 1)


def as_row(column, lanes):
    return jnp.sum(jnp.where(eye(column.shape[0], lanes), column, 0.0), axis=0, keepdims=True)


def as_column(row, rows):
    return jnp.sum(jnp.where(eye(rows, row.shape[1]), row, 0.0), axis=1, keepdims=True)


def project_kernel(
    latent_hbm, responses_hbm, prior_hbm, probes_hbm, map_hbm, out_ref, terms_ref, field_ref, map_ref, latent_ref,
    responses_ref, prior_ref, probes_ref, sems,
):
    blocks, bs = latent_ref.shape
    rows = out_ref.shape[0]
    count = probes_ref.shape[0]
    part = map_ref.shape[0] // MAP_PARTS
    cut = lambda ref, i: ref.at[i * part : (i + 1) * part]
    pairs = [(latent_hbm, latent_ref), (responses_hbm, responses_ref), (prior_hbm, prior_ref), (probes_hbm, probes_ref)]
    pairs += [(cut(map_hbm, i), cut(map_ref, i)) for i in range(MAP_PARTS)]
    copies = [pltpu.make_async_copy(a, b, sems.at[i]) for i, (a, b) in enumerate(pairs)]
    for copy in copies:
        copy.start()
    for copy in copies[:3]:
        copy.wait()
    probability = 1.0 / (1.0 + jnp.exp(-latent_ref[...]))
    weights = probability * (1.0 - probability)
    gradient = responses_ref[...].astype(F32) - probability
    inv_diag = 1.0 / (weights + prior_ref[...])
    terms_ref[0] = weights
    terms_ref[1] = inv_diag
    copies[3].wait()
    energy = jnp.zeros((rows, bs), F32)
    scaled = []
    for b in range(blocks):
        at = slice(b * bs, (b + 1) * bs)
        last = jnp.broadcast_to(gradient[b : b + 1], (rows - count, bs))
        field = pltpu.roll(jnp.concatenate([probes_ref[:, at], last], axis=0), 1, 0)
        field_ref[b] = field
        scaled.append(field * inv_diag[b : b + 1])
        energy += field * scaled[-1]
    summed = jnp.zeros(out_ref.shape, F32)
    for b in range(0, blocks, PAIR):
        if b * bs % part == 0:
            copies[4 + b * bs // part].wait()
        both = jnp.concatenate([scaled[b + i].astype(BF16) for i in range(PAIR)], axis=1)
        summed += jnp.dot(both, map_ref[b * bs : (b + PAIR) * bs], preferred_element_type=F32)
    out_ref[...] = summed
    out_ref[count + 1 : count + 2] = as_row(jnp.sum(energy, axis=1, keepdims=True), out_ref.shape[1])


def direction_kernel(sums_ref, inner_ref, terms_ref, field_ref, map_ref, dir_ref, msg_ref, product_ref, last_ref):
    blocks, _, bs = field_ref.shape
    count = msg_ref.shape[1]
    inv_diag_ref = terms_ref.at[1]
    product = jnp.dot(sums_ref[...], inner_ref[...], precision=lax.Precision.HIGH)
    product_ref[...] = product
    coeffs = product.astype(BF16)
    for b in range(0, blocks, PAIR):
        correction = jnp.dot(coeffs, map_ref[:, b * bs : (b + PAIR) * bs], preferred_element_type=F32)
        for c in range(b, b + PAIR):
            direction = (field_ref[c] + correction[:, (c - b) * bs : (c - b + 1) * bs]) * inv_diag_ref[c : c + 1]
            dir_ref[c] = direction
            msg_ref[c] = direction[:count].astype(BF16)
            last_ref[c : c + 1] = direction[count : count + 1]
    msg_ref[blocks] = last_ref[...].astype(BF16)


def turn_map_kernel(map_ref, after_ref, turned_ref):
    points, inducing = map_ref.shape
    for i in range(0, points, inducing):
        turned_ref[:, i : i + inducing] = map_ref[i : i + inducing].T


def load_kernel(factor_hbm, inner_hbm, after_ref, factor_ref, inner_ref, sems):
    copies = [
        pltpu.make_async_copy(factor_hbm, factor_ref, sems.at[0]),
        pltpu.make_async_copy(inner_hbm, inner_ref, sems.at[1]),
    ]
    for copy in copies:
        copy.start()
    for copy in copies:
        copy.wait()


def turn_kernel(factor_ref, after_ref, turned_ref):
    blocks, taps, bs, _ = factor_ref.shape
    for b in range(blocks):
        for k in range(1, taps):
            turned_ref[b, (k - 1) * bs : k * bs] = factor_ref[b, k].T


def tall_block(refs, lasts, at, tall):
    most = refs[at]
    last = jnp.broadcast_to(lasts[pl.ds(at, 1), :], (tall - most.shape[0], most.shape[1]))
    return jnp.concatenate([most, last.astype(BF16)], axis=0)


def own_image_kernel(tall, own_ref, factor_ref, image_ref, again_ref, zeros_ref, last_ref):
    blocks, bs = last_ref.shape
    again_ref[...] = own_ref[...]
    zeros_ref[...] = jnp.zeros_like(zeros_ref)
    last_ref[...] = own_ref[blocks].astype(F32)
    for b in range(blocks):
        image_ref[b] = lax.dot_general(
            tall_block(own_ref, last_ref, b, tall),
            factor_ref[b, 0],
            (((1,), (1,)), ((), ())),
            preferred_element_type=F32,
        )


def pass_on_kernel(own_ref, far_ref, after_ref, out_ref):
    @pl.when(is_even("space"))
    def _():
        out_ref[...] = own_ref[...]

    @pl.when(jnp.logical_not(is_even("space")))
    def _():
        out_ref[...] = far_ref[...]


def again_kernel(in_ref, after_ref, out_ref):
    out_ref[...] = in_ref[...]


def join_kernel(back_far_ref, got_ref, out_ref):
    out_ref[...] = (back_far_ref[...].astype(F32) + got_ref[...].astype(F32)).astype(BF16)


def own_back_kernel(
    rows, image_ref, factor_ref, total_ref, curve_ref, dir_ref, terms_ref, after_ref, base_ref, curve_out_ref
):
    blocks = factor_ref.shape[0]
    curve = curve_ref[...]
    for b in range(blocks):
        direction = dir_ref[b]
        weighted = terms_ref[0, b : b + 1] * direction
        curve += weighted * direction
        back = jnp.dot(image_ref[b], factor_ref[b, 0], preferred_element_type=F32)[:rows]
        base_ref[b] = total_ref[2 * blocks + b] + back + weighted
    curve_out_ref[...] = curve


def hessian_kernel(
    rows, ids_ref, factor_ref, turned_ref, own_image_ref, near_ref, far_even_ref, far_odd_ref, own_ref, zeros_ref,
    back_far_ref, back_near_ref, total_ref, curve_ref, image_ref, around_ref, around_last_ref, last_ref,
):
    blocks, taps, bs, _ = factor_ref.shape
    count = around_ref.shape[1]
    tall = image_ref.shape[1]
    for i, refs in enumerate(((far_even_ref, far_odd_ref), (near_ref,), (own_ref,))):
        at = slice(i * blocks, (i + 1) * blocks)
        around_ref[at] = functools.reduce(jnp.add, [ref[:blocks] for ref in refs])
        around_last_ref[at] = functools.reduce(jnp.add, [ref[blocks].astype(F32) for ref in refs])
    first = (lax.axis_index("space") - 2) * blocks
    curve = jnp.zeros((rows, bs), F32)
    ids = lambda b, k: ids_ref[k - 1, b] - first
    side_by_side = lambda b: jnp.concatenate([factor_ref[b, k] for k in range(1, taps)], axis=1)
    for b in range(blocks):
        chosen = [tall_block(around_ref, around_last_ref, ids(b, k), tall) for k in range(1, taps)]
        image = own_image_ref[b] + jnp.dot(
            jnp.concatenate(chosen, axis=1), turned_ref[b], preferred_element_type=F32
        )
        rounded = image.astype(BF16)
        image_ref[b] = rounded
        curve += (image * rounded.astype(F32))[:rows]
    curve_ref[...] = curve
    for b in range(blocks):
        back = jnp.dot(image_ref[b], side_by_side(b), preferred_element_type=F32)
        for k in range(1, taps):
            total_ref[ids(b, k)] += back[:rows, (k - 1) * bs : k * bs]
    for i, ref in enumerate((back_far_ref, back_near_ref)):
        for b in range(blocks):
            ref[b] = total_ref[i * blocks + b, :count].astype(BF16)
            last_ref[b : b + 1] = total_ref[i * blocks + b, count : count + 1]
        ref[blocks] = last_ref[...].astype(BF16)


def combine_kernel(
    base_ref, even_ref, odd_ref, mate_ref, curve_ref, terms_ref, field_ref, map_ref, hess_ref, out_ref
):
    blocks, rows, bs = field_ref.shape
    count = mate_ref.shape[1]
    inv_diag_ref = terms_ref.at[1]
    own_part = jnp.where(is_even("space"), 1.0, 0.0)
    arrived = lambda c: even_ref[c].astype(F32) + odd_ref[c].astype(F32) + own_part * mate_ref[c].astype(F32)
    from_last = arrived(blocks)
    cross = jnp.zeros((rows, bs), F32)
    square = jnp.zeros((rows, bs), F32)
    summed = jnp.zeros(out_ref.shape, F32)
    for b in range(0, blocks, PAIR):
        parts = []
        for c in range(b, b + PAIR):
            last = jnp.broadcast_to(from_last[c : c + 1], (rows - count, bs))
            hess = base_ref[c] + jnp.concatenate([arrived(c), last], axis=0)
            hess_ref[c] = hess
            scaled = hess * inv_diag_ref[c : c + 1]
            cross += field_ref[c] * scaled
            square += hess * scaled
            parts.append(scaled.astype(BF16))
        summed += jnp.dot(
            jnp.concatenate(parts, axis=1), map_ref[b * bs : (b + PAIR) * bs], preferred_element_type=F32
        )
    out_ref[...] = summed
    for i, acc in enumerate((curve_ref[...], cross, square)):
        out_ref[count + 1 + i : count + 2 + i] = as_row(jnp.sum(acc, axis=1, keepdims=True), out_ref.shape[1])


def finish_kernel(
    sums_ref, product_ref, hess_sums_ref, inner_ref, dir_ref, hess_ref, terms_ref, field_ref, map_ref, solution_hbm,
    residual_hbm, next_hbm, solution_ref, residual_ref, next_ref, sems,
):
    blocks, rows, bs = field_ref.shape
    whole = solution_ref.shape[0]
    inv_diag_ref = terms_ref.at[1]
    sums, product, hess_sums = sums_ref[...], product_ref[...], hess_sums_ref[...]
    column = lambda x, i: as_column(x[whole + i : whole + i + 1], rows)
    coeffs = product.astype(BF16)
    plain = column(sums, 0)
    energy = plain + jnp.sum(coeffs.astype(F32) * sums, axis=1, keepdims=True)
    step = energy / column(hess_sums, 0)
    left = sums - step * hess_sums
    hess_product = jnp.dot(hess_sums, inner_ref[...], precision=lax.Precision.HIGH)
    coeffs = (product - step * hess_product).astype(BF16)
    plain_next = plain - 2.0 * step * column(hess_sums, 1) + step * step * column(hess_sums, 2)
    energy_next = plain_next + jnp.sum(coeffs.astype(F32) * left, axis=1, keepdims=True)
    ratio = energy_next / energy
    part = blocks // OUT_PARTS
    copies = []

    def send(i, ref, hbm):
        at = pl.ds(i * part * bs, part * bs)
        copies.append(pltpu.make_async_copy(ref.at[:, at], hbm.at[:, at], sems.at[len(copies)]))
        copies[-1].start()

    residual_of = lambda c: field_ref[c] - step * hess_ref[c]
    for i in range(OUT_PARTS):
        for c in range(i * part, (i + 1) * part):
            at = slice(c * bs, (c + 1) * bs)
            solution_ref[:, at] = (step * dir_ref[c])[:whole]
            residual_ref[:, at] = residual_of(c)[:whole]
        send(i, solution_ref, solution_hbm)
        send(i, residual_ref, residual_hbm)
    for i in range(OUT_PARTS):
        for b in range(i * part, (i + 1) * part, PAIR):
            correction = jnp.dot(coeffs, map_ref[:, b * bs : (b + PAIR) * bs], preferred_element_type=F32)
            for c in range(b, b + PAIR):
                smoothed = (residual_of(c) + correction[:, (c - b) * bs : (c - b + 1) * bs]) * inv_diag_ref[c : c + 1]
                next_ref[:, c * bs : (c + 1) * bs] = (smoothed + ratio * dir_ref[c])[:whole]
        send(i, next_ref, next_hbm)
    for copy in copies:
        copy.wait()


def call(kernel, ins, outs, scratch=(), limit=16, keep=True, aliases={}):
    spec = lambda space: pl.BlockSpec(memory_space=space)
    shapes = tuple((pltpu.VMEM if keep else jax.ShapeDtypeStruct)(s, t) for s, t in outs)
    specs = (spec(pltpu.VMEM if keep else pl.ANY),) * len(shapes)
    return pl.pallas_call(
        kernel,
        out_shape=shapes if len(shapes) > 1 else shapes[0],
        in_specs=[spec(space) for space in ins],
        out_specs=specs if len(shapes) > 1 else specs[0],
        scratch_shapes=scratch,
        input_output_aliases=aliases,
        compiler_params=pltpu.CompilerParams(vmem_limit_bytes=limit * 1024 * 1024),
    )


def in_hbm(x):
    return pltpu.with_memory_space_constraint(x, pltpu.HBM)


def in_vmem(x):
    return pltpu.with_memory_space_constraint(x, pltpu.VMEM)


def body(latent, responses, probes, prior_diag, factor, cond_ids, inducing_map, inner_inverse):
    blocks, _, bs, _ = factor.shape
    count = probes.shape[0]
    rows, tall = count + 8, count + 16
    by_block = lambda x: x.reshape(blocks, bs)
    sum_shape = ((rows, inducing_map.shape[1]), F32)
    field = ((blocks, rows, bs), F32)
    packed = ((blocks + 1, count, bs), BF16)
    vmem, smem = pltpu.VMEM, pltpu.SMEM
    partial, terms, right_side, inducing_map = call(
        project_kernel,
        [pl.ANY] * 5,
        [sum_shape, ((2, blocks, bs), F32), field, (inducing_map.shape, BF16)],
        [
            vmem((blocks, bs), F32),
            vmem((blocks, bs), jnp.int32),
            vmem((blocks, bs), F32),
            vmem(probes.shape, F32),
            pltpu.SemaphoreType.DMA((4 + MAP_PARTS,)),
        ],
    )(*map(in_hbm, (by_block(latent), by_block(responses), by_block(prior_diag), probes, inducing_map)))
    points = (terms, right_side, inducing_map)

    def load(msg):
        outs = [(factor.shape, BF16), (inner_inverse.shape, F32)]
        return call(load_kernel, [pl.ANY] * 3, outs, [pltpu.SemaphoreType.DMA((2,))])(
            in_hbm(factor), in_hbm(inner_inverse), msg
        )

    def turn_map(msg):
        return (call(turn_map_kernel, [vmem, pl.ANY], [(inducing_map.shape[::-1], BF16)])(inducing_map, msg),)

    sums, ((turned_map,), (factor, inner_inverse)) = total(partial, "space", [turn_map, load])
    direction, rounded, product = call(
        direction_kernel, [vmem] * 5, [field, packed, sum_shape], [vmem((blocks, bs), F32)]
    )(sums, inner_inverse, terms, right_side, turned_map)
    far_odd = sent(rounded, "space", 2, (1,))
    around = ((3 * blocks, rows, bs), F32)
    own_image, again, zeros = call(
        functools.partial(own_image_kernel, tall),
        [vmem] * 2,
        [((blocks, tall, bs), F32), packed, around],
        [vmem((blocks, bs), F32)],
    )(rounded, factor)
    far_even = sent(again, "space", 2, (0,))
    shape = (blocks, (factor.shape[1] - 1) * bs, bs)
    turned = call(turn_kernel, [vmem, pl.ANY], [(shape, BF16)])(factor, own_image)
    near = swapped(call(pass_on_kernel, [vmem, vmem, pl.ANY], [packed])(rounded, far_odd, turned), "space")
    back_far, back_near, back_own, curve, image = call(
        functools.partial(hessian_kernel, rows),
        [smem] + [vmem] * 8,
        [packed, packed, around, ((rows, bs), F32), ((blocks, tall, bs), BF16)],
        [vmem((3 * blocks, count, bs), BF16), vmem((3 * blocks, bs), F32), vmem((blocks, bs), F32)],
        aliases={8: 2},
    )(cond_ids.T, factor, turned, own_image, near, far_even, far_odd, rounded, zeros)
    mate = swapped(back_near, "space")
    passing = sent(back_far, "space", -1, (0,))
    joined = call(join_kernel, [vmem] * 2, [packed])(back_far, mate)
    from_odd = sent(joined, "space", -2, (1,))
    base, curve = call(functools.partial(own_back_kernel, rows), [vmem] * 6 + [pl.ANY], [field, ((rows, bs), F32)])(
        image, factor, back_own, curve, direction, terms, joined
    )
    from_even = sent(call(again_kernel, [vmem, pl.ANY], [packed])(passing, curve), "space", -1, (1,))
    hess, partial = call(combine_kernel, [vmem] * 8, [field, sum_shape])(base, from_even, from_odd, mate, curve, *points)
    hess_sums, _ = total(partial, "space")
    whole = ((count + 1, blocks * bs), F32)
    scratch = [vmem(*whole)] * 3 + [pltpu.SemaphoreType.DMA((3 * OUT_PARTS,))]
    return call(finish_kernel, [vmem] * 9, [whole] * 3, scratch, keep=False)(
        *map(in_vmem, (sums, product, hess_sums, inner_inverse, direction, hess, terms, right_side, turned_map))
    )


def solution(mesh):
    return jax.shard_map(
        body,
        mesh=mesh,
        in_specs=(
            P(("groups", "space")),
            P(("groups", "space")),
            P(None, ("groups", "space")),
            P(("groups", "space")),
            P(("groups", "space"), None, None, None),
            P(("groups", "space"), None),
            P(("groups", "space"), None),
            P("groups", None),
        ),
        out_specs=(
            P(None, ("groups", "space")),
            P(None, ("groups", "space")),
            P(None, ("groups", "space")),
        ),
        check_vma=False,
    )
```

```python
import functools

import jax
import jax.numpy as jnp
from jax import lax
from jax.experimental import pallas as pl
from jax.experimental.pallas import tpu as pltpu
from jax.sharding import PartitionSpec as P

F32, BF16 = jnp.float32, jnp.bfloat16
PAIR = 2
MAP_PARTS = 4
OUT_PARTS = 4


def sent(block, axis, distance, parities=(0, 1)):
    devices = range(lax.axis_size(axis))
    return lax.ppermute(block, axis, [(i, i + distance) for i in devices if i % 2 in parities and i + distance in devices])


def swapped(block, axis):
    return lax.ppermute(block, axis, [(i, i ^ 1) for i in range(lax.axis_size(axis))])


def is_even(axis):
    return lax.rem(lax.axis_index(axis), 2) == 0


def write_message(msg_ref, x):
    top, half = x.shape[0] - 8, x.shape[1] // 2
    value, beside = x[top:, :half], x[top:, half:]
    high = value.astype(BF16).astype(F32)
    middle = (value - high).astype(BF16).astype(F32)
    low = value - high - middle
    row = lax.broadcasted_iota(jnp.int32, value.shape, 0)
    left = jnp.where(row < 4, high, pltpu.roll(low, 3, 0))
    right = jnp.where(row < 1, beside, middle)
    msg_ref[...] = jnp.concatenate([x[:top], jnp.concatenate([left, right], axis=1)], axis=0).astype(BF16)


def read_message(msg_ref):
    x = msg_ref[...].astype(F32)
    top, half = x.shape[0] - 8, x.shape[1] // 2
    left, right = x[top:, :half], x[top:, half:]
    row = lax.broadcasted_iota(jnp.int32, left.shape, 0)
    left = jnp.where(row < 1, left, left + right + pltpu.roll(left, 5, 0))
    return jnp.concatenate([x[:top], jnp.concatenate([left, right], axis=1)], axis=0)


def add_kernel(count, held, x_ref, *refs):
    in_refs, (out_ref, *msg_refs) = refs[: count - 1], refs[count - 1 + held :]
    x = x_ref[...]
    for ref in in_refs:
        x = x + (ref[...] if ref.dtype == F32 else read_message(ref))
    out_ref[...] = x
    for ref in msg_refs:
        write_message(ref, x)


def rounds_of(n):
    rounds = [(1,)] + [(3,)] * (n > 2)
    step = 4
    while step < n:
        rounds.append(tuple((m * step) ^ 1 for m in range(1, 4) if m * step < n))
        step *= 4
    return rounds


def total(x, axis, beside=()):
    n = lax.axis_size(axis)
    if n & (n - 1):
        return lax.psum(x, axis), [work(x) for work in beside]
    rounds = rounds_of(n)
    made, todo, msg = [], list(beside), x
    for i, partners in enumerate(rounds):
        got = [lax.ppermute(msg, axis, [(j, j ^ d) for j in range(n)]) for d in partners]
        last = i + 1 == len(rounds)
        held = ()
        while len(todo) >= max(len(rounds) - i, 1):
            made.append(todo.pop(0)(msg))
            held += made[-1]
        add = functools.partial(add_kernel, len(got) + 1, len(held))
        ins = [pltpu.VMEM] * (len(got) + 1) + [pl.ANY] * len(held)
        outs = [(x.shape, F32)] + [(x.shape, BF16)] * (not last)
        x, *rest = jax.tree.leaves(call(add, ins, outs)(x, *got, *held))
        msg = rest[0] if rest else None
    return x, made


def eye(rows, lanes):
    return lax.broadcasted_iota(jnp.int32, (rows, lanes), 0) == lax.broadcasted_iota(jnp.int32, (rows, lanes), 1)


def as_row(column, lanes):
    return jnp.sum(jnp.where(eye(column.shape[0], lanes), column, 0.0), axis=0, keepdims=True)


def as_column(row, rows):
    return jnp.sum(jnp.where(eye(rows, row.shape[1]), row, 0.0), axis=1, keepdims=True)


def project_kernel(
    latent_hbm, responses_hbm, prior_hbm, probes_hbm, map_hbm, out_ref, terms_ref, field_ref, map_ref, latent_ref,
    responses_ref, prior_ref, probes_ref, sems,
):
    blocks, bs = latent_ref.shape
    rows = out_ref.shape[0]
    count = probes_ref.shape[0]
    part = map_ref.shape[0] // MAP_PARTS
    cut = lambda ref, i: ref.at[i * part : (i + 1) * part]
    pairs = [(latent_hbm, latent_ref), (responses_hbm, responses_ref), (prior_hbm, prior_ref), (probes_hbm, probes_ref)]
    pairs += [(cut(map_hbm, i), cut(map_ref, i)) for i in range(MAP_PARTS)]
    copies = [pltpu.make_async_copy(a, b, sems.at[i]) for i, (a, b) in enumerate(pairs)]
    for copy in copies:
        copy.start()
    for copy in copies[:3]:
        copy.wait()
    probability = 1.0 / (1.0 + jnp.exp(-latent_ref[...]))
    weights = probability * (1.0 - probability)
    gradient = responses_ref[...].astype(F32) - probability
    inv_diag = 1.0 / (weights + prior_ref[...])
    terms_ref[0] = weights
    terms_ref[1] = inv_diag
    copies[3].wait()
    energy = jnp.zeros((rows, bs), F32)
    scaled = []
    for b in range(blocks):
        at = slice(b * bs, (b + 1) * bs)
        last = jnp.broadcast_to(gradient[b : b + 1], (rows - count, bs))
        field = pltpu.roll(jnp.concatenate([probes_ref[:, at], last], axis=0), 1, 0)
        field_ref[b] = field
        scaled.append(field * inv_diag[b : b + 1])
        energy += field * scaled[-1]
    summed = jnp.zeros(out_ref.shape, F32)
    for b in range(0, blocks, PAIR):
        if b * bs % part == 0:
            copies[4 + b * bs // part].wait()
        both = jnp.concatenate([scaled[b + i].astype(BF16) for i in range(PAIR)], axis=1)
        summed += jnp.dot(both, map_ref[b * bs : (b + PAIR) * bs], preferred_element_type=F32)
    out_ref[...] = summed
    out_ref[count + 1 : count + 2] = as_row(jnp.sum(energy, axis=1, keepdims=True), out_ref.shape[1])


def direction_kernel(sums_ref, inner_ref, terms_ref, field_ref, map_ref, dir_ref, msg_ref, product_ref, last_ref):
    blocks, _, bs = field_ref.shape
    count = msg_ref.shape[1]
    inv_diag_ref = terms_ref.at[1]
    product = jnp.dot(sums_ref[...], inner_ref[...], precision=lax.Precision.HIGH)
    product_ref[...] = product
    coeffs = product.astype(BF16)
    for b in range(0, blocks, PAIR):
        correction = jnp.dot(coeffs, map_ref[:, b * bs : (b + PAIR) * bs], preferred_element_type=F32)
        for c in range(b, b + PAIR):
            direction = (field_ref[c] + correction[:, (c - b) * bs : (c - b + 1) * bs]) * inv_diag_ref[c : c + 1]
            dir_ref[c] = direction
            msg_ref[c] = direction[:count].astype(BF16)
            last_ref[c : c + 1] = direction[count : count + 1]
    msg_ref[blocks] = last_ref[...].astype(BF16)


def turn_map_kernel(map_ref, after_ref, turned_ref):
    points, inducing = map_ref.shape
    for i in range(0, points, inducing):
        turned_ref[:, i : i + inducing] = map_ref[i : i + inducing].T


def load_kernel(factor_hbm, inner_hbm, after_ref, factor_ref, inner_ref, sems):
    copies = [
        pltpu.make_async_copy(factor_hbm, factor_ref, sems.at[0]),
        pltpu.make_async_copy(inner_hbm, inner_ref, sems.at[1]),
    ]
    for copy in copies:
        copy.start()
    for copy in copies:
        copy.wait()


def turn_kernel(factor_ref, ids_any, after_ref, turned_ref, ids_ref, sem):
    copy = pltpu.make_async_copy(ids_any, ids_ref, sem)
    copy.start()
    blocks, taps, bs, _ = factor_ref.shape
    for b in range(blocks):
        for k in range(1, taps):
            turned_ref[b, (k - 1) * bs : k * bs] = factor_ref[b, k].T
    copy.wait()


def tall_block(refs, lasts, at, tall):
    most = refs[at]
    last = jnp.broadcast_to(lasts[pl.ds(at, 1), :], (tall - most.shape[0], most.shape[1]))
    return jnp.concatenate([most, last.astype(BF16)], axis=0)


def own_image_kernel(tall, own_ref, factor_ref, image_ref, again_ref, zeros_ref, last_ref):
    blocks, bs = last_ref.shape
    again_ref[...] = own_ref[...]
    zeros_ref[...] = jnp.zeros_like(zeros_ref)
    last_ref[...] = own_ref[blocks].astype(F32)
    for b in range(blocks):
        image_ref[b] = lax.dot_general(
            tall_block(own_ref, last_ref, b, tall),
            factor_ref[b, 0],
            (((1,), (1,)), ((), ())),
            preferred_element_type=F32,
        )


def pass_on_kernel(own_ref, far_ref, after_ref, out_ref):
    @pl.when(is_even("space"))
    def _():
        out_ref[...] = own_ref[...]

    @pl.when(jnp.logical_not(is_even("space")))
    def _():
        out_ref[...] = far_ref[...]


def join_kernel(back_far_ref, got_ref, out_ref):
    out_ref[...] = (back_far_ref[...].astype(F32) + got_ref[...].astype(F32)).astype(BF16)


def own_back_kernel(rows, image_ref, factor_ref, total_ref, curve_ref, dir_ref, terms_ref, base_ref, curve_out_ref):
    blocks = factor_ref.shape[0]
    curve = curve_ref[...]
    for b in range(blocks):
        direction = dir_ref[b]
        weighted = terms_ref[0, b : b + 1] * direction
        curve += weighted * direction
        back = jnp.dot(image_ref[b], factor_ref[b, 0], preferred_element_type=F32)[:rows]
        base_ref[b] = total_ref[2 * blocks + b] + back + weighted
    curve_out_ref[...] = curve


def hessian_kernel(
    rows, ids_ref, factor_ref, turned_ref, own_image_ref, near_ref, far_even_ref, far_odd_ref, own_ref, zeros_ref,
    back_far_ref, back_near_ref, total_ref, curve_ref, image_ref, around_ref, around_last_ref, last_ref,
):
    blocks, taps, bs, _ = factor_ref.shape
    count = around_ref.shape[1]
    tall = image_ref.shape[1]
    for i, refs in enumerate(((far_even_ref, far_odd_ref), (near_ref,), (own_ref,))):
        at = slice(i * blocks, (i + 1) * blocks)
        around_ref[at] = functools.reduce(jnp.add, [ref[:blocks] for ref in refs])
        around_last_ref[at] = functools.reduce(jnp.add, [ref[blocks].astype(F32) for ref in refs])
    first = (lax.axis_index("space") - 2) * blocks
    curve = jnp.zeros((rows, bs), F32)
    ids = lambda b, k: ids_ref[k - 1, b] - first
    side_by_side = lambda b: jnp.concatenate([factor_ref[b, k] for k in range(1, taps)], axis=1)
    for b in range(blocks):
        chosen = [tall_block(around_ref, around_last_ref, ids(b, k), tall) for k in range(1, taps)]
        image = own_image_ref[b] + jnp.dot(
            jnp.concatenate(chosen, axis=1), turned_ref[b], preferred_element_type=F32
        )
        rounded = image.astype(BF16)
        image_ref[b] = rounded
        curve += (image * rounded.astype(F32))[:rows]
    curve_ref[...] = curve
    for b in range(blocks):
        back = jnp.dot(image_ref[b], side_by_side(b), preferred_element_type=F32)
        for k in range(1, taps):
            total_ref[ids(b, k)] += back[:rows, (k - 1) * bs : k * bs]
    for i, ref in enumerate((back_far_ref, back_near_ref)):
        for b in range(blocks):
            ref[b] = total_ref[i * blocks + b, :count].astype(BF16)
            last_ref[b : b + 1] = total_ref[i * blocks + b, count : count + 1]
        ref[blocks] = last_ref[...].astype(BF16)


def combine_kernel(
    base_ref, even_ref, odd_ref, mate_ref, curve_ref, terms_ref, field_ref, map_ref, hess_ref, out_ref
):
    blocks, rows, bs = field_ref.shape
    count = mate_ref.shape[1]
    inv_diag_ref = terms_ref.at[1]
    own_part = jnp.where(is_even("space"), 1.0, 0.0)
    arrived = lambda c: even_ref[c].astype(F32) + odd_ref[c].astype(F32) + own_part * mate_ref[c].astype(F32)
    from_last = arrived(blocks)
    cross = jnp.zeros((rows, bs), F32)
    square = jnp.zeros((rows, bs), F32)
    summed = jnp.zeros(out_ref.shape, F32)
    for b in range(0, blocks, PAIR):
        parts = []
        for c in range(b, b + PAIR):
            last = jnp.broadcast_to(from_last[c : c + 1], (rows - count, bs))
            hess = base_ref[c] + jnp.concatenate([arrived(c), last], axis=0)
            hess_ref[c] = hess
            scaled = hess * inv_diag_ref[c : c + 1]
            cross += field_ref[c] * scaled
            square += hess * scaled
            parts.append(scaled.astype(BF16))
        summed += jnp.dot(
            jnp.concatenate(parts, axis=1), map_ref[b * bs : (b + PAIR) * bs], preferred_element_type=F32
        )
    out_ref[...] = summed
    for i, acc in enumerate((curve_ref[...], cross, square)):
        out_ref[count + 1 + i : count + 2 + i] = as_row(jnp.sum(acc, axis=1, keepdims=True), out_ref.shape[1])


def finish_kernel(
    sums_ref, product_ref, hess_sums_ref, inner_ref, dir_ref, hess_ref, terms_ref, field_ref, map_ref, solution_hbm,
    residual_hbm, next_hbm, solution_ref, residual_ref, next_ref, sems,
):
    blocks, rows, bs = field_ref.shape
    whole = solution_ref.shape[0]
    inv_diag_ref = terms_ref.at[1]
    sums, product, hess_sums = sums_ref[...], product_ref[...], hess_sums_ref[...]
    column = lambda x, i: as_column(x[whole + i : whole + i + 1], rows)
    coeffs = product.astype(BF16)
    plain = column(sums, 0)
    energy = plain + jnp.sum(coeffs.astype(F32) * sums, axis=1, keepdims=True)
    step = energy / column(hess_sums, 0)
    left = sums - step * hess_sums
    hess_product = jnp.dot(hess_sums, inner_ref[...], precision=lax.Precision.HIGH)
    coeffs = (product - step * hess_product).astype(BF16)
    plain_next = plain - 2.0 * step * column(hess_sums, 1) + step * step * column(hess_sums, 2)
    energy_next = plain_next + jnp.sum(coeffs.astype(F32) * left, axis=1, keepdims=True)
    ratio = energy_next / energy
    part = blocks // OUT_PARTS
    copies = []

    def send(i, ref, hbm):
        at = pl.ds(i * part * bs, part * bs)
        copies.append(pltpu.make_async_copy(ref.at[:, at], hbm.at[:, at], sems.at[len(copies)]))
        copies[-1].start()

    residual_of = lambda c: field_ref[c] - step * hess_ref[c]
    for i in range(OUT_PARTS):
        for c in range(i * part, (i + 1) * part):
            at = slice(c * bs, (c + 1) * bs)
            solution_ref[:, at] = (step * dir_ref[c])[:whole]
            residual_ref[:, at] = residual_of(c)[:whole]
        send(i, solution_ref, solution_hbm)
        send(i, residual_ref, residual_hbm)
    for i in range(OUT_PARTS):
        for b in range(i * part, (i + 1) * part, PAIR):
            correction = jnp.dot(coeffs, map_ref[:, b * bs : (b + PAIR) * bs], preferred_element_type=F32)
            for c in range(b, b + PAIR):
                smoothed = (residual_of(c) + correction[:, (c - b) * bs : (c - b + 1) * bs]) * inv_diag_ref[c : c + 1]
                next_ref[:, c * bs : (c + 1) * bs] = (smoothed + ratio * dir_ref[c])[:whole]
        send(i, next_ref, next_hbm)
    for copy in copies:
        copy.wait()


def call(kernel, ins, outs, scratch=(), limit=16, keep=True, aliases={}, spaces=None):
    spec = lambda space: pl.BlockSpec(memory_space=space)
    spaces = spaces or (pltpu.VMEM,) * len(outs)
    shapes = tuple((space if keep else jax.ShapeDtypeStruct)(s, t) for space, (s, t) in zip(spaces, outs))
    specs = tuple(spec(space if keep else pl.ANY) for space in spaces)
    return pl.pallas_call(
        kernel,
        out_shape=shapes if len(shapes) > 1 else shapes[0],
        in_specs=[spec(space) for space in ins],
        out_specs=specs if len(shapes) > 1 else specs[0],
        scratch_shapes=scratch,
        input_output_aliases=aliases,
        compiler_params=pltpu.CompilerParams(vmem_limit_bytes=limit * 1024 * 1024),
    )


def in_hbm(x):
    return pltpu.with_memory_space_constraint(x, pltpu.HBM)


def in_vmem(x):
    return pltpu.with_memory_space_constraint(x, pltpu.VMEM)


def body(latent, responses, probes, prior_diag, factor, cond_ids, inducing_map, inner_inverse):
    blocks, _, bs, _ = factor.shape
    count = probes.shape[0]
    rows, tall = count + 8, count + 16
    by_block = lambda x: x.reshape(blocks, bs)
    sum_shape = ((rows, inducing_map.shape[1]), F32)
    field = ((blocks, rows, bs), F32)
    packed = ((blocks + 1, count, bs), BF16)
    vmem, smem = pltpu.VMEM, pltpu.SMEM
    partial, terms, right_side, inducing_map = call(
        project_kernel,
        [pl.ANY] * 5,
        [sum_shape, ((2, blocks, bs), F32), field, (inducing_map.shape, BF16)],
        [
            vmem((blocks, bs), F32),
            vmem((blocks, bs), jnp.int32),
            vmem((blocks, bs), F32),
            vmem(probes.shape, F32),
            pltpu.SemaphoreType.DMA((4 + MAP_PARTS,)),
        ],
    )(*map(in_hbm, (by_block(latent), by_block(responses), by_block(prior_diag), probes, inducing_map)))
    points = (terms, right_side, inducing_map)

    def load(msg):
        outs = [(factor.shape, BF16), (inner_inverse.shape, F32)]
        return call(load_kernel, [pl.ANY] * 3, outs, [pltpu.SemaphoreType.DMA((2,))])(
            in_hbm(factor), in_hbm(inner_inverse), msg
        )

    def turn_map(msg):
        return (call(turn_map_kernel, [vmem, pl.ANY], [(inducing_map.shape[::-1], BF16)])(inducing_map, msg),)

    sums, ((turned_map,), (factor, inner_inverse)) = total(partial, "space", [turn_map, load])
    direction, rounded, product = call(
        direction_kernel, [vmem] * 5, [field, packed, sum_shape], [vmem((blocks, bs), F32)]
    )(sums, inner_inverse, terms, right_side, turned_map)
    far_odd = sent(rounded, "space", 2, (1,))
    around = ((3 * blocks, rows, bs), F32)
    own_image, again, zeros = call(
        functools.partial(own_image_kernel, tall),
        [vmem] * 2,
        [((blocks, tall, bs), F32), packed, around],
        [vmem((blocks, bs), F32)],
    )(rounded, factor)
    far_even = sent(again, "space", 2, (0,))
    shape = (blocks, (factor.shape[1] - 1) * bs, bs)
    turned, ids = call(
        turn_kernel,
        [vmem, pl.ANY, pl.ANY],
        [(shape, BF16), (cond_ids.shape[::-1], jnp.int32)],
        [pltpu.SemaphoreType.DMA],
        spaces=(vmem, smem),
    )(factor, cond_ids.T, own_image)
    near = swapped(call(pass_on_kernel, [vmem, vmem, pl.ANY], [packed])(rounded, far_odd, turned), "space")
    back_far, back_near, back_own, curve, image = call(
        functools.partial(hessian_kernel, rows),
        [smem] + [vmem] * 8,
        [packed, packed, around, ((rows, bs), F32), ((blocks, tall, bs), BF16)],
        [vmem((3 * blocks, count, bs), BF16), vmem((3 * blocks, bs), F32), vmem((blocks, bs), F32)],
        aliases={8: 2},
    )(ids, factor, turned, own_image, near, far_even, far_odd, rounded, zeros)
    mate = swapped(back_near, "space")
    from_even = sent(back_far, "space", -2, (0,))
    from_odd = sent(call(join_kernel, [vmem] * 2, [packed])(back_far, mate), "space", -2, (1,))
    base, curve = call(functools.partial(own_back_kernel, rows), [vmem] * 6, [field, ((rows, bs), F32)])(
        image, factor, back_own, curve, direction, terms
    )
    hess, partial = call(combine_kernel, [vmem] * 8, [field, sum_shape])(base, from_even, from_odd, mate, curve, *points)
    hess_sums, _ = total(partial, "space")
    whole = ((count + 1, blocks * bs), F32)
    scratch = [vmem(*whole)] * 3 + [pltpu.SemaphoreType.DMA((3 * OUT_PARTS,))]
    return call(finish_kernel, [vmem] * 9, [whole] * 3, scratch, keep=False)(
        *map(in_vmem, (sums, product, hess_sums, inner_inverse, direction, hess, terms, right_side, turned_map))
    )


def solution(mesh):
    return jax.shard_map(
        body,
        mesh=mesh,
        in_specs=(
            P(("groups", "space")),
            P(("groups", "space")),
            P(None, ("groups", "space")),
            P(("groups", "space")),
            P(("groups", "space"), None, None, None),
            P(("groups", "space"), None),
            P(("groups", "space"), None),
            P("groups", None),
        ),
        out_specs=(
            P(None, ("groups", "space")),
            P(None, ("groups", "space")),
            P(None, ("groups", "space")),
        ),
        check_vma=False,
    )
```

```python
import functools

import jax
import jax.numpy as jnp
from jax import lax
from jax.experimental import pallas as pl
from jax.experimental.pallas import tpu as pltpu
from jax.sharding import PartitionSpec as P

F32, BF16 = jnp.float32, jnp.bfloat16
PAIR = 2
MAP_PARTS = 4
OUT_PARTS = 4


def sent(block, axis, distance, parities=(0, 1)):
    devices = range(lax.axis_size(axis))
    return lax.ppermute(block, axis, [(i, i + distance) for i in devices if i % 2 in parities and i + distance in devices])


def swapped(block, axis):
    return lax.ppermute(block, axis, [(i, i ^ 1) for i in range(lax.axis_size(axis))])


def is_even(axis):
    return lax.rem(lax.axis_index(axis), 2) == 0


def write_message(msg_ref, x):
    top, half = x.shape[0] - 8, x.shape[1] // 2
    value, beside = x[top:, :half], x[top:, half:]
    high = value.astype(BF16).astype(F32)
    middle = (value - high).astype(BF16).astype(F32)
    low = value - high - middle
    row = lax.broadcasted_iota(jnp.int32, value.shape, 0)
    left = jnp.where(row < 4, high, pltpu.roll(low, 3, 0))
    right = jnp.where(row < 1, beside, middle)
    msg_ref[...] = jnp.concatenate([x[:top], jnp.concatenate([left, right], axis=1)], axis=0).astype(BF16)


def read_message(msg_ref):
    x = msg_ref[...].astype(F32)
    top, half = x.shape[0] - 8, x.shape[1] // 2
    left, right = x[top:, :half], x[top:, half:]
    row = lax.broadcasted_iota(jnp.int32, left.shape, 0)
    left = jnp.where(row < 1, left, left + right + pltpu.roll(left, 5, 0))
    return jnp.concatenate([x[:top], jnp.concatenate([left, right], axis=1)], axis=0)


def add_kernel(count, held, x_ref, *refs):
    in_refs, (out_ref, *msg_refs) = refs[: count - 1], refs[count - 1 + held :]
    x = x_ref[...]
    for ref in in_refs:
        x = x + (ref[...] if ref.dtype == F32 else read_message(ref))
    out_ref[...] = x
    for ref in msg_refs:
        write_message(ref, x)


def rounds_of(n):
    rounds = [(1,)] + [(3,)] * (n > 2)
    step = 4
    while step < n:
        rounds.append(tuple((m * step) ^ 1 for m in range(1, 4) if m * step < n))
        step *= 4
    return rounds


def total(x, axis, beside=()):
    n = lax.axis_size(axis)
    if n & (n - 1):
        return lax.psum(x, axis), [work(x) for work in beside]
    rounds = rounds_of(n)
    made, todo, msg = [], list(beside), x
    for i, partners in enumerate(rounds):
        got = [lax.ppermute(msg, axis, [(j, j ^ d) for j in range(n)]) for d in partners]
        last = i + 1 == len(rounds)
        held = ()
        while len(todo) >= max(len(rounds) - i, 1):
            made.append(todo.pop(0)(msg))
            held += made[-1]
        add = functools.partial(add_kernel, len(got) + 1, len(held))
        ins = [pltpu.VMEM] * (len(got) + 1) + [pl.ANY] * len(held)
        outs = [(x.shape, F32)] + [(x.shape, BF16)] * (not last)
        x, *rest = jax.tree.leaves(call(add, ins, outs)(x, *got, *held))
        msg = rest[0] if rest else None
    return x, made


def eye(rows, lanes):
    return lax.broadcasted_iota(jnp.int32, (rows, lanes), 0) == lax.broadcasted_iota(jnp.int32, (rows, lanes), 1)


def as_row(column, lanes):
    return jnp.sum(jnp.where(eye(column.shape[0], lanes), column, 0.0), axis=0, keepdims=True)


def as_column(row, rows):
    return jnp.sum(jnp.where(eye(rows, row.shape[1]), row, 0.0), axis=1, keepdims=True)


def project_kernel(
    latent_hbm, responses_hbm, prior_hbm, probes_hbm, map_hbm, out_ref, terms_ref, field_ref, map_ref, latent_ref,
    responses_ref, prior_ref, probes_ref, sems,
):
    blocks, bs = latent_ref.shape
    rows = out_ref.shape[0]
    count = probes_ref.shape[0]
    part = map_ref.shape[0] // MAP_PARTS
    cut = lambda ref, i: ref.at[i * part : (i + 1) * part]
    pairs = [(latent_hbm, latent_ref), (responses_hbm, responses_ref), (prior_hbm, prior_ref), (probes_hbm, probes_ref)]
    pairs += [(cut(map_hbm, i), cut(map_ref, i)) for i in range(MAP_PARTS)]
    copies = [pltpu.make_async_copy(a, b, sems.at[i]) for i, (a, b) in enumerate(pairs)]
    for copy in copies:
        copy.start()
    for copy in copies[:3]:
        copy.wait()
    probability = 1.0 / (1.0 + jnp.exp(-latent_ref[...]))
    weights = probability * (1.0 - probability)
    gradient = responses_ref[...].astype(F32) - probability
    inv_diag = 1.0 / (weights + prior_ref[...])
    terms_ref[0] = weights
    terms_ref[1] = inv_diag
    copies[3].wait()
    energy = jnp.zeros((rows, bs), F32)
    scaled = []
    for b in range(blocks):
        at = slice(b * bs, (b + 1) * bs)
        last = jnp.broadcast_to(gradient[b : b + 1], (rows - count, bs))
        field = pltpu.roll(jnp.concatenate([probes_ref[:, at], last], axis=0), 1, 0)
        field_ref[b] = field
        scaled.append(field * inv_diag[b : b + 1])
        energy += field * scaled[-1]
    summed = jnp.zeros(out_ref.shape, F32)
    for b in range(0, blocks, PAIR):
        if b * bs % part == 0:
            copies[4 + b * bs // part].wait()
        both = jnp.concatenate([scaled[b + i].astype(BF16) for i in range(PAIR)], axis=1)
        summed += jnp.dot(both, map_ref[b * bs : (b + PAIR) * bs], preferred_element_type=F32)
    out_ref[...] = summed
    out_ref[count + 1 : count + 2] = as_row(jnp.sum(energy, axis=1, keepdims=True), out_ref.shape[1])


def direction_kernel(sums_ref, inner_ref, terms_ref, field_ref, map_ref, dir_ref, msg_ref, product_ref, last_ref):
    blocks, _, bs = field_ref.shape
    count = msg_ref.shape[1]
    inv_diag_ref = terms_ref.at[1]
    product = jnp.dot(sums_ref[...], inner_ref[...], precision=lax.Precision.HIGH)
    product_ref[...] = product
    coeffs = product.astype(BF16)
    for b in range(0, blocks, PAIR):
        correction = jnp.dot(coeffs, map_ref[:, b * bs : (b + PAIR) * bs], preferred_element_type=F32)
        for c in range(b, b + PAIR):
            direction = (field_ref[c] + correction[:, (c - b) * bs : (c - b + 1) * bs]) * inv_diag_ref[c : c + 1]
            dir_ref[c] = direction
            msg_ref[c] = direction[:count].astype(BF16)
            last_ref[c : c + 1] = direction[count : count + 1]
    msg_ref[blocks] = last_ref[...].astype(BF16)


def turn_map_kernel(map_ref, after_ref, turned_ref):
    points, inducing = map_ref.shape
    for i in range(0, points, inducing):
        turned_ref[:, i : i + inducing] = map_ref[i : i + inducing].T


def load_kernel(factor_hbm, inner_hbm, after_ref, factor_ref, inner_ref, sems):
    copies = [
        pltpu.make_async_copy(factor_hbm, factor_ref, sems.at[0]),
        pltpu.make_async_copy(inner_hbm, inner_ref, sems.at[1]),
    ]
    for copy in copies:
        copy.start()
    for copy in copies:
        copy.wait()


def turn_kernel(factor_ref, ids_any, after_ref, turned_ref, ids_ref, sem):
    copy = pltpu.make_async_copy(ids_any, ids_ref, sem)
    copy.start()
    blocks, taps, bs, _ = factor_ref.shape
    for b in range(blocks):
        for k in range(1, taps):
            turned_ref[b, (k - 1) * bs : k * bs] = factor_ref[b, k].T
    copy.wait()


def tall_block(refs, lasts, at, tall):
    most = refs[at]
    last = jnp.broadcast_to(lasts[pl.ds(at, 1), :], (tall - most.shape[0], most.shape[1]))
    return jnp.concatenate([most, last.astype(BF16)], axis=0)


def own_image_kernel(tall, own_ref, factor_ref, image_ref, zeros_ref, last_ref):
    blocks, bs = last_ref.shape
    zeros_ref[...] = jnp.zeros_like(zeros_ref)
    last_ref[...] = own_ref[blocks].astype(F32)
    for b in range(blocks):
        image_ref[b] = lax.dot_general(
            tall_block(own_ref, last_ref, b, tall),
            factor_ref[b, 0],
            (((1,), (1,)), ((), ())),
            preferred_element_type=F32,
        )


def pass_on_kernel(own_ref, far_ref, after_ref, out_ref):
    @pl.when(is_even("space"))
    def _():
        out_ref[...] = own_ref[...]

    @pl.when(jnp.logical_not(is_even("space")))
    def _():
        out_ref[...] = far_ref[...]


def join_kernel(back_far_ref, got_ref, out_ref):
    out_ref[...] = (back_far_ref[...].astype(F32) + got_ref[...].astype(F32)).astype(BF16)


def own_back_kernel(rows, image_ref, factor_ref, total_ref, curve_ref, dir_ref, terms_ref, base_ref, curve_out_ref):
    blocks = factor_ref.shape[0]
    curve = curve_ref[...]
    for b in range(blocks):
        direction = dir_ref[b]
        weighted = terms_ref[0, b : b + 1] * direction
        curve += weighted * direction
        back = jnp.dot(image_ref[b], factor_ref[b, 0], preferred_element_type=F32)[:rows]
        base_ref[b] = total_ref[2 * blocks + b] + back + weighted
    curve_out_ref[...] = curve


def hessian_kernel(
    rows, ids_ref, factor_ref, turned_ref, own_image_ref, near_ref, far_ref, own_ref, zeros_ref,
    back_far_ref, back_near_ref, total_ref, curve_ref, image_ref, around_ref, around_last_ref, last_ref,
):
    blocks, taps, bs, _ = factor_ref.shape
    count = around_ref.shape[1]
    tall = image_ref.shape[1]
    for i, ref in enumerate((far_ref, near_ref, own_ref)):
        at = slice(i * blocks, (i + 1) * blocks)
        around_ref[at] = ref[:blocks]
        around_last_ref[at] = ref[blocks].astype(F32)
    first = (lax.axis_index("space") - 2) * blocks
    curve = jnp.zeros((rows, bs), F32)
    ids = lambda b, k: ids_ref[k - 1, b] - first
    side_by_side = lambda b: jnp.concatenate([factor_ref[b, k] for k in range(1, taps)], axis=1)
    for b in range(blocks):
        chosen = [tall_block(around_ref, around_last_ref, ids(b, k), tall) for k in range(1, taps)]
        image = own_image_ref[b] + jnp.dot(
            jnp.concatenate(chosen, axis=1), turned_ref[b], preferred_element_type=F32
        )
        rounded = image.astype(BF16)
        image_ref[b] = rounded
        curve += (image * rounded.astype(F32))[:rows]
    curve_ref[...] = curve
    for b in range(blocks):
        back = jnp.dot(image_ref[b], side_by_side(b), preferred_element_type=F32)
        for k in range(1, taps):
            total_ref[ids(b, k)] += back[:rows, (k - 1) * bs : k * bs]
    for i, ref in enumerate((back_far_ref, back_near_ref)):
        for b in range(blocks):
            ref[b] = total_ref[i * blocks + b, :count].astype(BF16)
            last_ref[b : b + 1] = total_ref[i * blocks + b, count : count + 1]
        ref[blocks] = last_ref[...].astype(BF16)


def combine_kernel(
    base_ref, even_ref, odd_ref, mate_ref, curve_ref, terms_ref, field_ref, map_ref, hess_ref, out_ref
):
    blocks, rows, bs = field_ref.shape
    count = mate_ref.shape[1]
    inv_diag_ref = terms_ref.at[1]
    own_part = jnp.where(is_even("space"), 1.0, 0.0)
    arrived = lambda c: even_ref[c].astype(F32) + odd_ref[c].astype(F32) + own_part * mate_ref[c].astype(F32)
    from_last = arrived(blocks)
    cross = jnp.zeros((rows, bs), F32)
    square = jnp.zeros((rows, bs), F32)
    summed = jnp.zeros(out_ref.shape, F32)
    for b in range(0, blocks, PAIR):
        parts = []
        for c in range(b, b + PAIR):
            last = jnp.broadcast_to(from_last[c : c + 1], (rows - count, bs))
            hess = base_ref[c] + jnp.concatenate([arrived(c), last], axis=0)
            hess_ref[c] = hess
            scaled = hess * inv_diag_ref[c : c + 1]
            cross += field_ref[c] * scaled
            square += hess * scaled
            parts.append(scaled.astype(BF16))
        summed += jnp.dot(
            jnp.concatenate(parts, axis=1), map_ref[b * bs : (b + PAIR) * bs], preferred_element_type=F32
        )
    out_ref[...] = summed
    for i, acc in enumerate((curve_ref[...], cross, square)):
        out_ref[count + 1 + i : count + 2 + i] = as_row(jnp.sum(acc, axis=1, keepdims=True), out_ref.shape[1])


def finish_kernel(
    sums_ref, product_ref, hess_sums_ref, inner_ref, dir_ref, hess_ref, terms_ref, field_ref, map_ref, solution_hbm,
    residual_hbm, next_hbm, solution_ref, residual_ref, next_ref, sems,
):
    blocks, rows, bs = field_ref.shape
    whole = solution_ref.shape[0]
    inv_diag_ref = terms_ref.at[1]
    sums, product, hess_sums = sums_ref[...], product_ref[...], hess_sums_ref[...]
    column = lambda x, i: as_column(x[whole + i : whole + i + 1], rows)
    coeffs = product.astype(BF16)
    plain = column(sums, 0)
    energy = plain + jnp.sum(coeffs.astype(F32) * sums, axis=1, keepdims=True)
    step = energy / column(hess_sums, 0)
    left = sums - step * hess_sums
    hess_product = jnp.dot(hess_sums, inner_ref[...], precision=lax.Precision.HIGH)
    coeffs = (product - step * hess_product).astype(BF16)
    plain_next = plain - 2.0 * step * column(hess_sums, 1) + step * step * column(hess_sums, 2)
    energy_next = plain_next + jnp.sum(coeffs.astype(F32) * left, axis=1, keepdims=True)
    ratio = energy_next / energy
    part = blocks // OUT_PARTS
    copies = []

    def send(i, ref, hbm):
        at = pl.ds(i * part * bs, part * bs)
        copies.append(pltpu.make_async_copy(ref.at[:, at], hbm.at[:, at], sems.at[len(copies)]))
        copies[-1].start()

    residual_of = lambda c: field_ref[c] - step * hess_ref[c]
    for i in range(OUT_PARTS):
        for c in range(i * part, (i + 1) * part):
            at = slice(c * bs, (c + 1) * bs)
            solution_ref[:, at] = (step * dir_ref[c])[:whole]
            residual_ref[:, at] = residual_of(c)[:whole]
        send(i, solution_ref, solution_hbm)
        send(i, residual_ref, residual_hbm)
    for i in range(OUT_PARTS):
        for b in range(i * part, (i + 1) * part, PAIR):
            correction = jnp.dot(coeffs, map_ref[:, b * bs : (b + PAIR) * bs], preferred_element_type=F32)
            for c in range(b, b + PAIR):
                smoothed = (residual_of(c) + correction[:, (c - b) * bs : (c - b + 1) * bs]) * inv_diag_ref[c : c + 1]
                next_ref[:, c * bs : (c + 1) * bs] = (smoothed + ratio * dir_ref[c])[:whole]
        send(i, next_ref, next_hbm)
    for copy in copies:
        copy.wait()


def call(kernel, ins, outs, scratch=(), limit=16, keep=True, aliases={}, spaces=None):
    spec = lambda space: pl.BlockSpec(memory_space=space)
    spaces = spaces or (pltpu.VMEM,) * len(outs)
    shapes = tuple((space if keep else jax.ShapeDtypeStruct)(s, t) for space, (s, t) in zip(spaces, outs))
    specs = tuple(spec(space if keep else pl.ANY) for space in spaces)
    return pl.pallas_call(
        kernel,
        out_shape=shapes if len(shapes) > 1 else shapes[0],
        in_specs=[spec(space) for space in ins],
        out_specs=specs if len(shapes) > 1 else specs[0],
        scratch_shapes=scratch,
        input_output_aliases=aliases,
        compiler_params=pltpu.CompilerParams(vmem_limit_bytes=limit * 1024 * 1024),
    )


def in_hbm(x):
    return pltpu.with_memory_space_constraint(x, pltpu.HBM)


def in_vmem(x):
    return pltpu.with_memory_space_constraint(x, pltpu.VMEM)


def body(latent, responses, probes, prior_diag, factor, cond_ids, inducing_map, inner_inverse):
    blocks, _, bs, _ = factor.shape
    count = probes.shape[0]
    rows, tall = count + 8, count + 16
    by_block = lambda x: x.reshape(blocks, bs)
    sum_shape = ((rows, inducing_map.shape[1]), F32)
    field = ((blocks, rows, bs), F32)
    packed = ((blocks + 1, count, bs), BF16)
    vmem, smem = pltpu.VMEM, pltpu.SMEM
    partial, terms, right_side, inducing_map = call(
        project_kernel,
        [pl.ANY] * 5,
        [sum_shape, ((2, blocks, bs), F32), field, (inducing_map.shape, BF16)],
        [
            vmem((blocks, bs), F32),
            vmem((blocks, bs), jnp.int32),
            vmem((blocks, bs), F32),
            vmem(probes.shape, F32),
            pltpu.SemaphoreType.DMA((4 + MAP_PARTS,)),
        ],
    )(*map(in_hbm, (by_block(latent), by_block(responses), by_block(prior_diag), probes, inducing_map)))
    points = (terms, right_side, inducing_map)

    def load(msg):
        outs = [(factor.shape, BF16), (inner_inverse.shape, F32)]
        return call(load_kernel, [pl.ANY] * 3, outs, [pltpu.SemaphoreType.DMA((2,))])(
            in_hbm(factor), in_hbm(inner_inverse), msg
        )

    def turn_map(msg):
        return (call(turn_map_kernel, [vmem, pl.ANY], [(inducing_map.shape[::-1], BF16)])(inducing_map, msg),)

    sums, ((turned_map,), (factor, inner_inverse)) = total(partial, "space", [turn_map, load])
    direction, rounded, product = call(
        direction_kernel, [vmem] * 5, [field, packed, sum_shape], [vmem((blocks, bs), F32)]
    )(sums, inner_inverse, terms, right_side, turned_map)
    far = sent(rounded, "space", 2)
    around = ((3 * blocks, rows, bs), F32)
    own_image, zeros = call(
        functools.partial(own_image_kernel, tall),
        [vmem] * 2,
        [((blocks, tall, bs), F32), around],
        [vmem((blocks, bs), F32)],
    )(rounded, factor)
    shape = (blocks, (factor.shape[1] - 1) * bs, bs)
    turned, ids = call(
        turn_kernel,
        [vmem, pl.ANY, pl.ANY],
        [(shape, BF16), (cond_ids.shape[::-1], jnp.int32)],
        [pltpu.SemaphoreType.DMA],
        spaces=(vmem, smem),
    )(factor, cond_ids.T, own_image)
    near = swapped(call(pass_on_kernel, [vmem, vmem, pl.ANY], [packed])(rounded, far, turned), "space")
    back_far, back_near, back_own, curve, image = call(
        functools.partial(hessian_kernel, rows),
        [smem] + [vmem] * 7,
        [packed, packed, around, ((rows, bs), F32), ((blocks, tall, bs), BF16)],
        [vmem((3 * blocks, count, bs), BF16), vmem((3 * blocks, bs), F32), vmem((blocks, bs), F32)],
        aliases={7: 2},
    )(ids, factor, turned, own_image, near, far, rounded, zeros)
    mate = swapped(back_near, "space")
    from_even = sent(back_far, "space", -2, (0,))
    from_odd = sent(call(join_kernel, [vmem] * 2, [packed])(back_far, mate), "space", -2, (1,))
    base, curve = call(functools.partial(own_back_kernel, rows), [vmem] * 6, [field, ((rows, bs), F32)])(
        image, factor, back_own, curve, direction, terms
    )
    hess, partial = call(combine_kernel, [vmem] * 8, [field, sum_shape])(base, from_even, from_odd, mate, curve, *points)
    hess_sums, _ = total(partial, "space")
    whole = ((count + 1, blocks * bs), F32)
    scratch = [vmem(*whole)] * 3 + [pltpu.SemaphoreType.DMA((3 * OUT_PARTS,))]
    return call(finish_kernel, [vmem] * 9, [whole] * 3, scratch, keep=False)(
        *map(in_vmem, (sums, product, hess_sums, inner_inverse, direction, hess, terms, right_side, turned_map))
    )


def solution(mesh):
    return jax.shard_map(
        body,
        mesh=mesh,
        in_specs=(
            P(("groups", "space")),
            P(("groups", "space")),
            P(None, ("groups", "space")),
            P(("groups", "space")),
            P(("groups", "space"), None, None, None),
            P(("groups", "space"), None),
            P(("groups", "space"), None),
            P("groups", None),
        ),
        out_specs=(
            P(None, ("groups", "space")),
            P(None, ("groups", "space")),
            P(None, ("groups", "space")),
        ),
        check_vma=False,
    )
```

```python
import functools

import jax
import jax.numpy as jnp
from jax import lax
from jax.experimental import pallas as pl
from jax.experimental.pallas import tpu as pltpu
from jax.sharding import PartitionSpec as P

F32, BF16 = jnp.float32, jnp.bfloat16
PAIR = 2
MAP_PARTS = 4
OUT_PARTS = 4


def sent(block, axis, distance, parities=(0, 1)):
    devices = range(lax.axis_size(axis))
    return lax.ppermute(block, axis, [(i, i + distance) for i in devices if i % 2 in parities and i + distance in devices])


def swapped(block, axis):
    return lax.ppermute(block, axis, [(i, i ^ 1) for i in range(lax.axis_size(axis))])


def is_even(axis):
    return lax.rem(lax.axis_index(axis), 2) == 0


def write_message(msg_ref, x):
    top, half = x.shape[0] - 8, x.shape[1] // 2
    value, beside = x[top:, :half], x[top:, half:]
    high = value.astype(BF16).astype(F32)
    middle = (value - high).astype(BF16).astype(F32)
    low = value - high - middle
    row = lax.broadcasted_iota(jnp.int32, value.shape, 0)
    left = jnp.where(row < 4, high, pltpu.roll(low, 3, 0))
    right = jnp.where(row < 1, beside, middle)
    msg_ref[...] = jnp.concatenate([x[:top], jnp.concatenate([left, right], axis=1)], axis=0).astype(BF16)


def read_message(msg_ref):
    x = msg_ref[...].astype(F32)
    top, half = x.shape[0] - 8, x.shape[1] // 2
    left, right = x[top:, :half], x[top:, half:]
    row = lax.broadcasted_iota(jnp.int32, left.shape, 0)
    left = jnp.where(row < 1, left, left + right + pltpu.roll(left, 5, 0))
    return jnp.concatenate([x[:top], jnp.concatenate([left, right], axis=1)], axis=0)


def add_kernel(count, held, x_ref, *refs):
    in_refs, (out_ref, *msg_refs) = refs[: count - 1], refs[count - 1 + held :]
    x = x_ref[...]
    for ref in in_refs:
        x = x + (ref[...] if ref.dtype == F32 else read_message(ref))
    out_ref[...] = x
    for ref in msg_refs:
        write_message(ref, x)


def rounds_of(n):
    rounds = [(1,)] + [(3,)] * (n > 2)
    step = 4
    while step < n:
        rounds.append(tuple((m * step) ^ 1 for m in range(1, 4) if m * step < n))
        step *= 4
    return rounds


def total(x, axis, beside=()):
    n = lax.axis_size(axis)
    if n & (n - 1):
        return lax.psum(x, axis), [work(x) for work in beside]
    rounds = rounds_of(n)
    made, todo, msg = [], list(beside), x
    for i, partners in enumerate(rounds):
        got = [lax.ppermute(msg, axis, [(j, j ^ d) for j in range(n)]) for d in partners]
        last = i + 1 == len(rounds)
        held = ()
        while len(todo) >= max(len(rounds) - i, 1):
            made.append(todo.pop(0)(msg))
            held += made[-1]
        add = functools.partial(add_kernel, len(got) + 1, len(held))
        ins = [pltpu.VMEM] * (len(got) + 1) + [pl.ANY] * len(held)
        outs = [(x.shape, F32)] + [(x.shape, BF16)] * (not last)
        x, *rest = jax.tree.leaves(call(add, ins, outs)(x, *got, *held))
        msg = rest[0] if rest else None
    return x, made


def eye(rows, lanes):
    return lax.broadcasted_iota(jnp.int32, (rows, lanes), 0) == lax.broadcasted_iota(jnp.int32, (rows, lanes), 1)


def as_row(column, lanes):
    return jnp.sum(jnp.where(eye(column.shape[0], lanes), column, 0.0), axis=0, keepdims=True)


def as_column(row, rows):
    return jnp.sum(jnp.where(eye(rows, row.shape[1]), row, 0.0), axis=1, keepdims=True)


def project_kernel(
    latent_hbm, responses_hbm, prior_hbm, probes_hbm, map_hbm, out_ref, terms_ref, field_ref, map_ref, latent_ref,
    responses_ref, prior_ref, probes_ref, sems,
):
    blocks, bs = latent_ref.shape
    rows = out_ref.shape[0]
    count = probes_ref.shape[0]
    part = map_ref.shape[0] // MAP_PARTS
    cut = lambda ref, i: ref.at[i * part : (i + 1) * part]
    pairs = [(latent_hbm, latent_ref), (responses_hbm, responses_ref), (prior_hbm, prior_ref), (probes_hbm, probes_ref)]
    pairs += [(cut(map_hbm, i), cut(map_ref, i)) for i in range(MAP_PARTS)]
    copies = [pltpu.make_async_copy(a, b, sems.at[i]) for i, (a, b) in enumerate(pairs)]
    for copy in copies:
        copy.start()
    for copy in copies[:3]:
        copy.wait()
    probability = 1.0 / (1.0 + jnp.exp(-latent_ref[...]))
    weights = probability * (1.0 - probability)
    gradient = responses_ref[...].astype(F32) - probability
    inv_diag = 1.0 / (weights + prior_ref[...])
    terms_ref[0] = weights
    terms_ref[1] = inv_diag
    copies[3].wait()
    energy = jnp.zeros((rows, bs), F32)
    scaled = []
    for b in range(blocks):
        at = slice(b * bs, (b + 1) * bs)
        last = jnp.broadcast_to(gradient[b : b + 1], (rows - count, bs))
        field = pltpu.roll(jnp.concatenate([probes_ref[:, at], last], axis=0), 1, 0)
        field_ref[b] = field
        scaled.append(field * inv_diag[b : b + 1])
        energy += field * scaled[-1]
    summed = jnp.zeros(out_ref.shape, F32)
    for b in range(0, blocks, PAIR):
        if b * bs % part == 0:
            copies[4 + b * bs // part].wait()
        both = jnp.concatenate([scaled[b + i].astype(BF16) for i in range(PAIR)], axis=1)
        summed += jnp.dot(both, map_ref[b * bs : (b + PAIR) * bs], preferred_element_type=F32)
    out_ref[...] = summed
    out_ref[count + 1 : count + 2] = as_row(jnp.sum(energy, axis=1, keepdims=True), out_ref.shape[1])


def direction_kernel(sums_ref, inner_ref, terms_ref, field_ref, map_ref, dir_ref, msg_ref, product_ref, last_ref):
    blocks, _, bs = field_ref.shape
    count = msg_ref.shape[1]
    inv_diag_ref = terms_ref.at[1]
    product = jnp.dot(sums_ref[...], inner_ref[...], precision=lax.Precision.HIGH)
    product_ref[...] = product
    coeffs = product.astype(BF16)
    for b in range(0, blocks, PAIR):
        correction = jnp.dot(coeffs, map_ref[:, b * bs : (b + PAIR) * bs], preferred_element_type=F32)
        for c in range(b, b + PAIR):
            direction = (field_ref[c] + correction[:, (c - b) * bs : (c - b + 1) * bs]) * inv_diag_ref[c : c + 1]
            dir_ref[c] = direction
            msg_ref[c] = direction[:count].astype(BF16)
            last_ref[c : c + 1] = direction[count : count + 1]
    msg_ref[blocks] = last_ref[...].astype(BF16)


def turn_map_kernel(map_ref, after_ref, turned_ref):
    points, inducing = map_ref.shape
    for i in range(0, points, inducing):
        turned_ref[:, i : i + inducing] = map_ref[i : i + inducing].T


def load_kernel(factor_hbm, inner_hbm, after_ref, factor_ref, inner_ref, sems):
    copies = [
        pltpu.make_async_copy(factor_hbm, factor_ref, sems.at[0]),
        pltpu.make_async_copy(inner_hbm, inner_ref, sems.at[1]),
    ]
    for copy in copies:
        copy.start()
    for copy in copies:
        copy.wait()


def turn_kernel(factor_ref, ids_any, after_ref, turned_ref, ids_ref, sem):
    copy = pltpu.make_async_copy(ids_any, ids_ref, sem)
    copy.start()
    blocks, taps, bs, _ = factor_ref.shape
    for b in range(blocks):
        for k in range(1, taps):
            turned_ref[b, (k - 1) * bs : k * bs] = factor_ref[b, k].T
    copy.wait()


def tall_block(refs, lasts, at, tall):
    most = refs[at]
    last = jnp.broadcast_to(lasts[pl.ds(at, 1), :], (tall - most.shape[0], most.shape[1]))
    return jnp.concatenate([most, last.astype(BF16)], axis=0)


def own_image_kernel(tall, first, own_ref, factor_ref, *refs):
    image_ref, other_ref, last_ref = refs[-3:]
    blocks, bs = last_ref.shape
    other_ref[...] = jnp.zeros_like(other_ref) if first else own_ref[...]
    last_ref[...] = own_ref[blocks].astype(F32)
    for b in range(image_ref.shape[0]):
        image_ref[b] = lax.dot_general(
            tall_block(own_ref, last_ref, first + b, tall),
            factor_ref[first + b, 0],
            (((1,), (1,)), ((), ())),
            preferred_element_type=F32,
        )


def pass_on_kernel(own_ref, far_ref, after_ref, out_ref):
    @pl.when(is_even("space"))
    def _():
        out_ref[...] = own_ref[...]

    @pl.when(jnp.logical_not(is_even("space")))
    def _():
        out_ref[...] = far_ref[...]


def join_kernel(back_far_ref, got_ref, out_ref):
    out_ref[...] = (back_far_ref[...].astype(F32) + got_ref[...].astype(F32)).astype(BF16)


def own_back_kernel(rows, image_ref, factor_ref, total_ref, curve_ref, dir_ref, terms_ref, base_ref, curve_out_ref):
    blocks = factor_ref.shape[0]
    curve = curve_ref[...]
    for b in range(blocks):
        direction = dir_ref[b]
        weighted = terms_ref[0, b : b + 1] * direction
        curve += weighted * direction
        back = jnp.dot(image_ref[b], factor_ref[b, 0], preferred_element_type=F32)[:rows]
        base_ref[b] = total_ref[2 * blocks + b] + back + weighted
    curve_out_ref[...] = curve


def hessian_kernel(
    rows, ids_ref, factor_ref, turned_ref, image_one_ref, image_two_ref, near_ref, far_even_ref, far_odd_ref, own_ref,
    zeros_ref, back_far_ref, back_near_ref, total_ref, curve_ref, image_ref, around_ref, around_last_ref, last_ref,
):
    blocks, taps, bs, _ = factor_ref.shape
    count = around_ref.shape[1]
    tall = image_ref.shape[1]
    for i, refs in enumerate(((far_even_ref, far_odd_ref), (near_ref,), (own_ref,))):
        at = slice(i * blocks, (i + 1) * blocks)
        around_ref[at] = functools.reduce(jnp.add, [ref[:blocks] for ref in refs])
        around_last_ref[at] = functools.reduce(jnp.add, [ref[blocks].astype(F32) for ref in refs])
    first = (lax.axis_index("space") - 2) * blocks
    curve = jnp.zeros((rows, bs), F32)
    ids = lambda b, k: ids_ref[k - 1, b] - first
    side_by_side = lambda b: jnp.concatenate([factor_ref[b, k] for k in range(1, taps)], axis=1)
    for b in range(blocks):
        chosen = [tall_block(around_ref, around_last_ref, ids(b, k), tall) for k in range(1, taps)]
        half = image_one_ref.shape[0]
        own_image = image_one_ref[b] if b < half else image_two_ref[b - half]
        image = own_image + jnp.dot(
            jnp.concatenate(chosen, axis=1), turned_ref[b], preferred_element_type=F32
        )
        rounded = image.astype(BF16)
        image_ref[b] = rounded
        curve += (image * rounded.astype(F32))[:rows]
    curve_ref[...] = curve
    for b in range(blocks):
        back = jnp.dot(image_ref[b], side_by_side(b), preferred_element_type=F32)
        for k in range(1, taps):
            total_ref[ids(b, k)] += back[:rows, (k - 1) * bs : k * bs]
    for i, ref in enumerate((back_far_ref, back_near_ref)):
        for b in range(blocks):
            ref[b] = total_ref[i * blocks + b, :count].astype(BF16)
            last_ref[b : b + 1] = total_ref[i * blocks + b, count : count + 1]
        ref[blocks] = last_ref[...].astype(BF16)


def combine_kernel(
    base_ref, even_ref, odd_ref, mate_ref, curve_ref, terms_ref, field_ref, map_ref, hess_ref, out_ref
):
    blocks, rows, bs = field_ref.shape
    count = mate_ref.shape[1]
    inv_diag_ref = terms_ref.at[1]
    own_part = jnp.where(is_even("space"), 1.0, 0.0)
    arrived = lambda c: even_ref[c].astype(F32) + odd_ref[c].astype(F32) + own_part * mate_ref[c].astype(F32)
    from_last = arrived(blocks)
    cross = jnp.zeros((rows, bs), F32)
    square = jnp.zeros((rows, bs), F32)
    summed = jnp.zeros(out_ref.shape, F32)
    for b in range(0, blocks, PAIR):
        parts = []
        for c in range(b, b + PAIR):
            last = jnp.broadcast_to(from_last[c : c + 1], (rows - count, bs))
            hess = base_ref[c] + jnp.concatenate([arrived(c), last], axis=0)
            hess_ref[c] = hess
            scaled = hess * inv_diag_ref[c : c + 1]
            cross += field_ref[c] * scaled
            square += hess * scaled
            parts.append(scaled.astype(BF16))
        summed += jnp.dot(
            jnp.concatenate(parts, axis=1), map_ref[b * bs : (b + PAIR) * bs], preferred_element_type=F32
        )
    out_ref[...] = summed
    for i, acc in enumerate((curve_ref[...], cross, square)):
        out_ref[count + 1 + i : count + 2 + i] = as_row(jnp.sum(acc, axis=1, keepdims=True), out_ref.shape[1])


def finish_kernel(
    sums_ref, product_ref, hess_sums_ref, inner_ref, dir_ref, hess_ref, terms_ref, field_ref, map_ref, solution_hbm,
    residual_hbm, next_hbm, solution_ref, residual_ref, next_ref, sems,
):
    blocks, rows, bs = field_ref.shape
    whole = solution_ref.shape[0]
    inv_diag_ref = terms_ref.at[1]
    sums, product, hess_sums = sums_ref[...], product_ref[...], hess_sums_ref[...]
    column = lambda x, i: as_column(x[whole + i : whole + i + 1], rows)
    coeffs = product.astype(BF16)
    plain = column(sums, 0)
    energy = plain + jnp.sum(coeffs.astype(F32) * sums, axis=1, keepdims=True)
    step = energy / column(hess_sums, 0)
    left = sums - step * hess_sums
    hess_product = jnp.dot(hess_sums, inner_ref[...], precision=lax.Precision.HIGH)
    coeffs = (product - step * hess_product).astype(BF16)
    plain_next = plain - 2.0 * step * column(hess_sums, 1) + step * step * column(hess_sums, 2)
    energy_next = plain_next + jnp.sum(coeffs.astype(F32) * left, axis=1, keepdims=True)
    ratio = energy_next / energy
    part = blocks // OUT_PARTS
    copies = []

    def send(i, ref, hbm):
        at = pl.ds(i * part * bs, part * bs)
        copies.append(pltpu.make_async_copy(ref.at[:, at], hbm.at[:, at], sems.at[len(copies)]))
        copies[-1].start()

    residual_of = lambda c: field_ref[c] - step * hess_ref[c]
    for i in range(OUT_PARTS):
        for c in range(i * part, (i + 1) * part):
            at = slice(c * bs, (c + 1) * bs)
            solution_ref[:, at] = (step * dir_ref[c])[:whole]
            residual_ref[:, at] = residual_of(c)[:whole]
        send(i, solution_ref, solution_hbm)
        send(i, residual_ref, residual_hbm)
    for i in range(OUT_PARTS):
        for b in range(i * part, (i + 1) * part, PAIR):
            correction = jnp.dot(coeffs, map_ref[:, b * bs : (b + PAIR) * bs], preferred_element_type=F32)
            for c in range(b, b + PAIR):
                smoothed = (residual_of(c) + correction[:, (c - b) * bs : (c - b + 1) * bs]) * inv_diag_ref[c : c + 1]
                next_ref[:, c * bs : (c + 1) * bs] = (smoothed + ratio * dir_ref[c])[:whole]
        send(i, next_ref, next_hbm)
    for copy in copies:
        copy.wait()


def call(kernel, ins, outs, scratch=(), limit=16, keep=True, aliases={}, spaces=None):
    spec = lambda space: pl.BlockSpec(memory_space=space)
    spaces = spaces or (pltpu.VMEM,) * len(outs)
    shapes = tuple((space if keep else jax.ShapeDtypeStruct)(s, t) for space, (s, t) in zip(spaces, outs))
    specs = tuple(spec(space if keep else pl.ANY) for space in spaces)
    return pl.pallas_call(
        kernel,
        out_shape=shapes if len(shapes) > 1 else shapes[0],
        in_specs=[spec(space) for space in ins],
        out_specs=specs if len(shapes) > 1 else specs[0],
        scratch_shapes=scratch,
        input_output_aliases=aliases,
        compiler_params=pltpu.CompilerParams(vmem_limit_bytes=limit * 1024 * 1024),
    )


def in_hbm(x):
    return pltpu.with_memory_space_constraint(x, pltpu.HBM)


def in_vmem(x):
    return pltpu.with_memory_space_constraint(x, pltpu.VMEM)


def body(latent, responses, probes, prior_diag, factor, cond_ids, inducing_map, inner_inverse):
    blocks, _, bs, _ = factor.shape
    count = probes.shape[0]
    rows, tall = count + 8, count + 16
    by_block = lambda x: x.reshape(blocks, bs)
    sum_shape = ((rows, inducing_map.shape[1]), F32)
    field = ((blocks, rows, bs), F32)
    packed = ((blocks + 1, count, bs), BF16)
    vmem, smem = pltpu.VMEM, pltpu.SMEM
    partial, terms, right_side, inducing_map = call(
        project_kernel,
        [pl.ANY] * 5,
        [sum_shape, ((2, blocks, bs), F32), field, (inducing_map.shape, BF16)],
        [
            vmem((blocks, bs), F32),
            vmem((blocks, bs), jnp.int32),
            vmem((blocks, bs), F32),
            vmem(probes.shape, F32),
            pltpu.SemaphoreType.DMA((4 + MAP_PARTS,)),
        ],
    )(*map(in_hbm, (by_block(latent), by_block(responses), by_block(prior_diag), probes, inducing_map)))
    points = (terms, right_side, inducing_map)

    def load(msg):
        outs = [(factor.shape, BF16), (inner_inverse.shape, F32)]
        return call(load_kernel, [pl.ANY] * 3, outs, [pltpu.SemaphoreType.DMA((2,))])(
            in_hbm(factor), in_hbm(inner_inverse), msg
        )

    def turn_map(msg):
        return (call(turn_map_kernel, [vmem, pl.ANY], [(inducing_map.shape[::-1], BF16)])(inducing_map, msg),)

    sums, ((turned_map,), (factor, inner_inverse)) = total(partial, "space", [turn_map, load])
    direction, rounded, product = call(
        direction_kernel, [vmem] * 5, [field, packed, sum_shape], [vmem((blocks, bs), F32)]
    )(sums, inner_inverse, terms, right_side, turned_map)
    far_odd = sent(rounded, "space", 2, (1,))
    around = ((3 * blocks, rows, bs), F32)
    half = blocks // 2

    def own_image(first, other, *after):
        count = blocks - half if first else half
        return call(
            functools.partial(own_image_kernel, tall, first),
            [vmem] * 2 + [pl.ANY] * len(after),
            [((count, tall, bs), F32), other],
            [vmem((blocks, bs), F32)],
        )(rounded, factor, *after)

    image_one, again = own_image(0, packed)
    far_even = sent(again, "space", 2, (0,))
    image_two, zeros = own_image(half, around, image_one)
    shape = (blocks, (factor.shape[1] - 1) * bs, bs)
    turned, ids = call(
        turn_kernel,
        [vmem, pl.ANY, pl.ANY],
        [(shape, BF16), (cond_ids.shape[::-1], jnp.int32)],
        [pltpu.SemaphoreType.DMA],
        spaces=(vmem, smem),
    )(factor, cond_ids.T, image_two)
    near = swapped(call(pass_on_kernel, [vmem, vmem, pl.ANY], [packed])(rounded, far_odd, turned), "space")
    back_far, back_near, back_own, curve, image = call(
        functools.partial(hessian_kernel, rows),
        [smem] + [vmem] * 9,
        [packed, packed, around, ((rows, bs), F32), ((blocks, tall, bs), BF16)],
        [vmem((3 * blocks, count, bs), BF16), vmem((3 * blocks, bs), F32), vmem((blocks, bs), F32)],
        aliases={9: 2},
    )(ids, factor, turned, image_one, image_two, near, far_even, far_odd, rounded, zeros)
    mate = swapped(back_near, "space")
    from_even = sent(back_far, "space", -2, (0,))
    from_odd = sent(call(join_kernel, [vmem] * 2, [packed])(back_far, mate), "space", -2, (1,))
    base, curve = call(functools.partial(own_back_kernel, rows), [vmem] * 6, [field, ((rows, bs), F32)])(
        image, factor, back_own, curve, direction, terms
    )
    hess, partial = call(combine_kernel, [vmem] * 8, [field, sum_shape])(base, from_even, from_odd, mate, curve, *points)
    hess_sums, _ = total(partial, "space")
    whole = ((count + 1, blocks * bs), F32)
    scratch = [vmem(*whole)] * 3 + [pltpu.SemaphoreType.DMA((3 * OUT_PARTS,))]
    return call(finish_kernel, [vmem] * 9, [whole] * 3, scratch, keep=False)(
        *map(in_vmem, (sums, product, hess_sums, inner_inverse, direction, hess, terms, right_side, turned_map))
    )


def solution(mesh):
    return jax.shard_map(
        body,
        mesh=mesh,
        in_specs=(
            P(("groups", "space")),
            P(("groups", "space")),
            P(None, ("groups", "space")),
            P(("groups", "space")),
            P(("groups", "space"), None, None, None),
            P(("groups", "space"), None),
            P(("groups", "space"), None),
            P("groups", None),
        ),
        out_specs=(
            P(None, ("groups", "space")),
            P(None, ("groups", "space")),
            P(None, ("groups", "space")),
        ),
        check_vma=False,
    )
```

```python
import functools

import jax
import jax.numpy as jnp
from jax import lax
from jax.experimental import pallas as pl
from jax.experimental.pallas import tpu as pltpu
from jax.sharding import PartitionSpec as P

F32, BF16 = jnp.float32, jnp.bfloat16
PAIR = 2
MAP_PARTS = 4
OUT_PARTS = 4


def sent(block, axis, distance, parities=(0, 1)):
    devices = range(lax.axis_size(axis))
    return lax.ppermute(block, axis, [(i, i + distance) for i in devices if i % 2 in parities and i + distance in devices])


def swapped(block, axis):
    return lax.ppermute(block, axis, [(i, i ^ 1) for i in range(lax.axis_size(axis))])


def is_even(axis):
    return lax.rem(lax.axis_index(axis), 2) == 0


def add_kernel(count, held, x_ref, *refs):
    in_refs, out_ref = refs[: count - 1], refs[count - 1 + held]
    x = x_ref[...]
    for ref in in_refs:
        x = x + ref[...]
    out_ref[...] = x


def rounds_of(n):
    rounds = [(1,)] + [(3,)] * (n > 2)
    step = 4
    while step < n:
        rounds.append(tuple((m * step) ^ 1 for m in range(1, 4) if m * step < n))
        step *= 4
    return rounds


def total(x, axis, beside=()):
    n = lax.axis_size(axis)
    if n & (n - 1):
        return lax.psum(x, axis), [work(x) for work in beside]
    rounds = rounds_of(n)
    made, todo = [], list(beside)
    for i, partners in enumerate(rounds):
        got = [lax.ppermute(x, axis, [(j, j ^ d) for j in range(n)]) for d in partners]
        held = ()
        while len(todo) >= max(len(rounds) - i, 1):
            made.append(todo.pop(0)(x))
            held += made[-1]
        add = functools.partial(add_kernel, len(got) + 1, len(held))
        ins = [pltpu.VMEM] * (len(got) + 1) + [pl.ANY] * len(held)
        x = call(add, ins, [(x.shape, F32)])(x, *got, *held)
    return x, made


def eye(rows, lanes):
    return lax.broadcasted_iota(jnp.int32, (rows, lanes), 0) == lax.broadcasted_iota(jnp.int32, (rows, lanes), 1)


def as_row(column, lanes):
    return jnp.sum(jnp.where(eye(column.shape[0], lanes), column, 0.0), axis=0, keepdims=True)


def as_column(row, rows):
    return jnp.sum(jnp.where(eye(rows, row.shape[1]), row, 0.0), axis=1, keepdims=True)


def project_kernel(
    latent_hbm, responses_hbm, prior_hbm, probes_hbm, map_hbm, out_ref, terms_ref, field_ref, map_ref, latent_ref,
    responses_ref, prior_ref, probes_ref, sems,
):
    blocks, bs = latent_ref.shape
    rows = out_ref.shape[0]
    count = probes_ref.shape[0]
    part = map_ref.shape[0] // MAP_PARTS
    cut = lambda ref, i: ref.at[i * part : (i + 1) * part]
    pairs = [(latent_hbm, latent_ref), (responses_hbm, responses_ref), (prior_hbm, prior_ref), (probes_hbm, probes_ref)]
    pairs += [(cut(map_hbm, i), cut(map_ref, i)) for i in range(MAP_PARTS)]
    copies = [pltpu.make_async_copy(a, b, sems.at[i]) for i, (a, b) in enumerate(pairs)]
    for copy in copies:
        copy.start()
    for copy in copies[:3]:
        copy.wait()
    probability = 1.0 / (1.0 + jnp.exp(-latent_ref[...]))
    weights = probability * (1.0 - probability)
    gradient = responses_ref[...].astype(F32) - probability
    inv_diag = 1.0 / (weights + prior_ref[...])
    terms_ref[0] = weights
    terms_ref[1] = inv_diag
    copies[3].wait()
    energy = jnp.zeros((rows, bs), F32)
    scaled = []
    for b in range(blocks):
        at = slice(b * bs, (b + 1) * bs)
        last = jnp.broadcast_to(gradient[b : b + 1], (rows - count, bs))
        field = pltpu.roll(jnp.concatenate([probes_ref[:, at], last], axis=0), 1, 0)
        field_ref[b] = field
        scaled.append(field * inv_diag[b : b + 1])
        energy += field * scaled[-1]
    summed = jnp.zeros(out_ref.shape, F32)
    for b in range(0, blocks, PAIR):
        if b * bs % part == 0:
            copies[4 + b * bs // part].wait()
        both = jnp.concatenate([scaled[b + i].astype(BF16) for i in range(PAIR)], axis=1)
        summed += jnp.dot(both, map_ref[b * bs : (b + PAIR) * bs], preferred_element_type=F32)
    out_ref[...] = summed
    out_ref[count + 1 : count + 2] = as_row(jnp.sum(energy, axis=1, keepdims=True), out_ref.shape[1])


def direction_kernel(sums_ref, inner_ref, terms_ref, field_ref, map_ref, dir_ref, msg_ref, product_ref, last_ref):
    blocks, _, bs = field_ref.shape
    count = msg_ref.shape[1]
    inv_diag_ref = terms_ref.at[1]
    product = jnp.dot(sums_ref[...], inner_ref[...], precision=lax.Precision.HIGH)
    product_ref[...] = product
    coeffs = product.astype(BF16)
    for b in range(0, blocks, PAIR):
        correction = jnp.dot(coeffs, map_ref[:, b * bs : (b + PAIR) * bs], preferred_element_type=F32)
        for c in range(b, b + PAIR):
            direction = (field_ref[c] + correction[:, (c - b) * bs : (c - b + 1) * bs]) * inv_diag_ref[c : c + 1]
            dir_ref[c] = direction
            msg_ref[c] = direction[:count].astype(BF16)
            last_ref[c : c + 1] = direction[count : count + 1]
    msg_ref[blocks] = last_ref[...].astype(BF16)


def turn_map_kernel(map_ref, after_ref, turned_ref):
    points, inducing = map_ref.shape
    for i in range(0, points, inducing):
        turned_ref[:, i : i + inducing] = map_ref[i : i + inducing].T


def load_kernel(factor_hbm, inner_hbm, after_ref, factor_ref, inner_ref, sems):
    copies = [
        pltpu.make_async_copy(factor_hbm, factor_ref, sems.at[0]),
        pltpu.make_async_copy(inner_hbm, inner_ref, sems.at[1]),
    ]
    for copy in copies:
        copy.start()
    for copy in copies:
        copy.wait()


def turn_kernel(factor_ref, ids_any, after_ref, turned_ref, ids_ref, sem):
    copy = pltpu.make_async_copy(ids_any, ids_ref, sem)
    copy.start()
    blocks, taps, bs, _ = factor_ref.shape
    for b in range(blocks):
        for k in range(1, taps):
            turned_ref[b, (k - 1) * bs : k * bs] = factor_ref[b, k].T
    copy.wait()


def tall_block(refs, lasts, at, tall):
    most = refs[at]
    last = jnp.broadcast_to(lasts[pl.ds(at, 1), :], (tall - most.shape[0], most.shape[1]))
    return jnp.concatenate([most, last.astype(BF16)], axis=0)


def own_image_kernel(tall, first, own_ref, factor_ref, *refs):
    image_ref, other_ref, last_ref = refs[-3:]
    blocks, bs = last_ref.shape
    other_ref[...] = jnp.zeros_like(other_ref) if first else own_ref[...]
    last_ref[...] = own_ref[blocks].astype(F32)
    for b in range(image_ref.shape[0]):
        image_ref[b] = lax.dot_general(
            tall_block(own_ref, last_ref, first + b, tall),
            factor_ref[first + b, 0],
            (((1,), (1,)), ((), ())),
            preferred_element_type=F32,
        )


def pass_on_kernel(own_ref, far_ref, after_ref, out_ref):
    @pl.when(is_even("space"))
    def _():
        out_ref[...] = own_ref[...]

    @pl.when(jnp.logical_not(is_even("space")))
    def _():
        out_ref[...] = far_ref[...]


def join_kernel(back_far_ref, got_ref, out_ref):
    out_ref[...] = (back_far_ref[...].astype(F32) + got_ref[...].astype(F32)).astype(BF16)


def own_back_kernel(rows, image_ref, factor_ref, total_ref, curve_ref, dir_ref, terms_ref, base_ref, curve_out_ref):
    blocks = factor_ref.shape[0]
    curve = curve_ref[...]
    for b in range(blocks):
        direction = dir_ref[b]
        weighted = terms_ref[0, b : b + 1] * direction
        curve += weighted * direction
        back = jnp.dot(image_ref[b], factor_ref[b, 0], preferred_element_type=F32)[:rows]
        base_ref[b] = total_ref[2 * blocks + b] + back + weighted
    curve_out_ref[...] = curve


def hessian_kernel(
    rows, ids_ref, factor_ref, turned_ref, image_one_ref, image_two_ref, near_ref, far_even_ref, far_odd_ref, own_ref,
    zeros_ref, back_far_ref, back_near_ref, total_ref, curve_ref, image_ref, around_ref, around_last_ref, last_ref,
):
    blocks, taps, bs, _ = factor_ref.shape
    count = around_ref.shape[1]
    tall = image_ref.shape[1]
    for i, refs in enumerate(((far_even_ref, far_odd_ref), (near_ref,), (own_ref,))):
        at = slice(i * blocks, (i + 1) * blocks)
        around_ref[at] = functools.reduce(jnp.add, [ref[:blocks] for ref in refs])
        around_last_ref[at] = functools.reduce(jnp.add, [ref[blocks].astype(F32) for ref in refs])
    first = (lax.axis_index("space") - 2) * blocks
    curve = jnp.zeros((rows, bs), F32)
    ids = lambda b, k: ids_ref[k - 1, b] - first
    side_by_side = lambda b: jnp.concatenate([factor_ref[b, k] for k in range(1, taps)], axis=1)
    for b in range(blocks):
        chosen = [tall_block(around_ref, around_last_ref, ids(b, k), tall) for k in range(1, taps)]
        half = image_one_ref.shape[0]
        own_image = image_one_ref[b] if b < half else image_two_ref[b - half]
        image = own_image + jnp.dot(
            jnp.concatenate(chosen, axis=1), turned_ref[b], preferred_element_type=F32
        )
        rounded = image.astype(BF16)
        image_ref[b] = rounded
        curve += (image * rounded.astype(F32))[:rows]
    curve_ref[...] = curve
    for b in range(blocks):
        back = jnp.dot(image_ref[b], side_by_side(b), preferred_element_type=F32)
        for k in range(1, taps):
            total_ref[ids(b, k)] += back[:rows, (k - 1) * bs : k * bs]
    for i, ref in enumerate((back_far_ref, back_near_ref)):
        for b in range(blocks):
            ref[b] = total_ref[i * blocks + b, :count].astype(BF16)
            last_ref[b : b + 1] = total_ref[i * blocks + b, count : count + 1]
        ref[blocks] = last_ref[...].astype(BF16)


def combine_kernel(
    base_ref, even_ref, odd_ref, mate_ref, curve_ref, terms_ref, field_ref, map_ref, hess_ref, out_ref
):
    blocks, rows, bs = field_ref.shape
    count = mate_ref.shape[1]
    inv_diag_ref = terms_ref.at[1]
    own_part = jnp.where(is_even("space"), 1.0, 0.0)
    arrived = lambda c: even_ref[c].astype(F32) + odd_ref[c].astype(F32) + own_part * mate_ref[c].astype(F32)
    from_last = arrived(blocks)
    cross = jnp.zeros((rows, bs), F32)
    square = jnp.zeros((rows, bs), F32)
    summed = jnp.zeros(out_ref.shape, F32)
    for b in range(0, blocks, PAIR):
        parts = []
        for c in range(b, b + PAIR):
            last = jnp.broadcast_to(from_last[c : c + 1], (rows - count, bs))
            hess = base_ref[c] + jnp.concatenate([arrived(c), last], axis=0)
            hess_ref[c] = hess
            scaled = hess * inv_diag_ref[c : c + 1]
            cross += field_ref[c] * scaled
            square += hess * scaled
            parts.append(scaled.astype(BF16))
        summed += jnp.dot(
            jnp.concatenate(parts, axis=1), map_ref[b * bs : (b + PAIR) * bs], preferred_element_type=F32
        )
    out_ref[...] = summed
    for i, acc in enumerate((curve_ref[...], cross, square)):
        out_ref[count + 1 + i : count + 2 + i] = as_row(jnp.sum(acc, axis=1, keepdims=True), out_ref.shape[1])


def finish_kernel(
    sums_ref, product_ref, hess_sums_ref, inner_ref, dir_ref, hess_ref, terms_ref, field_ref, map_ref, solution_hbm,
    residual_hbm, next_hbm, solution_ref, residual_ref, next_ref, sems,
):
    blocks, rows, bs = field_ref.shape
    whole = solution_ref.shape[0]
    inv_diag_ref = terms_ref.at[1]
    sums, product, hess_sums = sums_ref[...], product_ref[...], hess_sums_ref[...]
    column = lambda x, i: as_column(x[whole + i : whole + i + 1], rows)
    coeffs = product.astype(BF16)
    plain = column(sums, 0)
    energy = plain + jnp.sum(coeffs.astype(F32) * sums, axis=1, keepdims=True)
    step = energy / column(hess_sums, 0)
    left = sums - step * hess_sums
    hess_product = jnp.dot(hess_sums, inner_ref[...], precision=lax.Precision.HIGH)
    coeffs = (product - step * hess_product).astype(BF16)
    plain_next = plain - 2.0 * step * column(hess_sums, 1) + step * step * column(hess_sums, 2)
    energy_next = plain_next + jnp.sum(coeffs.astype(F32) * left, axis=1, keepdims=True)
    ratio = energy_next / energy
    part = blocks // OUT_PARTS
    copies = []

    def send(i, ref, hbm):
        at = pl.ds(i * part * bs, part * bs)
        copies.append(pltpu.make_async_copy(ref.at[:, at], hbm.at[:, at], sems.at[len(copies)]))
        copies[-1].start()

    residual_of = lambda c: field_ref[c] - step * hess_ref[c]
    for i in range(OUT_PARTS):
        for c in range(i * part, (i + 1) * part):
            at = slice(c * bs, (c + 1) * bs)
            solution_ref[:, at] = (step * dir_ref[c])[:whole]
            residual_ref[:, at] = residual_of(c)[:whole]
        send(i, solution_ref, solution_hbm)
        send(i, residual_ref, residual_hbm)
    for i in range(OUT_PARTS):
        for b in range(i * part, (i + 1) * part, PAIR):
            correction = jnp.dot(coeffs, map_ref[:, b * bs : (b + PAIR) * bs], preferred_element_type=F32)
            for c in range(b, b + PAIR):
                smoothed = (residual_of(c) + correction[:, (c - b) * bs : (c - b + 1) * bs]) * inv_diag_ref[c : c + 1]
                next_ref[:, c * bs : (c + 1) * bs] = (smoothed + ratio * dir_ref[c])[:whole]
        send(i, next_ref, next_hbm)
    for copy in copies:
        copy.wait()


def call(kernel, ins, outs, scratch=(), limit=16, keep=True, aliases={}, spaces=None):
    spec = lambda space: pl.BlockSpec(memory_space=space)
    spaces = spaces or (pltpu.VMEM,) * len(outs)
    shapes = tuple((space if keep else jax.ShapeDtypeStruct)(s, t) for space, (s, t) in zip(spaces, outs))
    specs = tuple(spec(space if keep else pl.ANY) for space in spaces)
    return pl.pallas_call(
        kernel,
        out_shape=shapes if len(shapes) > 1 else shapes[0],
        in_specs=[spec(space) for space in ins],
        out_specs=specs if len(shapes) > 1 else specs[0],
        scratch_shapes=scratch,
        input_output_aliases=aliases,
        compiler_params=pltpu.CompilerParams(vmem_limit_bytes=limit * 1024 * 1024),
    )


def in_hbm(x):
    return pltpu.with_memory_space_constraint(x, pltpu.HBM)


def in_vmem(x):
    return pltpu.with_memory_space_constraint(x, pltpu.VMEM)


def body(latent, responses, probes, prior_diag, factor, cond_ids, inducing_map, inner_inverse):
    blocks, _, bs, _ = factor.shape
    count = probes.shape[0]
    rows, tall = count + 8, count + 16
    by_block = lambda x: x.reshape(blocks, bs)
    sum_shape = ((rows, inducing_map.shape[1]), F32)
    field = ((blocks, rows, bs), F32)
    packed = ((blocks + 1, count, bs), BF16)
    vmem, smem = pltpu.VMEM, pltpu.SMEM
    partial, terms, right_side, inducing_map = call(
        project_kernel,
        [pl.ANY] * 5,
        [sum_shape, ((2, blocks, bs), F32), field, (inducing_map.shape, BF16)],
        [
            vmem((blocks, bs), F32),
            vmem((blocks, bs), jnp.int32),
            vmem((blocks, bs), F32),
            vmem(probes.shape, F32),
            pltpu.SemaphoreType.DMA((4 + MAP_PARTS,)),
        ],
    )(*map(in_hbm, (by_block(latent), by_block(responses), by_block(prior_diag), probes, inducing_map)))
    points = (terms, right_side, inducing_map)

    def load(msg):
        outs = [(factor.shape, BF16), (inner_inverse.shape, F32)]
        return call(load_kernel, [pl.ANY] * 3, outs, [pltpu.SemaphoreType.DMA((2,))])(
            in_hbm(factor), in_hbm(inner_inverse), msg
        )

    def turn_map(msg):
        return (call(turn_map_kernel, [vmem, pl.ANY], [(inducing_map.shape[::-1], BF16)])(inducing_map, msg),)

    sums, ((turned_map,), (factor, inner_inverse)) = total(partial, "space", [turn_map, load])
    direction, rounded, product = call(
        direction_kernel, [vmem] * 5, [field, packed, sum_shape], [vmem((blocks, bs), F32)]
    )(sums, inner_inverse, terms, right_side, turned_map)
    far_odd = sent(rounded, "space", 2, (1,))
    around = ((3 * blocks, rows, bs), F32)
    half = blocks // 2

    def own_image(first, other, *after):
        count = blocks - half if first else half
        return call(
            functools.partial(own_image_kernel, tall, first),
            [vmem] * 2 + [pl.ANY] * len(after),
            [((count, tall, bs), F32), other],
            [vmem((blocks, bs), F32)],
        )(rounded, factor, *after)

    image_one, again = own_image(0, packed)
    far_even = sent(again, "space", 2, (0,))
    image_two, zeros = own_image(half, around, image_one)
    shape = (blocks, (factor.shape[1] - 1) * bs, bs)
    turned, ids = call(
        turn_kernel,
        [vmem, pl.ANY, pl.ANY],
        [(shape, BF16), (cond_ids.shape[::-1], jnp.int32)],
        [pltpu.SemaphoreType.DMA],
        spaces=(vmem, smem),
    )(factor, cond_ids.T, image_two)
    near = swapped(call(pass_on_kernel, [vmem, vmem, pl.ANY], [packed])(rounded, far_odd, turned), "space")
    back_far, back_near, back_own, curve, image = call(
        functools.partial(hessian_kernel, rows),
        [smem] + [vmem] * 9,
        [packed, packed, around, ((rows, bs), F32), ((blocks, tall, bs), BF16)],
        [vmem((3 * blocks, count, bs), BF16), vmem((3 * blocks, bs), F32), vmem((blocks, bs), F32)],
        aliases={9: 2},
    )(ids, factor, turned, image_one, image_two, near, far_even, far_odd, rounded, zeros)
    mate = swapped(back_near, "space")
    from_even = sent(back_far, "space", -2, (0,))
    from_odd = sent(call(join_kernel, [vmem] * 2, [packed])(back_far, mate), "space", -2, (1,))
    base, curve = call(functools.partial(own_back_kernel, rows), [vmem] * 6, [field, ((rows, bs), F32)])(
        image, factor, back_own, curve, direction, terms
    )
    hess, partial = call(combine_kernel, [vmem] * 8, [field, sum_shape])(base, from_even, from_odd, mate, curve, *points)
    hess_sums, _ = total(partial, "space")
    whole = ((count + 1, blocks * bs), F32)
    scratch = [vmem(*whole)] * 3 + [pltpu.SemaphoreType.DMA((3 * OUT_PARTS,))]
    return call(finish_kernel, [vmem] * 9, [whole] * 3, scratch, keep=False)(
        *map(in_vmem, (sums, product, hess_sums, inner_inverse, direction, hess, terms, right_side, turned_map))
    )


def solution(mesh):
    return jax.shard_map(
        body,
        mesh=mesh,
        in_specs=(
            P(("groups", "space")),
            P(("groups", "space")),
            P(None, ("groups", "space")),
            P(("groups", "space")),
            P(("groups", "space"), None, None, None),
            P(("groups", "space"), None),
            P(("groups", "space"), None),
            P("groups", None),
        ),
        out_specs=(
            P(None, ("groups", "space")),
            P(None, ("groups", "space")),
            P(None, ("groups", "space")),
        ),
        check_vma=False,
    )
```

```python
import functools

import jax
import jax.numpy as jnp
from jax import lax
from jax.experimental import pallas as pl
from jax.experimental.pallas import tpu as pltpu
from jax.sharding import PartitionSpec as P

F32, BF16 = jnp.float32, jnp.bfloat16
PAIR = 2
MAP_PARTS = 4
OUT_PARTS = 4


def sent(block, axis, distance, parities=(0, 1)):
    devices = range(lax.axis_size(axis))
    return lax.ppermute(block, axis, [(i, i + distance) for i in devices if i % 2 in parities and i + distance in devices])


def swapped(block, axis):
    return lax.ppermute(block, axis, [(i, i ^ 1) for i in range(lax.axis_size(axis))])


def is_even(axis):
    return lax.rem(lax.axis_index(axis), 2) == 0


def write_message(msg_ref, x):
    top, half = x.shape[0] - 8, x.shape[1] // 2
    value, beside = x[top:, :half], x[top:, half:]
    high = value.astype(BF16).astype(F32)
    middle = (value - high).astype(BF16).astype(F32)
    low = value - high - middle
    row = lax.broadcasted_iota(jnp.int32, value.shape, 0)
    left = jnp.where(row < 4, high, pltpu.roll(low, 3, 0))
    right = jnp.where(row < 1, beside, middle)
    msg_ref[...] = jnp.concatenate([x[:top], jnp.concatenate([left, right], axis=1)], axis=0).astype(BF16)


def read_message(msg_ref):
    x = msg_ref[...].astype(F32)
    top, half = x.shape[0] - 8, x.shape[1] // 2
    left, right = x[top:, :half], x[top:, half:]
    row = lax.broadcasted_iota(jnp.int32, left.shape, 0)
    left = jnp.where(row < 1, left, left + right + pltpu.roll(left, 5, 0))
    return jnp.concatenate([x[:top], jnp.concatenate([left, right], axis=1)], axis=0)


def add_kernel(count, held, x_ref, *refs):
    in_refs, (out_ref, *msg_refs) = refs[: count - 1], refs[count - 1 + held :]
    x = x_ref[...]
    for ref in in_refs:
        x = x + (ref[...] if ref.dtype == F32 else read_message(ref))
    out_ref[...] = x
    for ref in msg_refs:
        write_message(ref, x)


def rounds_of(n):
    rounds = [(1,)] + [(3,)] * (n > 2)
    step = 4
    while step < n:
        rounds.append(tuple((m * step) ^ 1 for m in range(1, 4) if m * step < n))
        step *= 4
    return rounds


def total(x, axis, wire, beside=()):
    n = lax.axis_size(axis)
    if n & (n - 1):
        return lax.psum(x, axis), [work(x) for work in beside]
    rounds = rounds_of(n)
    made, todo, msg = [], list(beside), x
    for i, partners in enumerate(rounds):
        got = [lax.ppermute(msg, axis, [(j, j ^ d) for j in range(n)]) for d in partners]
        last = i + 1 == len(rounds)
        held = ()
        while len(todo) >= max(len(rounds) - i, 1):
            made.append(todo.pop(0)(msg))
            held += made[-1]
        add = functools.partial(add_kernel, len(got) + 1, len(held))
        ins = [pltpu.VMEM] * (len(got) + 1) + [pl.ANY] * len(held)
        outs = [(x.shape, F32)] + [(x.shape, BF16)] * (wire == BF16 and not last)
        x, *rest = jax.tree.leaves(call(add, ins, outs)(x, *got, *held))
        msg = rest[0] if rest else x
    return x, made


def eye(rows, lanes):
    return lax.broadcasted_iota(jnp.int32, (rows, lanes), 0) == lax.broadcasted_iota(jnp.int32, (rows, lanes), 1)


def as_row(column, lanes):
    return jnp.sum(jnp.where(eye(column.shape[0], lanes), column, 0.0), axis=0, keepdims=True)


def as_column(row, rows):
    return jnp.sum(jnp.where(eye(rows, row.shape[1]), row, 0.0), axis=1, keepdims=True)


def project_kernel(
    latent_hbm, responses_hbm, prior_hbm, probes_hbm, map_hbm, out_ref, terms_ref, field_ref, map_ref, latent_ref,
    responses_ref, prior_ref, probes_ref, sems,
):
    blocks, bs = latent_ref.shape
    rows = out_ref.shape[0]
    count = probes_ref.shape[0]
    part = map_ref.shape[0] // MAP_PARTS
    cut = lambda ref, i: ref.at[i * part : (i + 1) * part]
    pairs = [(latent_hbm, latent_ref), (responses_hbm, responses_ref), (prior_hbm, prior_ref), (probes_hbm, probes_ref)]
    pairs += [(cut(map_hbm, i), cut(map_ref, i)) for i in range(MAP_PARTS)]
    copies = [pltpu.make_async_copy(a, b, sems.at[i]) for i, (a, b) in enumerate(pairs)]
    for copy in copies:
        copy.start()
    for copy in copies[:3]:
        copy.wait()
    probability = 1.0 / (1.0 + jnp.exp(-latent_ref[...]))
    weights = probability * (1.0 - probability)
    gradient = responses_ref[...].astype(F32) - probability
    inv_diag = 1.0 / (weights + prior_ref[...])
    terms_ref[0] = weights
    terms_ref[1] = inv_diag
    copies[3].wait()
    energy = jnp.zeros((rows, bs), F32)
    scaled = []
    for b in range(blocks):
        at = slice(b * bs, (b + 1) * bs)
        last = jnp.broadcast_to(gradient[b : b + 1], (rows - count, bs))
        field = pltpu.roll(jnp.concatenate([probes_ref[:, at], last], axis=0), 1, 0)
        field_ref[b] = field
        scaled.append(field * inv_diag[b : b + 1])
        energy += field * scaled[-1]
    summed = jnp.zeros(out_ref.shape, F32)
    for b in range(0, blocks, PAIR):
        if b * bs % part == 0:
            copies[4 + b * bs // part].wait()
        both = jnp.concatenate([scaled[b + i].astype(BF16) for i in range(PAIR)], axis=1)
        summed += jnp.dot(both, map_ref[b * bs : (b + PAIR) * bs], preferred_element_type=F32)
    out_ref[...] = summed
    out_ref[count + 1 : count + 2] = as_row(jnp.sum(energy, axis=1, keepdims=True), out_ref.shape[1])


def direction_kernel(sums_ref, inner_ref, terms_ref, field_ref, map_ref, dir_ref, msg_ref, product_ref, last_ref):
    blocks, _, bs = field_ref.shape
    count = msg_ref.shape[1]
    inv_diag_ref = terms_ref.at[1]
    product = jnp.dot(sums_ref[...], inner_ref[...], precision=lax.Precision.HIGH)
    product_ref[...] = product
    coeffs = product.astype(BF16)
    for b in range(0, blocks, PAIR):
        correction = jnp.dot(coeffs, map_ref[:, b * bs : (b + PAIR) * bs], preferred_element_type=F32)
        for c in range(b, b + PAIR):
            direction = (field_ref[c] + correction[:, (c - b) * bs : (c - b + 1) * bs]) * inv_diag_ref[c : c + 1]
            dir_ref[c] = direction
            msg_ref[c] = direction[:count].astype(BF16)
            last_ref[c : c + 1] = direction[count : count + 1]
    msg_ref[blocks] = last_ref[...].astype(BF16)


def turn_map_kernel(map_ref, after_ref, turned_ref):
    points, inducing = map_ref.shape
    for i in range(0, points, inducing):
        turned_ref[:, i : i + inducing] = map_ref[i : i + inducing].T


def load_kernel(factor_hbm, inner_hbm, after_ref, factor_ref, inner_ref, sems):
    copies = [
        pltpu.make_async_copy(factor_hbm, factor_ref, sems.at[0]),
        pltpu.make_async_copy(inner_hbm, inner_ref, sems.at[1]),
    ]
    for copy in copies:
        copy.start()
    for copy in copies:
        copy.wait()


def turn_kernel(factor_ref, ids_any, after_ref, turned_ref, ids_ref, sem):
    copy = pltpu.make_async_copy(ids_any, ids_ref, sem)
    copy.start()
    blocks, taps, bs, _ = factor_ref.shape
    for b in range(blocks):
        for k in range(1, taps):
            turned_ref[b, (k - 1) * bs : k * bs] = factor_ref[b, k].T
    copy.wait()


def tall_block(refs, lasts, at, tall):
    most = refs[at]
    last = jnp.broadcast_to(lasts[pl.ds(at, 1), :], (tall - most.shape[0], most.shape[1]))
    return jnp.concatenate([most, last.astype(BF16)], axis=0)


def own_image_kernel(tall, first, own_ref, factor_ref, *refs):
    image_ref, other_ref, last_ref = refs[-3:]
    blocks, bs = last_ref.shape
    other_ref[...] = jnp.zeros_like(other_ref) if first else own_ref[...]
    last_ref[...] = own_ref[blocks].astype(F32)
    for b in range(image_ref.shape[0]):
        image_ref[b] = lax.dot_general(
            tall_block(own_ref, last_ref, first + b, tall),
            factor_ref[first + b, 0],
            (((1,), (1,)), ((), ())),
            preferred_element_type=F32,
        )


def pass_on_kernel(own_ref, far_ref, after_ref, out_ref):
    @pl.when(is_even("space"))
    def _():
        out_ref[...] = own_ref[...]

    @pl.when(jnp.logical_not(is_even("space")))
    def _():
        out_ref[...] = far_ref[...]


def join_kernel(back_far_ref, got_ref, out_ref):
    out_ref[...] = (back_far_ref[...].astype(F32) + got_ref[...].astype(F32)).astype(BF16)


def own_back_kernel(rows, image_ref, factor_ref, total_ref, curve_ref, dir_ref, terms_ref, base_ref, curve_out_ref):
    blocks = factor_ref.shape[0]
    curve = curve_ref[...]
    for b in range(blocks):
        direction = dir_ref[b]
        weighted = terms_ref[0, b : b + 1] * direction
        curve += weighted * direction
        back = jnp.dot(image_ref[b], factor_ref[b, 0], preferred_element_type=F32)[:rows]
        base_ref[b] = total_ref[2 * blocks + b] + back + weighted
    curve_out_ref[...] = curve


def hessian_kernel(
    rows, ids_ref, factor_ref, turned_ref, image_one_ref, image_two_ref, near_ref, far_even_ref, far_odd_ref, own_ref,
    zeros_ref, back_far_ref, back_near_ref, total_ref, curve_ref, image_ref, around_ref, around_last_ref, last_ref,
):
    blocks, taps, bs, _ = factor_ref.shape
    count = around_ref.shape[1]
    tall = image_ref.shape[1]
    for i, refs in enumerate(((far_even_ref, far_odd_ref), (near_ref,), (own_ref,))):
        at = slice(i * blocks, (i + 1) * blocks)
        around_ref[at] = functools.reduce(jnp.add, [ref[:blocks] for ref in refs])
        around_last_ref[at] = functools.reduce(jnp.add, [ref[blocks].astype(F32) for ref in refs])
    first = (lax.axis_index("space") - 2) * blocks
    curve = jnp.zeros((rows, bs), F32)
    ids = lambda b, k: ids_ref[k - 1, b] - first
    side_by_side = lambda b: jnp.concatenate([factor_ref[b, k] for k in range(1, taps)], axis=1)
    for b in range(blocks):
        chosen = [tall_block(around_ref, around_last_ref, ids(b, k), tall) for k in range(1, taps)]
        half = image_one_ref.shape[0]
        own_image = image_one_ref[b] if b < half else image_two_ref[b - half]
        image = own_image + jnp.dot(
            jnp.concatenate(chosen, axis=1), turned_ref[b], preferred_element_type=F32
        )
        rounded = image.astype(BF16)
        image_ref[b] = rounded
        curve += (image * rounded.astype(F32))[:rows]
    curve_ref[...] = curve
    for b in range(blocks):
        back = jnp.dot(image_ref[b], side_by_side(b), preferred_element_type=F32)
        for k in range(1, taps):
            total_ref[ids(b, k)] += back[:rows, (k - 1) * bs : k * bs]
    for i, ref in enumerate((back_far_ref, back_near_ref)):
        for b in range(blocks):
            ref[b] = total_ref[i * blocks + b, :count].astype(BF16)
            last_ref[b : b + 1] = total_ref[i * blocks + b, count : count + 1]
        ref[blocks] = last_ref[...].astype(BF16)


def combine_kernel(
    base_ref, even_ref, odd_ref, mate_ref, curve_ref, terms_ref, field_ref, map_ref, hess_ref, out_ref
):
    blocks, rows, bs = field_ref.shape
    count = mate_ref.shape[1]
    inv_diag_ref = terms_ref.at[1]
    own_part = jnp.where(is_even("space"), 1.0, 0.0)
    arrived = lambda c: even_ref[c].astype(F32) + odd_ref[c].astype(F32) + own_part * mate_ref[c].astype(F32)
    from_last = arrived(blocks)
    cross = jnp.zeros((rows, bs), F32)
    square = jnp.zeros((rows, bs), F32)
    summed = jnp.zeros(out_ref.shape, F32)
    for b in range(0, blocks, PAIR):
        parts = []
        for c in range(b, b + PAIR):
            last = jnp.broadcast_to(from_last[c : c + 1], (rows - count, bs))
            hess = base_ref[c] + jnp.concatenate([arrived(c), last], axis=0)
            hess_ref[c] = hess
            scaled = hess * inv_diag_ref[c : c + 1]
            cross += field_ref[c] * scaled
            square += hess * scaled
            parts.append(scaled.astype(BF16))
        summed += jnp.dot(
            jnp.concatenate(parts, axis=1), map_ref[b * bs : (b + PAIR) * bs], preferred_element_type=F32
        )
    out_ref[...] = summed
    for i, acc in enumerate((curve_ref[...], cross, square)):
        out_ref[count + 1 + i : count + 2 + i] = as_row(jnp.sum(acc, axis=1, keepdims=True), out_ref.shape[1])


def finish_kernel(
    sums_ref, product_ref, hess_sums_ref, inner_ref, dir_ref, hess_ref, terms_ref, field_ref, map_ref, solution_hbm,
    residual_hbm, next_hbm, solution_ref, residual_ref, next_ref, sems,
):
    blocks, rows, bs = field_ref.shape
    whole = solution_ref.shape[0]
    inv_diag_ref = terms_ref.at[1]
    sums, product, hess_sums = sums_ref[...], product_ref[...], hess_sums_ref[...]
    column = lambda x, i: as_column(x[whole + i : whole + i + 1], rows)
    coeffs = product.astype(BF16)
    plain = column(sums, 0)
    energy = plain + jnp.sum(coeffs.astype(F32) * sums, axis=1, keepdims=True)
    step = energy / column(hess_sums, 0)
    left = sums - step * hess_sums
    hess_product = jnp.dot(hess_sums, inner_ref[...], precision=lax.Precision.HIGH)
    coeffs = (product - step * hess_product).astype(BF16)
    plain_next = plain - 2.0 * step * column(hess_sums, 1) + step * step * column(hess_sums, 2)
    energy_next = plain_next + jnp.sum(coeffs.astype(F32) * left, axis=1, keepdims=True)
    ratio = energy_next / energy
    part = blocks // OUT_PARTS
    copies = []

    def send(i, ref, hbm):
        at = pl.ds(i * part * bs, part * bs)
        copies.append(pltpu.make_async_copy(ref.at[:, at], hbm.at[:, at], sems.at[len(copies)]))
        copies[-1].start()

    residual_of = lambda c: field_ref[c] - step * hess_ref[c]
    for i in range(OUT_PARTS):
        for c in range(i * part, (i + 1) * part):
            at = slice(c * bs, (c + 1) * bs)
            solution_ref[:, at] = (step * dir_ref[c])[:whole]
            residual_ref[:, at] = residual_of(c)[:whole]
        send(i, solution_ref, solution_hbm)
        send(i, residual_ref, residual_hbm)
    for i in range(OUT_PARTS):
        for b in range(i * part, (i + 1) * part, PAIR):
            correction = jnp.dot(coeffs, map_ref[:, b * bs : (b + PAIR) * bs], preferred_element_type=F32)
            for c in range(b, b + PAIR):
                smoothed = (residual_of(c) + correction[:, (c - b) * bs : (c - b + 1) * bs]) * inv_diag_ref[c : c + 1]
                next_ref[:, c * bs : (c + 1) * bs] = (smoothed + ratio * dir_ref[c])[:whole]
        send(i, next_ref, next_hbm)
    for copy in copies:
        copy.wait()


def call(kernel, ins, outs, scratch=(), limit=16, keep=True, aliases={}, spaces=None):
    spec = lambda space: pl.BlockSpec(memory_space=space)
    spaces = spaces or (pltpu.VMEM,) * len(outs)
    shapes = tuple((space if keep else jax.ShapeDtypeStruct)(s, t) for space, (s, t) in zip(spaces, outs))
    specs = tuple(spec(space if keep else pl.ANY) for space in spaces)
    return pl.pallas_call(
        kernel,
        out_shape=shapes if len(shapes) > 1 else shapes[0],
        in_specs=[spec(space) for space in ins],
        out_specs=specs if len(shapes) > 1 else specs[0],
        scratch_shapes=scratch,
        input_output_aliases=aliases,
        compiler_params=pltpu.CompilerParams(vmem_limit_bytes=limit * 1024 * 1024),
    )


def in_hbm(x):
    return pltpu.with_memory_space_constraint(x, pltpu.HBM)


def in_vmem(x):
    return pltpu.with_memory_space_constraint(x, pltpu.VMEM)


def body(latent, responses, probes, prior_diag, factor, cond_ids, inducing_map, inner_inverse):
    blocks, _, bs, _ = factor.shape
    count = probes.shape[0]
    rows, tall = count + 8, count + 16
    by_block = lambda x: x.reshape(blocks, bs)
    sum_shape = ((rows, inducing_map.shape[1]), F32)
    field = ((blocks, rows, bs), F32)
    packed = ((blocks + 1, count, bs), BF16)
    vmem, smem = pltpu.VMEM, pltpu.SMEM
    partial, terms, right_side, inducing_map = call(
        project_kernel,
        [pl.ANY] * 5,
        [sum_shape, ((2, blocks, bs), F32), field, (inducing_map.shape, BF16)],
        [
            vmem((blocks, bs), F32),
            vmem((blocks, bs), jnp.int32),
            vmem((blocks, bs), F32),
            vmem(probes.shape, F32),
            pltpu.SemaphoreType.DMA((4 + MAP_PARTS,)),
        ],
    )(*map(in_hbm, (by_block(latent), by_block(responses), by_block(prior_diag), probes, inducing_map)))
    points = (terms, right_side, inducing_map)

    def load(msg):
        outs = [(factor.shape, BF16), (inner_inverse.shape, F32)]
        return call(load_kernel, [pl.ANY] * 3, outs, [pltpu.SemaphoreType.DMA((2,))])(
            in_hbm(factor), in_hbm(inner_inverse), msg
        )

    def turn_map(msg):
        return (call(turn_map_kernel, [vmem, pl.ANY], [(inducing_map.shape[::-1], BF16)])(inducing_map, msg),)

    sums, ((turned_map,), (factor, inner_inverse)) = total(partial, "space", BF16, [turn_map, load])
    direction, rounded, product = call(
        direction_kernel, [vmem] * 5, [field, packed, sum_shape], [vmem((blocks, bs), F32)]
    )(sums, inner_inverse, terms, right_side, turned_map)
    far_odd = sent(rounded, "space", 2, (1,))
    around = ((3 * blocks, rows, bs), F32)
    half = blocks // 2

    def own_image(first, other, *after):
        count = blocks - half if first else half
        return call(
            functools.partial(own_image_kernel, tall, first),
            [vmem] * 2 + [pl.ANY] * len(after),
            [((count, tall, bs), F32), other],
            [vmem((blocks, bs), F32)],
        )(rounded, factor, *after)

    image_one, again = own_image(0, packed)
    far_even = sent(again, "space", 2, (0,))
    image_two, zeros = own_image(half, around, image_one)
    shape = (blocks, (factor.shape[1] - 1) * bs, bs)
    turned, ids = call(
        turn_kernel,
        [vmem, pl.ANY, pl.ANY],
        [(shape, BF16), (cond_ids.shape[::-1], jnp.int32)],
        [pltpu.SemaphoreType.DMA],
        spaces=(vmem, smem),
    )(factor, cond_ids.T, image_two)
    near = swapped(call(pass_on_kernel, [vmem, vmem, pl.ANY], [packed])(rounded, far_odd, turned), "space")
    back_far, back_near, back_own, curve, image = call(
        functools.partial(hessian_kernel, rows),
        [smem] + [vmem] * 9,
        [packed, packed, around, ((rows, bs), F32), ((blocks, tall, bs), BF16)],
        [vmem((3 * blocks, count, bs), BF16), vmem((3 * blocks, bs), F32), vmem((blocks, bs), F32)],
        aliases={9: 2},
    )(ids, factor, turned, image_one, image_two, near, far_even, far_odd, rounded, zeros)
    mate = swapped(back_near, "space")
    from_even = sent(back_far, "space", -2, (0,))
    from_odd = sent(call(join_kernel, [vmem] * 2, [packed])(back_far, mate), "space", -2, (1,))
    base, curve = call(functools.partial(own_back_kernel, rows), [vmem] * 6, [field, ((rows, bs), F32)])(
        image, factor, back_own, curve, direction, terms
    )
    hess, partial = call(combine_kernel, [vmem] * 8, [field, sum_shape])(base, from_even, from_odd, mate, curve, *points)
    hess_sums, _ = total(partial, "space", F32)
    whole = ((count + 1, blocks * bs), F32)
    scratch = [vmem(*whole)] * 3 + [pltpu.SemaphoreType.DMA((3 * OUT_PARTS,))]
    return call(finish_kernel, [vmem] * 9, [whole] * 3, scratch, keep=False)(
        *map(in_vmem, (sums, product, hess_sums, inner_inverse, direction, hess, terms, right_side, turned_map))
    )


def solution(mesh):
    return jax.shard_map(
        body,
        mesh=mesh,
        in_specs=(
            P(("groups", "space")),
            P(("groups", "space")),
            P(None, ("groups", "space")),
            P(("groups", "space")),
            P(("groups", "space"), None, None, None),
            P(("groups", "space"), None),
            P(("groups", "space"), None),
            P("groups", None),
        ),
        out_specs=(
            P(None, ("groups", "space")),
            P(None, ("groups", "space")),
            P(None, ("groups", "space")),
        ),
        check_vma=False,
    )
```

```python
import functools

import jax
import jax.numpy as jnp
from jax import lax
from jax.experimental import pallas as pl
from jax.experimental.pallas import tpu as pltpu
from jax.sharding import PartitionSpec as P

F32, BF16 = jnp.float32, jnp.bfloat16
PAIR = 2
MAP_PARTS = 4
OUT_PARTS = 4


def sent(block, axis, distance, parities=(0, 1)):
    devices = range(lax.axis_size(axis))
    return lax.ppermute(block, axis, [(i, i + distance) for i in devices if i % 2 in parities and i + distance in devices])


def swapped(block, axis):
    return lax.ppermute(block, axis, [(i, i ^ 1) for i in range(lax.axis_size(axis))])


def is_even(axis):
    return lax.rem(lax.axis_index(axis), 2) == 0


def write_message(msg_ref, x):
    top, half = x.shape[0] - 8, x.shape[1] // 2
    value, beside = x[top:, :half], x[top:, half:]
    high = value.astype(BF16).astype(F32)
    middle = (value - high).astype(BF16).astype(F32)
    low = value - high - middle
    row = lax.broadcasted_iota(jnp.int32, value.shape, 0)
    left = jnp.where(row < 4, high, pltpu.roll(low, 3, 0))
    right = jnp.where(row < 1, beside, middle)
    msg_ref[...] = jnp.concatenate([x[:top], jnp.concatenate([left, right], axis=1)], axis=0).astype(BF16)


def read_message(msg_ref):
    x = msg_ref[...].astype(F32)
    top, half = x.shape[0] - 8, x.shape[1] // 2
    left, right = x[top:, :half], x[top:, half:]
    row = lax.broadcasted_iota(jnp.int32, left.shape, 0)
    left = jnp.where(row < 1, left, left + right + pltpu.roll(left, 5, 0))
    return jnp.concatenate([x[:top], jnp.concatenate([left, right], axis=1)], axis=0)


def add_kernel(count, held, x_ref, *refs):
    in_refs, (out_ref, *msg_refs) = refs[: count - 1], refs[count - 1 + held :]
    x = x_ref[...]
    for ref in in_refs:
        x = x + (ref[...] if ref.dtype == F32 else read_message(ref))
    out_ref[...] = x
    for ref in msg_refs:
        write_message(ref, x)


def rounds_of(n):
    rounds, step = [(1,)], n
    if n.bit_length() % 2:
        step //= 2
        rounds.append((step ^ 1,))
    while step > 2:
        step //= 4
        rounds.append(tuple((m * step) ^ 1 for m in range(1, 4)))
    return rounds


def total(x, axis, beside=()):
    n = lax.axis_size(axis)
    if n & (n - 1):
        return lax.psum(x, axis), [work(x) for work in beside]
    rounds = rounds_of(n)
    made, todo, msg = [], list(beside), x
    for i, partners in enumerate(rounds):
        got = [lax.ppermute(msg, axis, [(j, j ^ d) for j in range(n)]) for d in partners]
        last = i + 1 == len(rounds)
        held = ()
        while len(todo) >= max(len(rounds) - i, 1):
            made.append(todo.pop(0)(msg))
            held += made[-1]
        add = functools.partial(add_kernel, len(got) + 1, len(held))
        ins = [pltpu.VMEM] * (len(got) + 1) + [pl.ANY] * len(held)
        outs = [(x.shape, F32)] + [(x.shape, BF16)] * (not last)
        x, *rest = jax.tree.leaves(call(add, ins, outs)(x, *got, *held))
        msg = rest[0] if rest else None
    return x, made


def eye(rows, lanes):
    return lax.broadcasted_iota(jnp.int32, (rows, lanes), 0) == lax.broadcasted_iota(jnp.int32, (rows, lanes), 1)


def as_row(column, lanes):
    return jnp.sum(jnp.where(eye(column.shape[0], lanes), column, 0.0), axis=0, keepdims=True)


def as_column(row, rows):
    return jnp.sum(jnp.where(eye(rows, row.shape[1]), row, 0.0), axis=1, keepdims=True)


def project_kernel(
    latent_hbm, responses_hbm, prior_hbm, probes_hbm, map_hbm, out_ref, terms_ref, field_ref, map_ref, latent_ref,
    responses_ref, prior_ref, probes_ref, sems,
):
    blocks, bs = latent_ref.shape
    rows = out_ref.shape[0]
    count = probes_ref.shape[0]
    part = map_ref.shape[0] // MAP_PARTS
    cut = lambda ref, i: ref.at[i * part : (i + 1) * part]
    pairs = [(latent_hbm, latent_ref), (responses_hbm, responses_ref), (prior_hbm, prior_ref), (probes_hbm, probes_ref)]
    pairs += [(cut(map_hbm, i), cut(map_ref, i)) for i in range(MAP_PARTS)]
    copies = [pltpu.make_async_copy(a, b, sems.at[i]) for i, (a, b) in enumerate(pairs)]
    for copy in copies:
        copy.start()
    for copy in copies[:3]:
        copy.wait()
    probability = 1.0 / (1.0 + jnp.exp(-latent_ref[...]))
    weights = probability * (1.0 - probability)
    gradient = responses_ref[...].astype(F32) - probability
    inv_diag = 1.0 / (weights + prior_ref[...])
    terms_ref[0] = weights
    terms_ref[1] = inv_diag
    copies[3].wait()
    energy = jnp.zeros((rows, bs), F32)
    scaled = []
    for b in range(blocks):
        at = slice(b * bs, (b + 1) * bs)
        last = jnp.broadcast_to(gradient[b : b + 1], (rows - count, bs))
        field = pltpu.roll(jnp.concatenate([probes_ref[:, at], last], axis=0), 1, 0)
        field_ref[b] = field
        scaled.append(field * inv_diag[b : b + 1])
        energy += field * scaled[-1]
    summed = jnp.zeros(out_ref.shape, F32)
    for b in range(0, blocks, PAIR):
        if b * bs % part == 0:
            copies[4 + b * bs // part].wait()
        both = jnp.concatenate([scaled[b + i].astype(BF16) for i in range(PAIR)], axis=1)
        summed += jnp.dot(both, map_ref[b * bs : (b + PAIR) * bs], preferred_element_type=F32)
    out_ref[...] = summed
    out_ref[count + 1 : count + 2] = as_row(jnp.sum(energy, axis=1, keepdims=True), out_ref.shape[1])


def direction_kernel(sums_ref, inner_ref, terms_ref, field_ref, map_ref, dir_ref, msg_ref, product_ref, last_ref):
    blocks, _, bs = field_ref.shape
    count = msg_ref.shape[1]
    inv_diag_ref = terms_ref.at[1]
    product = jnp.dot(sums_ref[...], inner_ref[...], precision=lax.Precision.HIGH)
    product_ref[...] = product
    coeffs = product.astype(BF16)
    for b in range(0, blocks, PAIR):
        correction = jnp.dot(coeffs, map_ref[:, b * bs : (b + PAIR) * bs], preferred_element_type=F32)
        for c in range(b, b + PAIR):
            direction = (field_ref[c] + correction[:, (c - b) * bs : (c - b + 1) * bs]) * inv_diag_ref[c : c + 1]
            dir_ref[c] = direction
            msg_ref[c] = direction[:count].astype(BF16)
            last_ref[c : c + 1] = direction[count : count + 1]
    msg_ref[blocks] = last_ref[...].astype(BF16)


def turn_map_kernel(map_ref, after_ref, turned_ref):
    points, inducing = map_ref.shape
    for i in range(0, points, inducing):
        turned_ref[:, i : i + inducing] = map_ref[i : i + inducing].T


def load_kernel(factor_hbm, inner_hbm, after_ref, factor_ref, inner_ref, sems):
    copies = [
        pltpu.make_async_copy(factor_hbm, factor_ref, sems.at[0]),
        pltpu.make_async_copy(inner_hbm, inner_ref, sems.at[1]),
    ]
    for copy in copies:
        copy.start()
    for copy in copies:
        copy.wait()


def turn_kernel(factor_ref, ids_any, after_ref, turned_ref, ids_ref, sem):
    copy = pltpu.make_async_copy(ids_any, ids_ref, sem)
    copy.start()
    blocks, taps, bs, _ = factor_ref.shape
    for b in range(blocks):
        for k in range(1, taps):
            turned_ref[b, (k - 1) * bs : k * bs] = factor_ref[b, k].T
    copy.wait()


def tall_block(refs, lasts, at, tall):
    most = refs[at]
    last = jnp.broadcast_to(lasts[pl.ds(at, 1), :], (tall - most.shape[0], most.shape[1]))
    return jnp.concatenate([most, last.astype(BF16)], axis=0)


def own_image_kernel(tall, first, own_ref, factor_ref, *refs):
    image_ref, other_ref, last_ref = refs[-3:]
    blocks, bs = last_ref.shape
    other_ref[...] = jnp.zeros_like(other_ref) if first else own_ref[...]
    last_ref[...] = own_ref[blocks].astype(F32)
    for b in range(image_ref.shape[0]):
        image_ref[b] = lax.dot_general(
            tall_block(own_ref, last_ref, first + b, tall),
            factor_ref[first + b, 0],
            (((1,), (1,)), ((), ())),
            preferred_element_type=F32,
        )


def pass_on_kernel(own_ref, far_ref, after_ref, out_ref):
    @pl.when(is_even("space"))
    def _():
        out_ref[...] = own_ref[...]

    @pl.when(jnp.logical_not(is_even("space")))
    def _():
        out_ref[...] = far_ref[...]


def join_kernel(back_far_ref, got_ref, out_ref):
    out_ref[...] = (back_far_ref[...].astype(F32) + got_ref[...].astype(F32)).astype(BF16)


def own_back_kernel(rows, image_ref, factor_ref, total_ref, curve_ref, dir_ref, terms_ref, base_ref, curve_out_ref):
    blocks = factor_ref.shape[0]
    curve = curve_ref[...]
    for b in range(blocks):
        direction = dir_ref[b]
        weighted = terms_ref[0, b : b + 1] * direction
        curve += weighted * direction
        back = jnp.dot(image_ref[b], factor_ref[b, 0], preferred_element_type=F32)[:rows]
        base_ref[b] = total_ref[2 * blocks + b] + back + weighted
    curve_out_ref[...] = curve


def hessian_kernel(
    rows, ids_ref, factor_ref, turned_ref, image_one_ref, image_two_ref, near_ref, far_even_ref, far_odd_ref, own_ref,
    zeros_ref, back_far_ref, back_near_ref, total_ref, curve_ref, image_ref, around_ref, around_last_ref, last_ref,
):
    blocks, taps, bs, _ = factor_ref.shape
    count = around_ref.shape[1]
    tall = image_ref.shape[1]
    for i, refs in enumerate(((far_even_ref, far_odd_ref), (near_ref,), (own_ref,))):
        at = slice(i * blocks, (i + 1) * blocks)
        around_ref[at] = functools.reduce(jnp.add, [ref[:blocks] for ref in refs])
        around_last_ref[at] = functools.reduce(jnp.add, [ref[blocks].astype(F32) for ref in refs])
    first = (lax.axis_index("space") - 2) * blocks
    curve = jnp.zeros((rows, bs), F32)
    ids = lambda b, k: ids_ref[k - 1, b] - first
    side_by_side = lambda b: jnp.concatenate([factor_ref[b, k] for k in range(1, taps)], axis=1)
    for b in range(blocks):
        chosen = [tall_block(around_ref, around_last_ref, ids(b, k), tall) for k in range(1, taps)]
        half = image_one_ref.shape[0]
        own_image = image_one_ref[b] if b < half else image_two_ref[b - half]
        image = own_image + jnp.dot(
            jnp.concatenate(chosen, axis=1), turned_ref[b], preferred_element_type=F32
        )
        rounded = image.astype(BF16)
        image_ref[b] = rounded
        curve += (image * rounded.astype(F32))[:rows]
    curve_ref[...] = curve
    for b in range(blocks):
        back = jnp.dot(image_ref[b], side_by_side(b), preferred_element_type=F32)
        for k in range(1, taps):
            total_ref[ids(b, k)] += back[:rows, (k - 1) * bs : k * bs]
    for i, ref in enumerate((back_far_ref, back_near_ref)):
        for b in range(blocks):
            ref[b] = total_ref[i * blocks + b, :count].astype(BF16)
            last_ref[b : b + 1] = total_ref[i * blocks + b, count : count + 1]
        ref[blocks] = last_ref[...].astype(BF16)


def combine_kernel(
    base_ref, even_ref, odd_ref, mate_ref, curve_ref, terms_ref, field_ref, map_ref, hess_ref, out_ref
):
    blocks, rows, bs = field_ref.shape
    count = mate_ref.shape[1]
    inv_diag_ref = terms_ref.at[1]
    own_part = jnp.where(is_even("space"), 1.0, 0.0)
    arrived = lambda c: even_ref[c].astype(F32) + odd_ref[c].astype(F32) + own_part * mate_ref[c].astype(F32)
    from_last = arrived(blocks)
    cross = jnp.zeros((rows, bs), F32)
    square = jnp.zeros((rows, bs), F32)
    summed = jnp.zeros(out_ref.shape, F32)
    for b in range(0, blocks, PAIR):
        parts = []
        for c in range(b, b + PAIR):
            last = jnp.broadcast_to(from_last[c : c + 1], (rows - count, bs))
            hess = base_ref[c] + jnp.concatenate([arrived(c), last], axis=0)
            hess_ref[c] = hess
            scaled = hess * inv_diag_ref[c : c + 1]
            cross += field_ref[c] * scaled
            square += hess * scaled
            parts.append(scaled.astype(BF16))
        summed += jnp.dot(
            jnp.concatenate(parts, axis=1), map_ref[b * bs : (b + PAIR) * bs], preferred_element_type=F32
        )
    out_ref[...] = summed
    for i, acc in enumerate((curve_ref[...], cross, square)):
        out_ref[count + 1 + i : count + 2 + i] = as_row(jnp.sum(acc, axis=1, keepdims=True), out_ref.shape[1])


def finish_kernel(
    sums_ref, product_ref, hess_sums_ref, inner_ref, dir_ref, hess_ref, terms_ref, field_ref, map_ref, solution_hbm,
    residual_hbm, next_hbm, solution_ref, residual_ref, next_ref, sems,
):
    blocks, rows, bs = field_ref.shape
    whole = solution_ref.shape[0]
    inv_diag_ref = terms_ref.at[1]
    sums, product, hess_sums = sums_ref[...], product_ref[...], hess_sums_ref[...]
    column = lambda x, i: as_column(x[whole + i : whole + i + 1], rows)
    coeffs = product.astype(BF16)
    plain = column(sums, 0)
    energy = plain + jnp.sum(coeffs.astype(F32) * sums, axis=1, keepdims=True)
    step = energy / column(hess_sums, 0)
    left = sums - step * hess_sums
    hess_product = jnp.dot(hess_sums, inner_ref[...], precision=lax.Precision.HIGH)
    coeffs = (product - step * hess_product).astype(BF16)
    plain_next = plain - 2.0 * step * column(hess_sums, 1) + step * step * column(hess_sums, 2)
    energy_next = plain_next + jnp.sum(coeffs.astype(F32) * left, axis=1, keepdims=True)
    ratio = energy_next / energy
    part = blocks // OUT_PARTS
    copies = []

    def send(i, ref, hbm):
        at = pl.ds(i * part * bs, part * bs)
        copies.append(pltpu.make_async_copy(ref.at[:, at], hbm.at[:, at], sems.at[len(copies)]))
        copies[-1].start()

    residual_of = lambda c: field_ref[c] - step * hess_ref[c]
    for i in range(OUT_PARTS):
        for c in range(i * part, (i + 1) * part):
            at = slice(c * bs, (c + 1) * bs)
            solution_ref[:, at] = (step * dir_ref[c])[:whole]
            residual_ref[:, at] = residual_of(c)[:whole]
        send(i, solution_ref, solution_hbm)
        send(i, residual_ref, residual_hbm)
    for i in range(OUT_PARTS):
        for b in range(i * part, (i + 1) * part, PAIR):
            correction = jnp.dot(coeffs, map_ref[:, b * bs : (b + PAIR) * bs], preferred_element_type=F32)
            for c in range(b, b + PAIR):
                smoothed = (residual_of(c) + correction[:, (c - b) * bs : (c - b + 1) * bs]) * inv_diag_ref[c : c + 1]
                next_ref[:, c * bs : (c + 1) * bs] = (smoothed + ratio * dir_ref[c])[:whole]
        send(i, next_ref, next_hbm)
    for copy in copies:
        copy.wait()


def call(kernel, ins, outs, scratch=(), limit=16, keep=True, aliases={}, spaces=None):
    spec = lambda space: pl.BlockSpec(memory_space=space)
    spaces = spaces or (pltpu.VMEM,) * len(outs)
    shapes = tuple((space if keep else jax.ShapeDtypeStruct)(s, t) for space, (s, t) in zip(spaces, outs))
    specs = tuple(spec(space if keep else pl.ANY) for space in spaces)
    return pl.pallas_call(
        kernel,
        out_shape=shapes if len(shapes) > 1 else shapes[0],
        in_specs=[spec(space) for space in ins],
        out_specs=specs if len(shapes) > 1 else specs[0],
        scratch_shapes=scratch,
        input_output_aliases=aliases,
        compiler_params=pltpu.CompilerParams(vmem_limit_bytes=limit * 1024 * 1024),
    )


def in_hbm(x):
    return pltpu.with_memory_space_constraint(x, pltpu.HBM)


def in_vmem(x):
    return pltpu.with_memory_space_constraint(x, pltpu.VMEM)


def body(latent, responses, probes, prior_diag, factor, cond_ids, inducing_map, inner_inverse):
    blocks, _, bs, _ = factor.shape
    count = probes.shape[0]
    rows, tall = count + 8, count + 16
    by_block = lambda x: x.reshape(blocks, bs)
    sum_shape = ((rows, inducing_map.shape[1]), F32)
    field = ((blocks, rows, bs), F32)
    packed = ((blocks + 1, count, bs), BF16)
    vmem, smem = pltpu.VMEM, pltpu.SMEM
    partial, terms, right_side, inducing_map = call(
        project_kernel,
        [pl.ANY] * 5,
        [sum_shape, ((2, blocks, bs), F32), field, (inducing_map.shape, BF16)],
        [
            vmem((blocks, bs), F32),
            vmem((blocks, bs), jnp.int32),
            vmem((blocks, bs), F32),
            vmem(probes.shape, F32),
            pltpu.SemaphoreType.DMA((4 + MAP_PARTS,)),
        ],
    )(*map(in_hbm, (by_block(latent), by_block(responses), by_block(prior_diag), probes, inducing_map)))
    points = (terms, right_side, inducing_map)

    def load(msg):
        outs = [(factor.shape, BF16), (inner_inverse.shape, F32)]
        return call(load_kernel, [pl.ANY] * 3, outs, [pltpu.SemaphoreType.DMA((2,))])(
            in_hbm(factor), in_hbm(inner_inverse), msg
        )

    def turn_map(msg):
        return (call(turn_map_kernel, [vmem, pl.ANY], [(inducing_map.shape[::-1], BF16)])(inducing_map, msg),)

    sums, ((turned_map,), (factor, inner_inverse)) = total(partial, "space", [turn_map, load])
    direction, rounded, product = call(
        direction_kernel, [vmem] * 5, [field, packed, sum_shape], [vmem((blocks, bs), F32)]
    )(sums, inner_inverse, terms, right_side, turned_map)
    far_odd = sent(rounded, "space", 2, (1,))
    around = ((3 * blocks, rows, bs), F32)
    half = blocks // 2

    def own_image(first, other, *after):
        count = blocks - half if first else half
        return call(
            functools.partial(own_image_kernel, tall, first),
            [vmem] * 2 + [pl.ANY] * len(after),
            [((count, tall, bs), F32), other],
            [vmem((blocks, bs), F32)],
        )(rounded, factor, *after)

    image_one, again = own_image(0, packed)
    far_even = sent(again, "space", 2, (0,))
    image_two, zeros = own_image(half, around, image_one)
    shape = (blocks, (factor.shape[1] - 1) * bs, bs)
    turned, ids = call(
        turn_kernel,
        [vmem, pl.ANY, pl.ANY],
        [(shape, BF16), (cond_ids.shape[::-1], jnp.int32)],
        [pltpu.SemaphoreType.DMA],
        spaces=(vmem, smem),
    )(factor, cond_ids.T, image_two)
    near = swapped(call(pass_on_kernel, [vmem, vmem, pl.ANY], [packed])(rounded, far_odd, turned), "space")
    back_far, back_near, back_own, curve, image = call(
        functools.partial(hessian_kernel, rows),
        [smem] + [vmem] * 9,
        [packed, packed, around, ((rows, bs), F32), ((blocks, tall, bs), BF16)],
        [vmem((3 * blocks, count, bs), BF16), vmem((3 * blocks, bs), F32), vmem((blocks, bs), F32)],
        aliases={9: 2},
    )(ids, factor, turned, image_one, image_two, near, far_even, far_odd, rounded, zeros)
    mate = swapped(back_near, "space")
    from_even = sent(back_far, "space", -2, (0,))
    from_odd = sent(call(join_kernel, [vmem] * 2, [packed])(back_far, mate), "space", -2, (1,))
    base, curve = call(functools.partial(own_back_kernel, rows), [vmem] * 6, [field, ((rows, bs), F32)])(
        image, factor, back_own, curve, direction, terms
    )
    hess, partial = call(combine_kernel, [vmem] * 8, [field, sum_shape])(base, from_even, from_odd, mate, curve, *points)
    hess_sums, _ = total(partial, "space")
    whole = ((count + 1, blocks * bs), F32)
    scratch = [vmem(*whole)] * 3 + [pltpu.SemaphoreType.DMA((3 * OUT_PARTS,))]
    return call(finish_kernel, [vmem] * 9, [whole] * 3, scratch, keep=False)(
        *map(in_vmem, (sums, product, hess_sums, inner_inverse, direction, hess, terms, right_side, turned_map))
    )


def solution(mesh):
    return jax.shard_map(
        body,
        mesh=mesh,
        in_specs=(
            P(("groups", "space")),
            P(("groups", "space")),
            P(None, ("groups", "space")),
            P(("groups", "space")),
            P(("groups", "space"), None, None, None),
            P(("groups", "space"), None),
            P(("groups", "space"), None),
            P("groups", None),
        ),
        out_specs=(
            P(None, ("groups", "space")),
            P(None, ("groups", "space")),
            P(None, ("groups", "space")),
        ),
        check_vma=False,
    )
```

```python
import functools

import jax
import jax.numpy as jnp
from jax import lax
from jax.experimental import pallas as pl
from jax.experimental.pallas import tpu as pltpu
from jax.sharding import PartitionSpec as P

F32, BF16 = jnp.float32, jnp.bfloat16
PAIR = 2
MAP_PARTS = 4
OUT_PARTS = 4


def sent(block, axis, distance, parities=(0, 1)):
    devices = range(lax.axis_size(axis))
    return lax.ppermute(block, axis, [(i, i + distance) for i in devices if i % 2 in parities and i + distance in devices])


def swapped(block, axis):
    return lax.ppermute(block, axis, [(i, i ^ 1) for i in range(lax.axis_size(axis))])


def is_even(axis):
    return lax.rem(lax.axis_index(axis), 2) == 0


def write_message(msg_ref, x):
    top, half = x.shape[0] - 8, x.shape[1] // 2
    value, beside = x[top:, :half], x[top:, half:]
    high = value.astype(BF16).astype(F32)
    middle = (value - high).astype(BF16).astype(F32)
    low = value - high - middle
    row = lax.broadcasted_iota(jnp.int32, value.shape, 0)
    left = jnp.where(row < 4, high, pltpu.roll(low, 3, 0))
    right = jnp.where(row < 1, beside, middle)
    msg_ref[...] = jnp.concatenate([x[:top], jnp.concatenate([left, right], axis=1)], axis=0).astype(BF16)


def read_message(msg_ref):
    x = msg_ref[...].astype(F32)
    top, half = x.shape[0] - 8, x.shape[1] // 2
    left, right = x[top:, :half], x[top:, half:]
    row = lax.broadcasted_iota(jnp.int32, left.shape, 0)
    left = jnp.where(row < 1, left, left + right + pltpu.roll(left, 5, 0))
    return jnp.concatenate([x[:top], jnp.concatenate([left, right], axis=1)], axis=0)


def add_kernel(count, held, x_ref, *refs):
    in_refs, (out_ref, *msg_refs) = refs[: count - 1], refs[count - 1 + held :]
    x = x_ref[...]
    for ref in in_refs:
        x = x + (ref[...] if ref.dtype == F32 else read_message(ref))
    out_ref[...] = x
    for ref in msg_refs:
        write_message(ref, x)


def rounds_of(n):
    rounds, step = [(1,)], n
    if n.bit_length() % 2:
        step //= 2
        rounds.append((step ^ 1,))
    while step > 2:
        step //= 4
        rounds.append(tuple((m * step) ^ 1 for m in range(1, 4)))
    return rounds


def total(x, axis, beside=()):
    n = lax.axis_size(axis)
    if n & (n - 1):
        return lax.psum(x, axis), [work(x) for work in beside]
    rounds = rounds_of(n)
    made, todo, msg = [], list(beside), x
    for i, partners in enumerate(rounds):
        got = [lax.ppermute(msg, axis, [(j, j ^ d) for j in range(n)]) for d in partners]
        last = i + 1 == len(rounds)
        held = ()
        while len(todo) >= max(len(rounds) - i, 1):
            made.append(todo.pop(0)(msg))
            held += made[-1]
        add = functools.partial(add_kernel, len(got) + 1, len(held))
        ins = [pltpu.VMEM] * (len(got) + 1) + [pl.ANY] * len(held)
        outs = [(x.shape, F32)] + [(x.shape, BF16)] * (not last)
        x, *rest = jax.tree.leaves(call(add, ins, outs)(x, *got, *held))
        msg = rest[0] if rest else None
    return x, made


def eye(rows, lanes):
    return lax.broadcasted_iota(jnp.int32, (rows, lanes), 0) == lax.broadcasted_iota(jnp.int32, (rows, lanes), 1)


def as_row(column, lanes):
    return jnp.sum(jnp.where(eye(column.shape[0], lanes), column, 0.0), axis=0, keepdims=True)


def as_column(row, rows):
    return jnp.sum(jnp.where(eye(rows, row.shape[1]), row, 0.0), axis=1, keepdims=True)


def project_kernel(
    latent_hbm, responses_hbm, prior_hbm, probes_hbm, map_hbm, out_ref, terms_ref, field_ref, map_ref, latent_ref,
    responses_ref, prior_ref, probes_ref, sems,
):
    blocks, bs = latent_ref.shape
    rows = out_ref.shape[0]
    count = probes_ref.shape[0]
    part = map_ref.shape[0] // MAP_PARTS
    cut = lambda ref, i: ref.at[i * part : (i + 1) * part]
    pairs = [(latent_hbm, latent_ref), (responses_hbm, responses_ref), (prior_hbm, prior_ref), (probes_hbm, probes_ref)]
    pairs += [(cut(map_hbm, i), cut(map_ref, i)) for i in range(MAP_PARTS)]
    copies = [pltpu.make_async_copy(a, b, sems.at[i]) for i, (a, b) in enumerate(pairs)]
    for copy in copies:
        copy.start()
    for copy in copies[:3]:
        copy.wait()
    probability = 1.0 / (1.0 + jnp.exp(-latent_ref[...]))
    weights = probability * (1.0 - probability)
    gradient = responses_ref[...].astype(F32) - probability
    inv_diag = 1.0 / (weights + prior_ref[...])
    terms_ref[0] = weights
    terms_ref[1] = inv_diag
    copies[3].wait()
    energy = jnp.zeros((rows, bs), F32)
    scaled = []
    for b in range(blocks):
        at = slice(b * bs, (b + 1) * bs)
        last = jnp.broadcast_to(gradient[b : b + 1], (rows - count, bs))
        field = pltpu.roll(jnp.concatenate([probes_ref[:, at], last], axis=0), 1, 0)
        field_ref[b] = field
        scaled.append(field * inv_diag[b : b + 1])
        energy += field * scaled[-1]
    summed = jnp.zeros(out_ref.shape, F32)
    for b in range(0, blocks, PAIR):
        if b * bs % part == 0:
            copies[4 + b * bs // part].wait()
        both = jnp.concatenate([scaled[b + i].astype(BF16) for i in range(PAIR)], axis=1)
        summed += jnp.dot(both, map_ref[b * bs : (b + PAIR) * bs], preferred_element_type=F32)
    out_ref[...] = summed
    out_ref[count + 1 : count + 2] = as_row(jnp.sum(energy, axis=1, keepdims=True), out_ref.shape[1])


def direction_kernel(sums_ref, inner_ref, terms_ref, field_ref, map_ref, dir_ref, msg_ref, product_ref, last_ref):
    blocks, _, bs = field_ref.shape
    count = msg_ref.shape[1]
    inv_diag_ref = terms_ref.at[1]
    product = jnp.dot(sums_ref[...], inner_ref[...], precision=lax.Precision.HIGH)
    product_ref[...] = product
    coeffs = product.astype(BF16)
    for b in range(0, blocks, PAIR):
        correction = jnp.dot(coeffs, map_ref[:, b * bs : (b + PAIR) * bs], preferred_element_type=F32)
        for c in range(b, b + PAIR):
            direction = (field_ref[c] + correction[:, (c - b) * bs : (c - b + 1) * bs]) * inv_diag_ref[c : c + 1]
            dir_ref[c] = direction
            msg_ref[c] = direction[:count].astype(BF16)
            last_ref[c : c + 1] = direction[count : count + 1]
    msg_ref[blocks] = last_ref[...].astype(BF16)


def turn_map_kernel(map_ref, after_ref, turned_ref):
    points, inducing = map_ref.shape
    for i in range(0, points, inducing):
        turned_ref[:, i : i + inducing] = map_ref[i : i + inducing].T


def load_kernel(factor_hbm, inner_hbm, after_ref, factor_ref, inner_ref, sems):
    half = factor_ref.shape[0] // 2
    copies = [
        pltpu.make_async_copy(factor_hbm.at[:half], factor_ref.at[:half], sems.at[0]),
        pltpu.make_async_copy(inner_hbm, inner_ref, sems.at[1]),
    ]
    for copy in copies:
        copy.start()
    for copy in copies:
        copy.wait()


def load_rest_kernel(factor_hbm, begun_ref, after_ref, factor_ref, sem):
    half = factor_ref.shape[0] // 2
    copy = pltpu.make_async_copy(factor_hbm.at[half:], factor_ref.at[half:], sem)
    copy.start()
    copy.wait()


def turn_kernel(factor_ref, ids_any, after_ref, turned_ref, ids_ref, sem):
    copy = pltpu.make_async_copy(ids_any, ids_ref, sem)
    copy.start()
    blocks, taps, bs, _ = factor_ref.shape
    for b in range(blocks):
        for k in range(1, taps):
            turned_ref[b, (k - 1) * bs : k * bs] = factor_ref[b, k].T
    copy.wait()


def tall_block(refs, lasts, at, tall):
    most = refs[at]
    last = jnp.broadcast_to(lasts[pl.ds(at, 1), :], (tall - most.shape[0], most.shape[1]))
    return jnp.concatenate([most, last.astype(BF16)], axis=0)


def own_image_kernel(tall, first, own_ref, factor_ref, *refs):
    image_ref, other_ref, last_ref = refs[-3:]
    blocks, bs = last_ref.shape
    other_ref[...] = jnp.zeros_like(other_ref) if first else own_ref[...]
    last_ref[...] = own_ref[blocks].astype(F32)
    for b in range(image_ref.shape[0]):
        image_ref[b] = lax.dot_general(
            tall_block(own_ref, last_ref, first + b, tall),
            factor_ref[first + b, 0],
            (((1,), (1,)), ((), ())),
            preferred_element_type=F32,
        )


def pass_on_kernel(own_ref, far_ref, after_ref, out_ref):
    @pl.when(is_even("space"))
    def _():
        out_ref[...] = own_ref[...]

    @pl.when(jnp.logical_not(is_even("space")))
    def _():
        out_ref[...] = far_ref[...]


def join_kernel(back_far_ref, got_ref, out_ref):
    out_ref[...] = (back_far_ref[...].astype(F32) + got_ref[...].astype(F32)).astype(BF16)


def own_back_kernel(rows, image_ref, factor_ref, total_ref, curve_ref, dir_ref, terms_ref, base_ref, curve_out_ref):
    blocks = factor_ref.shape[0]
    curve = curve_ref[...]
    for b in range(blocks):
        direction = dir_ref[b]
        weighted = terms_ref[0, b : b + 1] * direction
        curve += weighted * direction
        back = jnp.dot(image_ref[b], factor_ref[b, 0], preferred_element_type=F32)[:rows]
        base_ref[b] = total_ref[2 * blocks + b] + back + weighted
    curve_out_ref[...] = curve


def hessian_kernel(
    rows, ids_ref, factor_ref, turned_ref, image_one_ref, image_two_ref, near_ref, far_even_ref, far_odd_ref, own_ref,
    zeros_ref, back_far_ref, back_near_ref, total_ref, curve_ref, image_ref, around_ref, around_last_ref, last_ref,
):
    blocks, taps, bs, _ = factor_ref.shape
    count = around_ref.shape[1]
    tall = image_ref.shape[1]
    for i, refs in enumerate(((far_even_ref, far_odd_ref), (near_ref,), (own_ref,))):
        at = slice(i * blocks, (i + 1) * blocks)
        around_ref[at] = functools.reduce(jnp.add, [ref[:blocks] for ref in refs])
        around_last_ref[at] = functools.reduce(jnp.add, [ref[blocks].astype(F32) for ref in refs])
    first = (lax.axis_index("space") - 2) * blocks
    curve = jnp.zeros((rows, bs), F32)
    ids = lambda b, k: ids_ref[k - 1, b] - first
    side_by_side = lambda b: jnp.concatenate([factor_ref[b, k] for k in range(1, taps)], axis=1)
    for b in range(blocks):
        chosen = [tall_block(around_ref, around_last_ref, ids(b, k), tall) for k in range(1, taps)]
        half = image_one_ref.shape[0]
        own_image = image_one_ref[b] if b < half else image_two_ref[b - half]
        image = own_image + jnp.dot(
            jnp.concatenate(chosen, axis=1), turned_ref[b], preferred_element_type=F32
        )
        rounded = image.astype(BF16)
        image_ref[b] = rounded
        curve += (image * rounded.astype(F32))[:rows]
    curve_ref[...] = curve
    for b in range(blocks):
        back = jnp.dot(image_ref[b], side_by_side(b), preferred_element_type=F32)
        for k in range(1, taps):
            total_ref[ids(b, k)] += back[:rows, (k - 1) * bs : k * bs]
    for i, ref in enumerate((back_far_ref, back_near_ref)):
        for b in range(blocks):
            ref[b] = total_ref[i * blocks + b, :count].astype(BF16)
            last_ref[b : b + 1] = total_ref[i * blocks + b, count : count + 1]
        ref[blocks] = last_ref[...].astype(BF16)


def combine_kernel(
    base_ref, even_ref, odd_ref, mate_ref, curve_ref, terms_ref, field_ref, map_ref, hess_ref, out_ref
):
    blocks, rows, bs = field_ref.shape
    count = mate_ref.shape[1]
    inv_diag_ref = terms_ref.at[1]
    own_part = jnp.where(is_even("space"), 1.0, 0.0)
    arrived = lambda c: even_ref[c].astype(F32) + odd_ref[c].astype(F32) + own_part * mate_ref[c].astype(F32)
    from_last = arrived(blocks)
    cross = jnp.zeros((rows, bs), F32)
    square = jnp.zeros((rows, bs), F32)
    summed = jnp.zeros(out_ref.shape, F32)
    for b in range(0, blocks, PAIR):
        parts = []
        for c in range(b, b + PAIR):
            last = jnp.broadcast_to(from_last[c : c + 1], (rows - count, bs))
            hess = base_ref[c] + jnp.concatenate([arrived(c), last], axis=0)
            hess_ref[c] = hess
            scaled = hess * inv_diag_ref[c : c + 1]
            cross += field_ref[c] * scaled
            square += hess * scaled
            parts.append(scaled.astype(BF16))
        summed += jnp.dot(
            jnp.concatenate(parts, axis=1), map_ref[b * bs : (b + PAIR) * bs], preferred_element_type=F32
        )
    out_ref[...] = summed
    for i, acc in enumerate((curve_ref[...], cross, square)):
        out_ref[count + 1 + i : count + 2 + i] = as_row(jnp.sum(acc, axis=1, keepdims=True), out_ref.shape[1])


def finish_kernel(
    sums_ref, product_ref, hess_sums_ref, inner_ref, dir_ref, hess_ref, terms_ref, field_ref, map_ref, solution_hbm,
    residual_hbm, next_hbm, solution_ref, residual_ref, next_ref, sems,
):
    blocks, rows, bs = field_ref.shape
    whole = solution_ref.shape[0]
    inv_diag_ref = terms_ref.at[1]
    sums, product, hess_sums = sums_ref[...], product_ref[...], hess_sums_ref[...]
    column = lambda x, i: as_column(x[whole + i : whole + i + 1], rows)
    coeffs = product.astype(BF16)
    plain = column(sums, 0)
    energy = plain + jnp.sum(coeffs.astype(F32) * sums, axis=1, keepdims=True)
    step = energy / column(hess_sums, 0)
    left = sums - step * hess_sums
    hess_product = jnp.dot(hess_sums, inner_ref[...], precision=lax.Precision.HIGH)
    coeffs = (product - step * hess_product).astype(BF16)
    plain_next = plain - 2.0 * step * column(hess_sums, 1) + step * step * column(hess_sums, 2)
    energy_next = plain_next + jnp.sum(coeffs.astype(F32) * left, axis=1, keepdims=True)
    ratio = energy_next / energy
    part = blocks // OUT_PARTS
    copies = []

    def send(i, ref, hbm):
        at = pl.ds(i * part * bs, part * bs)
        copies.append(pltpu.make_async_copy(ref.at[:, at], hbm.at[:, at], sems.at[len(copies)]))
        copies[-1].start()

    residual_of = lambda c: field_ref[c] - step * hess_ref[c]
    for i in range(OUT_PARTS):
        for c in range(i * part, (i + 1) * part):
            at = slice(c * bs, (c + 1) * bs)
            solution_ref[:, at] = (step * dir_ref[c])[:whole]
            residual_ref[:, at] = residual_of(c)[:whole]
        send(i, solution_ref, solution_hbm)
        send(i, residual_ref, residual_hbm)
    for i in range(OUT_PARTS):
        for b in range(i * part, (i + 1) * part, PAIR):
            correction = jnp.dot(coeffs, map_ref[:, b * bs : (b + PAIR) * bs], preferred_element_type=F32)
            for c in range(b, b + PAIR):
                smoothed = (residual_of(c) + correction[:, (c - b) * bs : (c - b + 1) * bs]) * inv_diag_ref[c : c + 1]
                next_ref[:, c * bs : (c + 1) * bs] = (smoothed + ratio * dir_ref[c])[:whole]
        send(i, next_ref, next_hbm)
    for copy in copies:
        copy.wait()


def call(kernel, ins, outs, scratch=(), limit=16, keep=True, aliases={}, spaces=None):
    spec = lambda space: pl.BlockSpec(memory_space=space)
    spaces = spaces or (pltpu.VMEM,) * len(outs)
    shapes = tuple((space if keep else jax.ShapeDtypeStruct)(s, t) for space, (s, t) in zip(spaces, outs))
    specs = tuple(spec(space if keep else pl.ANY) for space in spaces)
    return pl.pallas_call(
        kernel,
        out_shape=shapes if len(shapes) > 1 else shapes[0],
        in_specs=[spec(space) for space in ins],
        out_specs=specs if len(shapes) > 1 else specs[0],
        scratch_shapes=scratch,
        input_output_aliases=aliases,
        compiler_params=pltpu.CompilerParams(vmem_limit_bytes=limit * 1024 * 1024),
    )


def in_hbm(x):
    return pltpu.with_memory_space_constraint(x, pltpu.HBM)


def in_vmem(x):
    return pltpu.with_memory_space_constraint(x, pltpu.VMEM)


def body(latent, responses, probes, prior_diag, factor, cond_ids, inducing_map, inner_inverse):
    blocks, _, bs, _ = factor.shape
    count = probes.shape[0]
    rows, tall = count + 8, count + 16
    by_block = lambda x: x.reshape(blocks, bs)
    sum_shape = ((rows, inducing_map.shape[1]), F32)
    field = ((blocks, rows, bs), F32)
    packed = ((blocks + 1, count, bs), BF16)
    vmem, smem = pltpu.VMEM, pltpu.SMEM
    partial, terms, right_side, inducing_map = call(
        project_kernel,
        [pl.ANY] * 5,
        [sum_shape, ((2, blocks, bs), F32), field, (inducing_map.shape, BF16)],
        [
            vmem((blocks, bs), F32),
            vmem((blocks, bs), jnp.int32),
            vmem((blocks, bs), F32),
            vmem(probes.shape, F32),
            pltpu.SemaphoreType.DMA((4 + MAP_PARTS,)),
        ],
    )(*map(in_hbm, (by_block(latent), by_block(responses), by_block(prior_diag), probes, inducing_map)))
    points = (terms, right_side, inducing_map)

    def load(msg):
        outs = [(factor.shape, BF16), (inner_inverse.shape, F32)]
        return call(load_kernel, [pl.ANY] * 3, outs, [pltpu.SemaphoreType.DMA((2,))])(
            in_hbm(factor), in_hbm(inner_inverse), msg
        )

    def turn_map(msg):
        return (call(turn_map_kernel, [vmem, pl.ANY], [(inducing_map.shape[::-1], BF16)])(inducing_map, msg),)

    begun = []

    def first_step(msg):
        begun.extend(load(msg))
        return (*begun, *turn_map(msg))

    def second_step(msg):
        rest = call(
            load_rest_kernel, [pl.ANY, vmem, pl.ANY], [(factor.shape, BF16)], [pltpu.SemaphoreType.DMA], aliases={1: 0}
        )
        return (rest(in_hbm(factor), begun[0], msg),)

    sums, ((_, inner_inverse, turned_map), (factor_here,)) = total(partial, "space", [first_step, second_step])
    factor = factor_here
    direction, rounded, product = call(
        direction_kernel, [vmem] * 5, [field, packed, sum_shape], [vmem((blocks, bs), F32)]
    )(sums, inner_inverse, terms, right_side, turned_map)
    far_odd = sent(rounded, "space", 2, (1,))
    around = ((3 * blocks, rows, bs), F32)
    half = blocks // 2

    def own_image(first, other, *after):
        count = blocks - half if first else half
        return call(
            functools.partial(own_image_kernel, tall, first),
            [vmem] * 2 + [pl.ANY] * len(after),
            [((count, tall, bs), F32), other],
            [vmem((blocks, bs), F32)],
        )(rounded, factor, *after)

    image_one, again = own_image(0, packed)
    far_even = sent(again, "space", 2, (0,))
    image_two, zeros = own_image(half, around, image_one)
    shape = (blocks, (factor.shape[1] - 1) * bs, bs)
    turned, ids = call(
        turn_kernel,
        [vmem, pl.ANY, pl.ANY],
        [(shape, BF16), (cond_ids.shape[::-1], jnp.int32)],
        [pltpu.SemaphoreType.DMA],
        spaces=(vmem, smem),
    )(factor, cond_ids.T, image_two)
    near = swapped(call(pass_on_kernel, [vmem, vmem, pl.ANY], [packed])(rounded, far_odd, turned), "space")
    back_far, back_near, back_own, curve, image = call(
        functools.partial(hessian_kernel, rows),
        [smem] + [vmem] * 9,
        [packed, packed, around, ((rows, bs), F32), ((blocks, tall, bs), BF16)],
        [vmem((3 * blocks, count, bs), BF16), vmem((3 * blocks, bs), F32), vmem((blocks, bs), F32)],
        aliases={9: 2},
    )(ids, factor, turned, image_one, image_two, near, far_even, far_odd, rounded, zeros)
    mate = swapped(back_near, "space")
    from_even = sent(back_far, "space", -2, (0,))
    from_odd = sent(call(join_kernel, [vmem] * 2, [packed])(back_far, mate), "space", -2, (1,))
    base, curve = call(functools.partial(own_back_kernel, rows), [vmem] * 6, [field, ((rows, bs), F32)])(
        image, factor, back_own, curve, direction, terms
    )
    hess, partial = call(combine_kernel, [vmem] * 8, [field, sum_shape])(base, from_even, from_odd, mate, curve, *points)
    hess_sums, _ = total(partial, "space")
    whole = ((count + 1, blocks * bs), F32)
    scratch = [vmem(*whole)] * 3 + [pltpu.SemaphoreType.DMA((3 * OUT_PARTS,))]
    return call(finish_kernel, [vmem] * 9, [whole] * 3, scratch, keep=False)(
        *map(in_vmem, (sums, product, hess_sums, inner_inverse, direction, hess, terms, right_side, turned_map))
    )


def solution(mesh):
    return jax.shard_map(
        body,
        mesh=mesh,
        in_specs=(
            P(("groups", "space")),
            P(("groups", "space")),
            P(None, ("groups", "space")),
            P(("groups", "space")),
            P(("groups", "space"), None, None, None),
            P(("groups", "space"), None),
            P(("groups", "space"), None),
            P("groups", None),
        ),
        out_specs=(
            P(None, ("groups", "space")),
            P(None, ("groups", "space")),
            P(None, ("groups", "space")),
        ),
        check_vma=False,
    )
```
